512 devices in a mesh: vid: 16 (over z_hi, y, core), seq: 32 (over x, z_lo).
Axes of the slice: x: 4, y: 4, z: 16 (z_hi: 2, z_lo: 8; z = z_hi * 8 + z_lo), core: 2. Of those that a mesh axis runs over, the one named last changes fastest.
Arguments:
- time_qkv: bfloat16 [3, 16, 32, 256, 704], P(None, 'vid', None, 'seq'), may hold values from -6 to 6
- space_qkv: bfloat16 [3, 16, 32, 256, 704], P(None, 'vid', 'seq'), may hold values from -6 to 6
- residual: bfloat16 [16, 32, 256, 1408], P('vid', 'seq'), may hold values from -6.4 to 6.4
- space_proj: bfloat16 [704, 1408], P('seq', 'vid'), may hold values from -0.875 to 0.875
- time_proj: bfloat16 [704, 1408], P('seq', 'vid'), may hold values from -0.875 to 0.875
- norm_gain: float32 [1408], replicated, may hold values from 0.1 to 1.9
- text_emb: float32 [16, 1408], P('vid'), may hold values from -6.8 to 6.8
- teacher: int32 [16, 16], P('vid'), may hold values from 0 to 40
Outputs:
- space_qkv_grad: bfloat16 [3, 16, 32, 256, 704], P(None, 'vid', 'seq')
- time_qkv_grad: bfloat16 [3, 16, 32, 256, 704], P(None, 'vid', None, 'seq')
- score_grad: float32 [16, 16], P('vid')
The draws below stay inside these ranges and needn't reach their ends.
All inputs are finite; a program needn't handle non-finite values.
Results may differ from the reference program's by a relative error of at most 0.0049.
Values may be sent and summed in bfloat16 or wider, within the bound.
No kernel may reach another device: no remote copies, remote signals or barrier semaphores. Data moves between devices by JAX's collectives and lax.ppermute only.
A program may use at most 64 MiB of HBM per device.

```python
import math
import jax
import jax.numpy as jnp
from jax import lax

D = 1408
HEAD_DIM = 88
HEADS = 8
PATCHES = 256
ATT = 704
FRAMES = 32
VIDEOS = 16


def attention_inputs(key):
    base_key = jax.random.fold_in(key, 0)
    values = jax.random.truncated_normal(base_key, -6.0, 6.0, (3, VIDEOS, FRAMES, PATCHES, ATT), jnp.float32)
    return values.astype(jnp.bfloat16)


def shared_directions(key):
    return jax.random.truncated_normal(key, -4.0, 4.0, (VIDEOS, D), jnp.float32)


def draw_time_qkv(key, part):
    key = jax.random.fold_in(key, 3)
    return attention_inputs(key)


def draw_space_qkv(key, part):
    key = jax.random.fold_in(key, 5)
    return attention_inputs(key)


def draw_residual(key, part):
    directions = shared_directions(key)
    key = jax.random.fold_in(key, 7)
    noise_key = jax.random.fold_in(key, 0)
    position = jnp.arange(FRAMES, dtype=jnp.float32) / max(FRAMES - 1, 1)
    shape = (VIDEOS, FRAMES, PATCHES, D)
    noise = jax.random.truncated_normal(noise_key, -6.0, 6.0, shape, jnp.float32)
    strength = 0.02 * 5.0 ** position
    mixed_values = noise + strength[None, :, None, None] * directions[:, None, None, :]
    return mixed_values.astype(jnp.bfloat16)


def draw_text_emb(key, part):
    directions = shared_directions(key)
    key = jax.random.fold_in(key, 9)
    noise = jax.random.truncated_normal(key, -6.0, 6.0, (VIDEOS, D), jnp.float32)
    return directions / 5.0 + noise


def with_ends(drawn, own_key, low, high):
    index_at = [jax.random.randint(jax.random.fold_in(own_key, axis), (), 0, length) for axis, length in enumerate(drawn.shape)]
    widest = drawn.shape.index(max(drawn.shape))
    beside = index_at[:widest] + [(index_at[widest] + 1) % drawn.shape[widest]] + index_at[widest + 1:]
    return drawn.at[tuple(index_at)].set(low).at[tuple(beside)].set(high)


def levels(key, dims, pieces, low, high):
    def one(dim, shards_of):
        steps = jax.random.uniform(jax.random.fold_in(jax.random.fold_in(key, 6), dim), (shards_of,), jnp.float32, low / len(pieces), high / len(pieces))
        return jnp.repeat(jnp.exp(steps), dims[dim] // shards_of).reshape((-1,) + (1,) * (len(dims) - dim - 1))

    level = one(*pieces[0])
    for cut in pieces[1:]:
        level = level * one(*cut)
    return level


def gaussian(stream_key, shape, width, reach, pieces=(), held_as=jnp.bfloat16):
    result = width * jax.random.normal(stream_key, shape, jnp.float32)
    if pieces:
        result = result * levels(stream_key, shape, pieces, -0.22, 0.18)
    return jnp.clip(result, -reach, reach).astype(held_as)


def setup_inputs(seed: int = 0) -> dict:
    seeds = jax.random.split(jax.random.key(seed), 9)
    return {
        "time_qkv": draw_time_qkv(jax.random.fold_in(seeds[8], 71), 0),
        "space_qkv": draw_space_qkv(jax.random.fold_in(seeds[8], 71), 0),
        "residual": draw_residual(jax.random.fold_in(seeds[8], 71), 0),
        "space_proj": gaussian(seeds[3], (ATT, D), (ATT // 16) ** -0.5, 0.875, ((0, 32), (1, 16))),
        "time_proj": gaussian(seeds[4], (ATT, D), (ATT // 16) ** -0.5, 0.875, ((0, 32), (1, 16))),
        "norm_gain": jnp.clip(1.0 + 0.18 * jax.random.normal(seeds[5], (D,), jnp.float32), 0.1, 1.9),
        "text_emb": draw_text_emb(jax.random.fold_in(seeds[8], 71), 0),
        "teacher": with_ends(jax.random.randint(seeds[7], (VIDEOS, VIDEOS), 0, 41), jax.random.fold_in(seeds[7], 1), 0, 40).astype(jnp.int32),
    }


logit_scale = 20.0
teacher_softness = 4.0
space_layout = ('blhe', 'bmhe', 'bhlm')
time_layout = ('lbhe', 'mbhe', 'bhlm')

def probabilities(queries, key_rows, layout):
    scores = jnp.einsum(layout[0] + ',' + layout[1] + '->' + layout[2], queries.astype(jnp.float32), key_rows.astype(jnp.float32)) / math.sqrt(queries.shape[-1])
    row_peak = lax.optimization_barrier(jnp.max(scores, axis=-1, keepdims=True))
    weights = jnp.exp(scores - row_peak)
    weights = weights / lax.optimization_barrier(jnp.sum(weights, axis=-1, keepdims=True))
    return (weights, weights.astype(jnp.bfloat16))

def attention_back(queries, key_rows, values, weights, weights_low, grad_out, layout):
    out_dots = jnp.einsum(layout[0] + ',' + layout[1] + '->' + layout[2], grad_out.astype(jnp.float32), values.astype(jnp.float32))
    row_delta = lax.optimization_barrier(jnp.sum(weights * out_dots, axis=-1, keepdims=True))
    slopes = (weights * (out_dots - row_delta) / math.sqrt(queries.shape[-1])).astype(jnp.bfloat16)
    grad_queries = jnp.einsum(layout[2] + ',' + layout[1] + '->' + layout[0], slopes.astype(jnp.float32), key_rows.astype(jnp.float32)).astype(jnp.bfloat16)
    grad_keys = jnp.einsum(layout[2] + ',' + layout[0] + '->' + layout[1], slopes.astype(jnp.float32), queries.astype(jnp.float32)).astype(jnp.bfloat16)
    grad_values = jnp.einsum(layout[2] + ',' + layout[0] + '->' + layout[1], weights_low.astype(jnp.float32), grad_out.astype(jnp.float32)).astype(jnp.bfloat16)
    return jnp.stack([grad_queries, grad_keys, grad_values])

def layer_norm(mixed_sum):
    center = mixed_sum - lax.optimization_barrier(jnp.mean(mixed_sum, axis=-1, keepdims=True))
    inv_scale = 1.0 / jnp.sqrt(lax.optimization_barrier(jnp.mean(center * center, axis=-1, keepdims=True)) + 1e-05)
    return (center * inv_scale, inv_scale)

def unit_rows(matrix):
    row_norm = jnp.sqrt(lax.optimization_barrier(jnp.sum(matrix * matrix, axis=-1, keepdims=True)) + 1e-06)
    return (matrix / row_norm, row_norm)

def split_heads(qkv_video):
    return [qkv_video[slot].reshape(FRAMES, PATCHES, HEADS, HEAD_DIM) for slot in range(3)]

def space_forward(qkv_video, residual_video, space_proj, norm_gain):
    queries, key_rows, values = split_heads(qkv_video)
    weights, weights_low = probabilities(queries, key_rows, space_layout)
    attended = jnp.einsum('bhlm,bmhe->blhe', weights_low.astype(jnp.float32), values.astype(jnp.float32)).astype(jnp.bfloat16)
    attended = attended.reshape(FRAMES * PATCHES, ATT)
    mixed_sum = residual_video.reshape(FRAMES * PATCHES, D).astype(jnp.float32) + jnp.dot(attended, space_proj, preferred_element_type=jnp.float32)
    normalized_rows, inv_scale = layer_norm(mixed_sum)
    frame_emb = lax.optimization_barrier(jnp.mean((normalized_rows * norm_gain).reshape(FRAMES, PATCHES, D), axis=1))
    return (queries, key_rows, values, weights, weights_low, normalized_rows, inv_scale, frame_emb)

def reference(time_qkv, space_qkv, residual, space_proj, time_proj, norm_gain, text_emb, teacher):
    space_videos = jnp.moveaxis(space_qkv, 1, 0)
    time_videos = jnp.moveaxis(time_qkv, 1, 0)

    def embed_video(items):
        return space_forward(items[0], items[1], space_proj, norm_gain)[7]
    frame_emb = lax.map(embed_video, (space_videos, residual))
    frame_unit, frame_norm = unit_rows(frame_emb)
    text_unit = unit_rows(text_emb)[0]
    scores = logit_scale / FRAMES * jnp.einsum('vfd,jd->vj', frame_unit, text_unit, precision=lax.Precision.HIGHEST)
    exp_scores = jnp.exp(scores)
    row_soft = exp_scores / lax.optimization_barrier(jnp.sum(exp_scores, axis=1, keepdims=True))
    col_soft = exp_scores / lax.optimization_barrier(jnp.sum(exp_scores, axis=0, keepdims=True))
    teacher_exponent = jnp.exp(teacher.astype(jnp.float32) / teacher_softness)
    teacher_soft = teacher_exponent / lax.optimization_barrier(jnp.sum(teacher_exponent, axis=1, keepdims=True))
    identity = jnp.eye(VIDEOS, dtype=jnp.float32)
    score_grad = (row_soft - identity + (col_soft - identity)) / (2.0 * VIDEOS) + (row_soft - teacher_soft) / VIDEOS
    direction = VIDEOS * logit_scale * jnp.dot(score_grad, text_unit, precision=lax.Precision.HIGHEST)
    along = lax.optimization_barrier(jnp.sum(frame_unit * direction[:, None, :], axis=-1, keepdims=True))
    frame_grad = (direction[:, None, :] - frame_unit * along) / frame_norm

    def video_backward(items):
        space_video, residual_video, time_video, frame_grad_video = items
        queries, key_rows, values, weights, weights_low, normalized_rows, inv_scale, unused_emb = space_forward(space_video, residual_video, space_proj, norm_gain)
        token_grad = jnp.broadcast_to((frame_grad_video * norm_gain)[:, None, :], (FRAMES, PATCHES, D)).reshape(FRAMES * PATCHES, D)
        mean_grad = lax.optimization_barrier(jnp.mean(token_grad, axis=-1, keepdims=True))
        mean_cross = lax.optimization_barrier(jnp.mean(token_grad * normalized_rows, axis=-1, keepdims=True))
        mixed_grad = (inv_scale * (token_grad - mean_grad - normalized_rows * mean_cross)).astype(jnp.bfloat16)
        space_out_grad = jnp.dot(mixed_grad, space_proj.T, preferred_element_type=jnp.float32).astype(jnp.bfloat16)
        space_out_grad = space_out_grad.reshape(FRAMES, PATCHES, HEADS, HEAD_DIM)
        space_grad = attention_back(queries, key_rows, values, weights, weights_low, space_out_grad, space_layout)
        time_out_grad = jnp.dot(mixed_grad, time_proj.T, preferred_element_type=jnp.float32).astype(jnp.bfloat16)
        time_out_grad = time_out_grad.reshape(FRAMES, PATCHES, HEADS, HEAD_DIM)
        time_queries, time_keys, temporal_value_rows = split_heads(time_video)
        time_weights, time_low = probabilities(time_queries, time_keys, time_layout)
        time_grad = attention_back(time_queries, time_keys, temporal_value_rows, time_weights, time_low, time_out_grad, time_layout)
        return (space_grad.reshape(3, FRAMES, PATCHES, ATT), time_grad.reshape(3, FRAMES, PATCHES, ATT))
    space_grads, time_grads = lax.map(video_backward, (space_videos, residual, time_videos, frame_grad))
    return (jnp.moveaxis(space_grads, 0, 1), jnp.moveaxis(time_grads, 0, 1), score_grad)
```

```python
import math

import jax
import jax.numpy as jnp
from jax import lax
from jax.sharding import Mesh
from jax.sharding import PartitionSpec as P

HEAD_DIM = 88
VID = ("zh", "y", "c")
SEQ = ("x", "zl")
RING = ("zh", "zl")
SIZES = {"zh": 2, "y": 4, "c": 2, "x": 4, "zl": 8}

logit_scale = 20.0
teacher_softness = 4.0
space_layout = ("blhe", "bmhe", "bhlm")
time_layout = ("lbhe", "mbhe", "bhlm")


def probabilities(queries, key_rows, layout):
    scores = jnp.einsum(
        layout[0] + "," + layout[1] + "->" + layout[2],
        queries,
        key_rows,
        preferred_element_type=jnp.float32,
    ) / math.sqrt(queries.shape[-1])
    row_peak = jnp.max(scores, axis=-1, keepdims=True)
    weights = jnp.exp(scores - row_peak)
    weights = weights / jnp.sum(weights, axis=-1, keepdims=True)
    return (weights, weights.astype(jnp.bfloat16))


def attention_back(queries, key_rows, values, weights, weights_low, grad_out, layout):
    out_dots = jnp.einsum(
        layout[0] + "," + layout[1] + "->" + layout[2],
        grad_out,
        values,
        preferred_element_type=jnp.float32,
    )
    row_delta = jnp.sum(weights * out_dots, axis=-1, keepdims=True)
    slopes = (weights * (out_dots - row_delta) / math.sqrt(queries.shape[-1])).astype(jnp.bfloat16)
    grad_queries = jnp.einsum(
        layout[2] + "," + layout[1] + "->" + layout[0],
        slopes,
        key_rows,
        preferred_element_type=jnp.float32,
    ).astype(jnp.bfloat16)
    grad_keys = jnp.einsum(
        layout[2] + "," + layout[0] + "->" + layout[1],
        slopes,
        queries,
        preferred_element_type=jnp.float32,
    ).astype(jnp.bfloat16)
    grad_values = jnp.einsum(
        layout[2] + "," + layout[0] + "->" + layout[1],
        weights_low,
        grad_out,
        preferred_element_type=jnp.float32,
    ).astype(jnp.bfloat16)
    return jnp.stack([grad_queries, grad_keys, grad_values])


def spread(block, axes):
    count = math.prod(SIZES[axis] for axis in axes)
    return lax.all_to_all(jnp.broadcast_to(block[None], (count,) + block.shape), axes, 0, 0)


def swap(block, axis):
    return lax.ppermute(block, axis, [(0, 1), (1, 0)])


def in_order(own, other, axis):
    first = lax.axis_index(axis) == 0
    return jnp.where(first, jnp.stack([own, other]), jnp.stack([other, own]))


def gather_texts(text_emb):
    pair = in_order(text_emb, swap(text_emb, "zh"), "zh")
    turns = [pair] + [
        lax.ppermute(pair, "y", [(i, (i + k) % 4) for i in range(4)]) for k in range(1, 4)
    ]
    turns = jnp.stack(turns)[(lax.axis_index("y") - jnp.arange(4)) % 4]
    both = in_order(turns, swap(turns, "c"), "c")
    return both.transpose(2, 1, 0, 3, 4).reshape(16, -1)


def gather_projections(space_proj, time_proj):
    rows, cols = space_proj.shape
    pack = jnp.pad(jnp.concatenate([space_proj, time_proj]), ((0, 48 - 2 * rows), (0, 128 - cols)))
    ring = spread(pack, RING).reshape(2, 8, 48, 128)

    def columns(blocks):
        return blocks.transpose(0, 3, 1, 2).reshape(2, cols, 8 * rows)

    space = columns(ring[:, :, :rows, :cols])
    time = columns(ring[:, :, rows : 2 * rows, :cols])
    w_time = lax.all_gather(time, ("c", "x", "y"))
    own = spread(space, ("x", "y"))
    w_space = in_order(own, swap(own, "c"), "c")

    def natural(w):
        return (
            w.reshape(2, 4, 4, 2, cols, 8 * rows)
            .transpose(3, 2, 0, 4, 1, 5)
            .reshape(16 * cols, 32 * rows)
        )

    return natural(w_space), natural(w_time)


def shards(time_qkv, space_qkv, residual, space_proj, time_proj, norm_gain, text_emb, teacher):
    w_space, w_time = gather_projections(space_proj, time_proj)
    model_width = residual.shape[3]
    frames_dev = residual.shape[1]
    patches = residual.shape[2]
    head_width = w_space.shape[1]
    head_count = head_width // HEAD_DIM
    frames = frames_dev * 32
    patch_dev = time_qkv.shape[3]
    videos = 16
    token_count = frames_dev * patches
    space_parts = [
        space_qkv[slot, 0].reshape(frames_dev, patches, head_count, HEAD_DIM) for slot in range(3)
    ]
    weights, weights_low = probabilities(space_parts[0], space_parts[1], space_layout)
    attended = jnp.einsum(
        "bhlm,bmhe->blhe", weights_low, space_parts[2], preferred_element_type=jnp.float32
    ).astype(jnp.bfloat16)
    attended = attended.reshape(token_count, head_width)
    mixed_sum = residual[0].reshape(token_count, model_width).astype(jnp.float32) + jnp.einsum(
        "ta,da->td", attended, w_space, preferred_element_type=jnp.float32
    )
    center = mixed_sum - jnp.mean(mixed_sum, axis=-1, keepdims=True)
    inv_scale = 1.0 / jnp.sqrt(jnp.mean(center * center, axis=-1, keepdims=True) + 1e-05)
    normalized_rows = center * inv_scale
    frame_emb = jnp.mean(
        (normalized_rows * norm_gain).reshape(frames_dev, patches, model_width), axis=1
    )
    frame_norm = jnp.sqrt(jnp.sum(frame_emb * frame_emb, axis=-1, keepdims=True) + 1e-06)
    frame_unit = frame_emb / frame_norm
    texts = gather_texts(text_emb)
    text_unit = texts / jnp.sqrt(jnp.sum(texts * texts, axis=-1, keepdims=True) + 1e-06)
    frame_cosines = jnp.dot(frame_unit, text_unit.T, precision=lax.Precision.HIGHEST)
    partial_row = logit_scale / frames * jnp.sum(frame_cosines, axis=0)
    along_ring = spread(partial_row, RING).reshape(2, 8, videos).sum(1)
    everywhere = spread(along_ring, ("y", "c", "x")).reshape(4, 2, 4, 2, videos).sum(2)
    all_scores = everywhere.transpose(2, 0, 1, 3).reshape(videos, videos)
    own_video = lax.axis_index(VID)
    own_row = lax.dynamic_index_in_dim(all_scores, own_video, 0, False)
    one_hot = (jnp.arange(videos) == own_video).astype(jnp.float32)
    own_exp = jnp.exp(own_row)
    row_soft = own_exp / jnp.sum(own_exp)
    col_soft = own_exp / jnp.sum(jnp.exp(all_scores), axis=0)
    teacher_exponent = jnp.exp(teacher[0].astype(jnp.float32) / teacher_softness)
    teacher_soft = teacher_exponent / jnp.sum(teacher_exponent)
    gradient_row_slice = (row_soft - one_hot + (col_soft - one_hot)) / (2.0 * videos) + (
        row_soft - teacher_soft
    ) / videos
    direction = (
        videos
        * logit_scale
        * jnp.dot(gradient_row_slice, text_unit, precision=lax.Precision.HIGHEST)
    )
    along = jnp.sum(frame_unit * direction[None, :], axis=-1, keepdims=True)
    frame_grad = (direction[None, :] - frame_unit * along) / frame_norm
    token_grad = jnp.broadcast_to(
        (frame_grad * norm_gain)[:, None, :], (frames_dev, patches, model_width)
    ).reshape(token_count, model_width)
    mean_grad = jnp.mean(token_grad, axis=-1, keepdims=True)
    mean_cross = jnp.mean(token_grad * normalized_rows, axis=-1, keepdims=True)
    mixed_grad = (inv_scale * (token_grad - mean_grad - normalized_rows * mean_cross)).astype(
        jnp.bfloat16
    )
    time_out_grad = jnp.einsum(
        "td,da->ta", mixed_grad, w_time, preferred_element_type=jnp.float32
    ).astype(jnp.bfloat16)
    moved = lax.all_to_all(time_out_grad.reshape(32, patch_dev, head_width), SEQ, 0, 0)
    space_out_grad = jnp.einsum(
        "td,da->ta", mixed_grad, w_space, preferred_element_type=jnp.float32
    ).astype(jnp.bfloat16)
    space_out_grad = space_out_grad.reshape(frames_dev, patches, head_count, HEAD_DIM)
    space_grad = attention_back(
        space_parts[0],
        space_parts[1],
        space_parts[2],
        weights,
        weights_low,
        space_out_grad,
        space_layout,
    )
    space_grad = space_grad.reshape(3, 1, frames_dev, patches, head_width)
    time_out_grad = moved.reshape(frames, patch_dev, head_count, HEAD_DIM)
    time_parts = [
        time_qkv[slot, 0].reshape(frames, patch_dev, head_count, HEAD_DIM) for slot in range(3)
    ]
    time_weights, time_low = probabilities(time_parts[0], time_parts[1], time_layout)
    time_grad = attention_back(
        time_parts[0],
        time_parts[1],
        time_parts[2],
        time_weights,
        time_low,
        time_out_grad,
        time_layout,
    )
    time_grad = time_grad.reshape(3, 1, frames, patch_dev, head_width)
    return (space_grad, time_grad, gradient_row_slice[None, :])


def solution(mesh):
    fine = Mesh(mesh.devices.reshape(2, 4, 2, 4, 8), ("zh", "y", "c", "x", "zl"))
    in_specs = (
        P(None, VID, None, SEQ, None),
        P(None, VID, SEQ, None, None),
        P(VID, SEQ, None, None),
        P(SEQ, VID),
        P(SEQ, VID),
        P(),
        P(VID, None),
        P(VID, None),
    )
    out_specs = (
        P(None, VID, SEQ, None, None),
        P(None, VID, None, SEQ, None),
        P(VID, None),
    )
    return jax.shard_map(shards, mesh=fine, in_specs=in_specs, out_specs=out_specs, check_vma=False)
```

```python
import functools
import math

import jax
import jax.numpy as jnp
from jax import lax
from jax.experimental import pallas as pl
from jax.experimental.pallas import tpu as pltpu
from jax.sharding import Mesh
from jax.sharding import PartitionSpec as P

HEAD_DIM = 88
HEADS = 8
ATT = 704
WIDTH = 1408
HALF = 704
TOKENS = 256
VIDEOS = 16
FRAMES = 32
PAIR = 2 * HEAD_DIM
WINDOW = 96
BACK = PAIR - WINDOW
VID = ("zh", "y", "c")
SEQ = ("x", "zl")
RING = ("zh", "zl")
SIZES = {"zh": 2, "y": 4, "c": 2, "x": 4, "zl": 8}

logit_scale = 20.0
teacher_softness = 4.0
F32 = jnp.float32
BF16 = jnp.bfloat16
ROOT = 1.0 / math.sqrt(HEAD_DIM)
VMEM = pl.BlockSpec(memory_space=pltpu.VMEM)
SMEM = pl.BlockSpec(memory_space=pltpu.SMEM)


def dot(a, b, contract):
    return lax.dot_general(a, b, (contract, ((), ())), preferred_element_type=F32)


NN = ((1,), (0,))
NT = ((1,), (1,))
TN = ((0,), (0,))


def call(kernel, out_shape, args, flops, moved, scalars=0):
    return pl.pallas_call(
        kernel,
        out_shape=out_shape,
        in_specs=[SMEM] * scalars + [VMEM] * (len(args) - scalars),
        out_specs=jax.tree.map(lambda _: VMEM, out_shape),
        compiler_params=pltpu.CompilerParams(vmem_limit_bytes=16 * 2**20),
        cost_estimate=pl.CostEstimate(flops=flops, bytes_accessed=moved, transcendentals=0),
    )(*args)


def spread(block, axes):
    count = math.prod(SIZES[axis] for axis in axes)
    return lax.all_to_all(jnp.broadcast_to(block[None], (count,) + block.shape), axes, 0, 0)


def swap(block, axis):
    return lax.ppermute(block, axis, [(0, 1), (1, 0)])


def in_order(own, other, axis):
    first = lax.axis_index(axis) == 0
    return jnp.where(first, jnp.stack([own, other]), jnp.stack([other, own]))


def gather_column_texts(text_emb):
    both = in_order(text_emb, swap(text_emb, "c"), "c")
    turns = [both] + [
        lax.ppermute(both, "y", [(i, (i + k) % 4) for i in range(4)]) for k in range(1, 4)
    ]
    return jnp.stack(turns)[(lax.axis_index("y") - jnp.arange(4)) % 4]


def halves(rows):
    parts = []
    for c in range(2):
        blocks = [(zh * 4 + y) * 2 + c for y in range(4) for zh in range(2)]
        parts.append(
            jnp.concatenate([rows[:, b * HEAD_DIM : (b + 1) * HEAD_DIM] for b in blocks], axis=1)
        )
    return parts


def split_kernel(core_ref, res_ref, gain_ref, res_out, gain_out):
    core = core_ref[0]
    for ref, out in ((res_ref, res_out), (gain_ref, gain_out)):
        parts = halves(ref[...])
        for c in range(2):
            out[core ^ c] = parts[c]


def text_kernel(core_ref, text_ref, out):
    core = core_ref[0]
    text = text_ref[...]
    unit = text / jnp.sqrt(jnp.sum(text * text, axis=1, keepdims=True) + 1e-06)
    parts = halves(unit)
    for c in range(2):
        out[core ^ c] = parts[c]


def assemble_kernel(ring_ref, space_out, time_out):
    rows = 22
    piece = lax.broadcasted_iota(jnp.int32, (48, PAIR), 0)
    column = lax.broadcasted_iota(jnp.int32, (48, PAIR), 1)
    for first, out in ((0, space_out), (rows, time_out)):
        pick = jnp.concatenate(
            [
                ((piece - first + rows * zl == column) & (piece >= first) & (piece < first + rows))
                .astype(F32)
                .astype(BF16)
                for zl in range(8)
            ]
        )
        both = []
        for zh in range(2):
            blocks = ring_ref[8 * zh : 8 * zh + 8].reshape(8 * 48, 128)
            both.append(dot(blocks, pick, TN)[:HEAD_DIM])
        whole = jnp.concatenate(both).astype(BF16)
        if len(out.shape) == 3:
            for i in range(out.shape[0]):
                out[i] = whole
        else:
            out[...] = whole


def head_rows(head):
    start = (head // 2) * PAIR + (head % 2) * BACK
    return slice(start, start + WINDOW)


def head_valid(head):
    row = lax.broadcasted_iota(jnp.int32, (WINDOW, 1), 0)
    return row < HEAD_DIM if head % 2 == 0 else row >= WINDOW - HEAD_DIM


def own_rows(block, head):
    return block[:HEAD_DIM] if head % 2 == 0 else block[WINDOW - HEAD_DIM :]


def keep(valid, block):
    return jnp.where(valid, block, jnp.zeros_like(block))


def softmax_down(scores):
    peak = jnp.max(scores, axis=0, keepdims=True)
    weights = jnp.exp(scores - peak)
    return (weights * (1.0 / jnp.sum(weights, axis=0, keepdims=True))).astype(BF16)


def slopes_down(weights, dots):
    weights = weights.astype(F32)
    delta = jnp.sum(weights * dots, axis=0, keepdims=True)
    return (weights * (dots - delta) * ROOT).astype(BF16)


def space_forward_kernel(qkv_ref, weights_out, att_out):
    pair = []
    for head in range(HEADS):
        rows, valid = head_rows(head), head_valid(head)
        scores = dot(qkv_ref[1, rows], keep(valid, qkv_ref[0, rows]), TN) * ROOT
        weights = softmax_down(scores)
        weights_out[head] = weights
        pair.append(own_rows(dot(qkv_ref[2, rows], weights, NN), head))
        if head % 2:
            att_out[head // 2] = jnp.concatenate(pair).T.astype(BF16)
            pair = []


def space_back_kernel(mixed_ref, own_ref, other_ref, qkv_ref, weights_ref, out):
    for x in range(4):
        grad = dot(mixed_ref[0], own_ref[x], NN) + dot(mixed_ref[1], other_ref[x], NN)
        grad = grad.T.astype(BF16)
        pairs = [[], [], []]
        for head in (2 * x, 2 * x + 1):
            rows, valid = head_rows(head), head_valid(head)
            grad_rows = grad[:WINDOW] if head % 2 == 0 else grad[BACK:]
            dots = dot(qkv_ref[2, rows], keep(valid, grad_rows), TN)
            weights = weights_ref[head]
            slopes = slopes_down(weights, dots)
            pairs[0].append(own_rows(dot(qkv_ref[1, rows], slopes, NN), head))
            pairs[1].append(own_rows(dot(qkv_ref[0, rows], slopes, NT), head))
            pairs[2].append(own_rows(dot(grad_rows, weights, NT), head))
        for slot in range(3):
            out[slot, x * PAIR : (x + 1) * PAIR] = jnp.concatenate(pairs[slot]).astype(BF16)


def head_lanes(head):
    start = (head * HEAD_DIM) // 128 * 128
    width = min(256, ATT - start)
    lane = lax.broadcasted_iota(jnp.int32, (1, width), 1) + (start - head * HEAD_DIM)
    return slice(start, start + width), (lane >= 0) & (lane < HEAD_DIM)


def time_forward_kernel(qkv_ref, weights_out):
    key = lax.broadcasted_iota(jnp.int32, (TOKENS, TOKENS), 0)
    query = lax.broadcasted_iota(jnp.int32, (TOKENS, TOKENS), 1)
    same = ((key ^ query) & 7) == 0
    for head in range(HEADS):
        lanes, valid = head_lanes(head)
        scores = dot(qkv_ref[1, :, lanes], keep(valid, qkv_ref[0, :, lanes]), NT) * ROOT
        weights_out[head] = softmax_down(jnp.where(same, scores, -1e30))


def time_back_kernel(grad_ref, qkv_ref, weights_ref, out, total):
    for head in range(HEADS):
        lanes, valid = head_lanes(head)
        grad = grad_ref[:, lanes]
        dots = dot(qkv_ref[2, :, lanes], keep(valid, grad), NT)
        weights = weights_ref[head]
        slopes = slopes_down(weights, dots)
        for slot, part in enumerate(
            (
                dot(slopes, qkv_ref[1, :, lanes], TN),
                dot(slopes, qkv_ref[0, :, lanes], NN),
                dot(weights, grad, NN),
            )
        ):
            total[slot, :, lanes] = jnp.where(valid, part, total[slot, :, lanes])
    out[...] = total[...].astype(BF16)


def eye():
    row = lax.broadcasted_iota(jnp.int32, (VIDEOS, 128), 0)
    column = lax.broadcasted_iota(jnp.int32, (VIDEOS, 128), 1)
    return (row == column).astype(F32)


def embed_kernel(
    att_ref, res_ref, own_ref, other_ref, gain_ref, text_ref, normed_out, inv_out, unit_out, norm_out, row_out
):
    sums = []
    for half, w_ref in enumerate((own_ref, other_ref)):
        mixed = res_ref[half].astype(F32)
        for x in range(4):
            mixed += dot(att_ref[x], w_ref[x], NT)
        sums.append(mixed)
    mean = sum(jnp.sum(s, axis=1, keepdims=True) for s in sums) / WIDTH
    sums = [s - mean for s in sums]
    square = sum(jnp.sum(s * s, axis=1, keepdims=True) for s in sums) / WIDTH
    inv = 1.0 / jnp.sqrt(square + 1e-05)
    inv_out[...] = inv
    embs = []
    for half in range(2):
        normed = sums[half] * inv
        normed_out[half] = normed
        embs.append(jnp.sum(normed, axis=0, keepdims=True) * gain_ref[half] / TOKENS)
    norm = jnp.sqrt(sum(jnp.sum(e * e, axis=1, keepdims=True) for e in embs) + 1e-06)
    norm_out[...] = norm
    cosines = jnp.zeros((VIDEOS, 1), F32)
    for half in range(2):
        unit = embs[half] / norm
        unit_out[half] = unit
        cosines += jnp.sum(text_ref[half] * unit, axis=1, keepdims=True)
    row = jnp.sum(cosines * (logit_scale / FRAMES) * eye(), axis=0, keepdims=True)
    for i in range(VIDEOS):
        row_out[i] = row


def mixed_grad_kernel(
    place_ref,
    shares_ref,
    teacher_ref,
    normed_ref,
    inv_ref,
    unit_ref,
    norm_ref,
    gain_ref,
    text_ref,
    w_ref,
    score_out,
    mixed_out,
    time_out,
):
    core, own = place_ref[0], place_ref[1]
    scores = shares_ref[...].reshape(8, 4, 2, 128).sum(axis=1)
    video = lax.broadcasted_iota(jnp.int32, scores.shape, 0) + 8 * lax.broadcasted_iota(
        jnp.int32, scores.shape, 1
    )
    lane = lax.broadcasted_iota(jnp.int32, (1, 128), 1)
    exps = jnp.exp(scores)
    own_exp = jnp.sum(jnp.sum(jnp.where(video == own, exps, 0.0), axis=0), axis=0, keepdims=True)
    own_exp = jnp.where(lane < VIDEOS, own_exp, 0.0)
    column = jnp.sum(jnp.sum(exps, axis=0), axis=0, keepdims=True)
    row_soft = own_exp / jnp.sum(own_exp, axis=1, keepdims=True)
    col_soft = own_exp / column
    teacher = jnp.exp(teacher_ref[...].astype(F32) / teacher_softness)
    teacher = jnp.where(lane < VIDEOS, teacher, 0.0)
    teacher_soft = teacher / jnp.sum(teacher, axis=1, keepdims=True)
    one_hot = (lane == own).astype(F32)
    score_grad = (row_soft - one_hot + (col_soft - one_hot)) / (2.0 * VIDEOS) + (
        row_soft - teacher_soft
    ) / VIDEOS
    score_out[...] = score_grad[:, :VIDEOS]
    pull = jnp.sum(score_grad * eye(), axis=1, keepdims=True) * (VIDEOS * logit_scale)
    direction = [jnp.sum(pull * text_ref[half], axis=0, keepdims=True) for half in range(2)]
    along = sum(
        jnp.sum(unit_ref[half] * direction[half], axis=1, keepdims=True) for half in range(2)
    )
    token = [
        (direction[half] - unit_ref[half] * along) / norm_ref[...] * gain_ref[half]
        for half in range(2)
    ]
    mean = sum(jnp.sum(t, axis=1, keepdims=True) for t in token) / WIDTH
    cross = (
        sum(jnp.sum(normed_ref[half] * token[half], axis=1, keepdims=True) for half in range(2))
        / WIDTH
    )
    inv = inv_ref[...]
    mixed = []
    for half in range(2):
        part = (inv * (token[half] - mean - normed_ref[half] * cross)).astype(BF16)
        mixed_out[half] = part
        mixed.append(part)
    parts = [
        dot(mixed[0], w_ref[core, x], NN) + dot(mixed[1], w_ref[1 - core, x], NN) for x in range(4)
    ]
    time_out[...] = jnp.concatenate(parts, axis=1).astype(BF16)


def shaped(shape, dtype):
    return jax.ShapeDtypeStruct(shape, dtype)


def shards(time_qkv, space_qkv, residual, space_proj, time_proj, norm_gain, text_emb, teacher):
    core = lax.axis_index("c")
    own_video = lax.axis_index(VID)
    rows, cols = space_proj.shape
    pack = jnp.pad(jnp.concatenate([space_proj, time_proj]), ((0, 48 - 2 * rows), (0, 128 - cols)))
    ring = spread(pack, RING)

    space = space_qkv.reshape(3, TOKENS, ATT).swapaxes(1, 2)
    space_weights, attended = call(
        space_forward_kernel,
        (shaped((HEADS, TOKENS, TOKENS), BF16), shaped((4, TOKENS, PAIR), BF16)),
        (space,),
        6 * 10**8,
        3 * 10**6,
    )
    res, gain = call(
        split_kernel,
        (shaped((2, TOKENS, HALF), BF16), shaped((2, 1, HALF), F32)),
        (core[None], residual.reshape(TOKENS, WIDTH), norm_gain[None]),
        10**8,
        2 * 10**6,
        scalars=1,
    )
    texts = gather_column_texts(text_emb)
    ring, space_weights, attended, res, gain, texts = lax.optimization_barrier(
        (ring, space_weights, attended, res, gain, texts)
    )

    space_copies, time_piece = call(
        assemble_kernel,
        (shaped((16, PAIR, PAIR), BF16), shaped((PAIR, PAIR), BF16)),
        (ring,),
        2 * 10**7,
        2 * 10**6,
    )
    w_time = lax.all_gather(time_piece, ("c", "x", "y")).reshape(2, 4, HALF, PAIR)
    w_own = lax.all_to_all(space_copies, ("x", "y"), 0, 0)

    text = call(
        text_kernel,
        shaped((2, VIDEOS, HALF), F32),
        (core[None], in_order(texts, swap(texts, "zh"), "zh").reshape(VIDEOS, WIDTH)),
        10**6,
        10**6,
        scalars=1,
    )
    time = time_qkv.reshape(3, TOKENS, ATT)
    time_weights = call(
        time_forward_kernel,
        shaped((HEADS, TOKENS, TOKENS), BF16),
        (time,),
        6 * 10**8,
        3 * 10**6,
    )
    w_own, text, time_weights = lax.optimization_barrier((w_own, text, time_weights))
    w_other = swap(w_own, "c").reshape(4, HALF, PAIR)
    w_own = w_own.reshape(4, HALF, PAIR)

    normed, inv, unit, norm, row = call(
        embed_kernel,
        (
            shaped((2, TOKENS, HALF), F32),
            shaped((TOKENS, 1), F32),
            shaped((2, 1, HALF), F32),
            shaped((1, 1), F32),
            shaped((VIDEOS, 1, 128), F32),
        ),
        (attended, res, w_own, w_other, gain, text),
        10**9,
        6 * 10**6,
    )
    ring_rows = lax.all_to_all(row, RING, 0, 0).reshape(2, 8, 128).sum(axis=1)
    shares = spread(ring_rows, ("y", "c", "x"))
    score_grad, mixed, time_grad = call(
        mixed_grad_kernel,
        (
            shaped((1, VIDEOS), F32),
            shaped((2, TOKENS, HALF), BF16),
            shaped((TOKENS, ATT), BF16),
        ),
        (
            jnp.stack([core, own_video]),
            shares,
            jnp.pad(teacher, ((0, 0), (0, 128 - VIDEOS))),
            normed,
            inv,
            unit,
            norm,
            gain,
            text,
            w_time,
        ),
        10**9,
        6 * 10**6,
        scalars=1,
    )
    moved = lax.all_to_all(time_grad.reshape(FRAMES, 8, ATT), SEQ, 0, 0).reshape(TOKENS, ATT)
    space_grad = call(
        space_back_kernel,
        shaped((3, ATT, TOKENS), BF16),
        (mixed, w_own, w_other, space, space_weights),
        2 * 10**9,
        8 * 10**6,
    )
    moved, space_grad = lax.optimization_barrier((moved, space_grad))
    time_out = pl.pallas_call(
        time_back_kernel,
        out_shape=shaped((3, TOKENS, ATT), BF16),
        in_specs=[VMEM] * 3,
        out_specs=VMEM,
        scratch_shapes=[pltpu.VMEM((3, TOKENS, ATT), F32)],
        compiler_params=pltpu.CompilerParams(vmem_limit_bytes=16 * 2**20),
        cost_estimate=pl.CostEstimate(flops=10**9, bytes_accessed=5 * 10**6, transcendentals=0),
    )(moved, time, time_weights)
    return (
        space_grad.swapaxes(1, 2).reshape(3, 1, 1, TOKENS, ATT),
        time_out.reshape(3, 1, FRAMES, 8, ATT),
        score_grad,
    )


def solution(mesh):
    fine = Mesh(mesh.devices.reshape(2, 4, 2, 4, 8), ("zh", "y", "c", "x", "zl"))
    in_specs = (
        P(None, VID, None, SEQ, None),
        P(None, VID, SEQ, None, None),
        P(VID, SEQ, None, None),
        P(SEQ, VID),
        P(SEQ, VID),
        P(),
        P(VID, None),
        P(VID, None),
    )
    out_specs = (
        P(None, VID, SEQ, None, None),
        P(None, VID, None, SEQ, None),
        P(VID, None),
    )
    return jax.shard_map(shards, mesh=fine, in_specs=in_specs, out_specs=out_specs, check_vma=False)
```

```python
import math

import jax
import jax.numpy as jnp
from jax import lax
from jax.experimental import pallas as pl
from jax.experimental.pallas import tpu as pltpu
from jax.sharding import Mesh
from jax.sharding import PartitionSpec as P

HEAD_DIM = 88
HEADS = 8
ATT = 704
WIDTH = 1408
HALF = 704
TOKENS = 256
VIDEOS = 16
FRAMES = 32
PAIR = 2 * HEAD_DIM
WINDOW = 96
BACK = PAIR - WINDOW
VID = ("zh", "y", "c")
SEQ = ("x", "zl")
RING = ("zh", "zl")
SIZES = {"zh": 2, "y": 4, "c": 2, "x": 4, "zl": 8}

logit_scale = 20.0
teacher_softness = 4.0
F32 = jnp.float32
BF16 = jnp.bfloat16
ROOT = 1.0 / math.sqrt(HEAD_DIM)
VMEM = pl.BlockSpec(memory_space=pltpu.VMEM)
SMEM = pl.BlockSpec(memory_space=pltpu.SMEM)
HBM = pl.BlockSpec(memory_space=pltpu.HBM)
MAIN = 128
REST = PAIR - MAIN
FOLD = 96
PACKED = PAIR + FOLD
LABELLED = PACKED + 16


def dot(a, b, contract):
    return lax.dot_general(a, b, (contract, ((), ())), preferred_element_type=F32)


NN = ((1,), (0,))
NT = ((1,), (1,))
TN = ((0,), (0,))


def call(kernel, out_shape, args, flops, moved, ins="", outs="", scratch=(), copies=0):
    places = {"s": SMEM, "v": VMEM, "h": HBM, "d": pl.BlockSpec()}
    sems = [pltpu.SemaphoreType.DMA((copies,))] if copies else []
    single = not isinstance(out_shape, tuple)
    shapes = [
        pltpu.HBM(o.shape, o.dtype) if p == "h" else o
        for o, p in zip((out_shape,) if single else out_shape, outs)
    ]
    specs = [places[p] for p in outs]
    args = [
        pltpu.with_memory_space_constraint(a, pltpu.HBM) if p == "h" else a
        for a, p in zip(args, ins)
    ]
    return pl.pallas_call(
        kernel,
        out_shape=shapes[0] if single else tuple(shapes),
        in_specs=[places[p] for p in ins],
        out_specs=specs[0] if single else tuple(specs),
        scratch_shapes=list(scratch) + sems,
        compiler_params=pltpu.CompilerParams(vmem_limit_bytes=20 * 2**20),
        cost_estimate=pl.CostEstimate(flops=flops, bytes_accessed=moved, transcendentals=0),
    )(*args)


def begin(source, target, sem):
    copy = pltpu.make_async_copy(source, target, sem)
    copy.start()
    return copy


def spread(block, axes):
    count = math.prod(SIZES[axis] for axis in axes)
    return lax.all_to_all(jnp.broadcast_to(block[None], (count,) + block.shape), axes, 0, 0)


def swap(block, axis):
    return lax.ppermute(block, axis, [(0, 1), (1, 0)])


def halves(rows):
    parts = []
    for c in range(2):
        blocks = [(zh * 4 + y) * 2 + c for y in range(4) for zh in range(2)]
        parts.append(
            jnp.concatenate([rows[:, b * HEAD_DIM : (b + 1) * HEAD_DIM] for b in blocks], axis=1)
        )
    return parts


def split_kernel(core_ref, res_ref, gain_ref, res_out, gain_out):
    core = core_ref[0]
    for ref, out in ((res_ref, res_out), (gain_ref, gain_out)):
        parts = halves(ref[...])
        for c in range(2):
            out[core ^ c] = parts[c]


def pack_kernel(place_ref, space_ref, time_ref, text_ref, out):
    zl = place_ref[0]
    rows = []
    for side, ref in enumerate((space_ref, time_ref)):
        block = jnp.zeros((1, HEAD_DIM), F32)
        for i in range(8):
            first = (2 * i + side) * HEAD_DIM
            block = jnp.where(zl == i, text_ref[:, first : first + HEAD_DIM], block)
        high = block.astype(BF16).astype(F32)
        rows += [ref[...].astype(F32), high, block - high]
    rows = jnp.concatenate(rows)
    rows = jnp.concatenate([rows, jnp.zeros((48, 128 - HEAD_DIM), F32)], axis=1).astype(BF16)
    for i in range(16):
        out[i] = rows


def assemble_kernel(place_ref, ring_ref, space_out, time_out, pieces, sems):
    rows, x = 22, place_ref[0]
    labels = [[], []]
    for zh in range(2):
        for pair in range(2):
            block = ring_ref[8 * zh + 2 * x + pair].astype(F32)
            for side in range(2):
                for term in range(2):
                    row = rows + 24 * side + term
                    labels[term].append(block[row : row + 1])
    pieces[0, PACKED:] = jnp.concatenate(labels[0] + labels[1]).astype(BF16)
    piece = lax.broadcasted_iota(jnp.int32, (48, PAIR), 0)
    column = lax.broadcasted_iota(jnp.int32, (48, PAIR), 1)
    copies = []
    for slot, first in enumerate((0, 24)):
        pick = jnp.concatenate(
            [
                ((piece - first + rows * zl == column) & (piece >= first) & (piece < first + rows))
                .astype(F32)
                .astype(BF16)
                for zl in range(8)
            ]
        )
        both = []
        for zh in range(2):
            blocks = ring_ref[8 * zh : 8 * zh + 8].reshape(8 * 48, 128)
            both.append(dot(blocks, pick, TN)[:HEAD_DIM])
        whole = jnp.concatenate(both)
        rest = whole[:, MAIN:]
        low = jnp.concatenate([rest[FOLD:], jnp.zeros((2 * FOLD - PAIR, REST), F32)])
        fold = jnp.concatenate([rest[:FOLD], low, jnp.zeros((FOLD, 128 - 2 * REST), F32)], axis=1)
        pieces[slot, :PAIR] = whole[:, :MAIN].astype(BF16)
        pieces[slot, PAIR:PACKED] = fold.astype(BF16)
        if slot == 0:
            for i in range(16):
                copies.append(begin(pieces.at[0], space_out.at[i], sems.at[i]))
        else:
            copies.append(begin(pieces.at[1, pl.ds(0, PACKED)], time_out, sems.at[16]))
    for copy in copies:
        copy.wait()


def unfold(packed, wide, narrow):
    for y in range(4):
        rows = slice(PAIR * y, PAIR * (y + 1))
        rest = []
        for x in range(4):
            wide[rows, MAIN * x : MAIN * (x + 1)] = packed[4 * x + y, :PAIR]
            fold = packed[4 * x + y, PAIR:PACKED]
            rest.append(jnp.concatenate([fold[:, :REST], fold[: PAIR - FOLD, REST : 2 * REST]]))
        narrow[rows] = jnp.concatenate(rest, axis=1)


def head_rows(head):
    start = (head // 2) * PAIR + (head % 2) * BACK
    return slice(start, start + WINDOW)


def head_valid(head):
    row = lax.broadcasted_iota(jnp.int32, (WINDOW, 1), 0)
    return row < HEAD_DIM if head % 2 == 0 else row >= WINDOW - HEAD_DIM


def own_rows(block, head):
    return block[:HEAD_DIM] if head % 2 == 0 else block[WINDOW - HEAD_DIM :]


def keep(valid, block):
    return jnp.where(valid, block, jnp.zeros_like(block))


def softmax_down(scores):
    peak = jnp.max(scores, axis=0, keepdims=True)
    weights = jnp.exp(scores - peak)
    return (weights * (1.0 / jnp.sum(weights, axis=0, keepdims=True))).astype(BF16)


def slopes_down(weights, dots):
    weights = weights.astype(F32)
    delta = jnp.sum(weights * dots, axis=0, keepdims=True)
    return (weights * (dots - delta) * ROOT).astype(BF16)


def space_forward_kernel(
    qkv_ref, weights_out, wide_out, narrow_out, kept, wide, narrow, down, sems
):
    pair, copies = [], []
    for head in range(HEADS):
        rows, valid = head_rows(head), head_valid(head)
        scores = dot(qkv_ref[1, rows], keep(valid, qkv_ref[0, rows]), TN) * ROOT
        weights = softmax_down(scores)
        kept[head] = weights
        copies.append(begin(kept.at[head], weights_out.at[head], sems.at[head]))
        pair.append(own_rows(dot(qkv_ref[2, rows], weights, NN), head))
        if head % 2:
            x = head // 2
            both = jnp.concatenate(pair)
            wide[:, MAIN * x : MAIN * (x + 1)] = both[:MAIN].T.astype(BF16)
            down[REST * x : REST * (x + 1)] = both[MAIN:]
            pair = []
    copies.append(begin(wide, wide_out, sems.at[HEADS]))
    narrow[...] = down[...].T.astype(BF16)
    copies.append(begin(narrow, narrow_out, sems.at[HEADS + 1]))
    for copy in copies:
        copy.wait()


def space_back_kernel(mixed_ref, own_ref, other_ref, qkv_ref, weights_ref, out, wide, narrow):
    grads = []
    for half, w_ref in enumerate((own_ref, other_ref)):
        unfold(w_ref, wide, narrow)
        grads.append((dot(mixed_ref[half], wide[...], NN), dot(mixed_ref[half], narrow[...], NN)))
    main = (grads[0][0] + grads[1][0]).T.astype(BF16)
    rest = (grads[0][1] + grads[1][1]).T.astype(BF16)
    for x in range(4):
        grad = jnp.concatenate([main[MAIN * x : MAIN * (x + 1)], rest[REST * x : REST * (x + 1)]])
        pairs = [[], [], []]
        for head in (2 * x, 2 * x + 1):
            rows, valid = head_rows(head), head_valid(head)
            grad_rows = grad[:WINDOW] if head % 2 == 0 else grad[BACK:]
            dots = dot(qkv_ref[2, rows], keep(valid, grad_rows), TN)
            weights = weights_ref[head]
            slopes = slopes_down(weights, dots)
            pairs[0].append(own_rows(dot(qkv_ref[1, rows], slopes, NN), head))
            pairs[1].append(own_rows(dot(qkv_ref[0, rows], slopes, NT), head))
            pairs[2].append(own_rows(dot(grad_rows, weights, NT), head))
        for slot in range(3):
            out[slot, x * PAIR : (x + 1) * PAIR] = jnp.concatenate(pairs[slot]).astype(BF16)


def head_lanes(head):
    start = (head * HEAD_DIM) // 128 * 128
    width = min(256, ATT - start)
    lane = lax.broadcasted_iota(jnp.int32, (1, width), 1) + (start - head * HEAD_DIM)
    return slice(start, start + width), (lane >= 0) & (lane < HEAD_DIM)


def time_forward_kernel(qkv_ref, weights_out, kept, sems):
    key = lax.broadcasted_iota(jnp.int32, (TOKENS, TOKENS), 0)
    query = lax.broadcasted_iota(jnp.int32, (TOKENS, TOKENS), 1)
    same = ((key ^ query) & 7) == 0
    copies = []
    for head in range(HEADS):
        lanes, valid = head_lanes(head)
        scores = dot(qkv_ref[1, :, lanes], keep(valid, qkv_ref[0, :, lanes]), NT) * ROOT
        kept[head] = softmax_down(jnp.where(same, scores, -1e30))
        copies.append(begin(kept.at[head], weights_out.at[head], sems.at[head]))
    for copy in copies:
        copy.wait()


def time_back_kernel(grad_ref, qkv_ref, weights_ref, out, kept, total, sems):
    loads = [begin(weights_ref.at[head], kept.at[head], sems.at[head]) for head in range(HEADS)]
    for head in range(HEADS):
        lanes, valid = head_lanes(head)
        grad = grad_ref[:, lanes]
        dots = dot(qkv_ref[2, :, lanes], keep(valid, grad), NT)
        loads[head].wait()
        weights = kept[head]
        slopes = slopes_down(weights, dots)
        for slot, part in enumerate(
            (
                dot(slopes, qkv_ref[1, :, lanes], TN),
                dot(slopes, qkv_ref[0, :, lanes], NN),
                dot(weights, grad, NN),
            )
        ):
            total[slot, :, lanes] = jnp.where(valid, part, total[slot, :, lanes])
    out[...] = total[...].astype(BF16)


def labels_of(y, core, half):
    row = lax.broadcasted_iota(jnp.int32, (8, 1), 0)
    return (row // 4 * 4 + y) * 2 + (core ^ half)


def embed_own_kernel(wide_ref, narrow_ref, res_ref, own_ref, out, att, rest, w_wide, w_narrow, sems):
    loads = [begin(wide_ref, att, sems.at[0]), begin(narrow_ref, rest, sems.at[1])]
    unfold(own_ref, w_wide, w_narrow)
    for load in loads:
        load.wait()
    out[...] = (
        res_ref[0].astype(F32)
        + dot(att[...], w_wide[...], NT)
        + dot(rest[...], w_narrow[...], NT)
    )


def embed_kernel(
    place_ref,
    wide_ref,
    narrow_ref,
    res_ref,
    mixed_ref,
    own_ref,
    other_ref,
    gain_ref,
    normed_out,
    inv_out,
    unit_out,
    norm_out,
    text_out,
    row_out,
    att,
    rest,
    w_wide,
    w_narrow,
    normed,
    inv_kept,
    sems,
):
    core = place_ref[0]
    loads = [begin(wide_ref, att, sems.at[0]), begin(narrow_ref, rest, sems.at[1])]
    unfold(other_ref, w_wide, w_narrow)
    for half, ref in enumerate((own_ref, other_ref)):
        for y in range(4):
            tiles, square = [], 0.0
            for x in range(4):
                terms = ref[4 * x + y, PACKED:].astype(F32)
                tiles.append(terms[:8] + terms[8:])
                square += jnp.sum(tiles[x] * tiles[x], axis=1, keepdims=True)
            upper = lax.broadcasted_iota(jnp.int32, (8, 1), 0) < 4
            first = jnp.sum(jnp.where(upper, square, 0.0), axis=0, keepdims=True)
            second = jnp.sum(jnp.where(upper, 0.0, square), axis=0, keepdims=True)
            size = jnp.sqrt(jnp.where(upper, first, second) + 1e-06)
            for x in range(4):
                text_out[half, 4 * x + y] = tiles[x] / size
    for load in loads:
        load.wait()
    sums = [mixed_ref[...]]
    sums.append(
        res_ref[1].astype(F32) + dot(att[...], w_wide[...], NT) + dot(rest[...], w_narrow[...], NT)
    )
    mean = sum(jnp.sum(s, axis=1, keepdims=True) for s in sums) / WIDTH
    sums = [s - mean for s in sums]
    square = sum(jnp.sum(s * s, axis=1, keepdims=True) for s in sums) / WIDTH
    inv = 1.0 / jnp.sqrt(square + 1e-05)
    inv_kept[...] = jnp.broadcast_to(inv, (TOKENS, 128))
    copies = [begin(inv_kept, inv_out, sems.at[2])]
    embs = []
    for half in range(2):
        part = sums[half] * inv
        normed[half] = part
        copies.append(begin(normed.at[half], normed_out.at[half], sems.at[3 + half]))
        embs.append(jnp.sum(part, axis=0, keepdims=True) * gain_ref[half] / TOKENS)
    norm = jnp.sqrt(sum(jnp.sum(e * e, axis=1, keepdims=True) for e in embs) + 1e-06)
    norm_out[...] = norm
    units = [e / norm for e in embs]
    for half in range(2):
        unit_out[half] = units[half]
    by_core = [jnp.where(core == c, units[0], units[1]) for c in range(2)]
    blank = jnp.zeros((8, 128 - HEAD_DIM), F32)
    blocks = []
    for x in range(4):
        four = []
        for q in range(4):
            start = ((x % 2 * 2 + q // 2) * 2 + x // 2) * HEAD_DIM
            four.append(by_core[q % 2][:, start : start + HEAD_DIM])
        blocks.append(jnp.concatenate([jnp.concatenate(four + four), blank], axis=1))
    lane = lax.broadcasted_iota(jnp.int32, (8, 128), 1)
    row = jnp.zeros((1, 128), F32)
    for half in range(2):
        for y in range(4):
            products = sum(text_out[half, 4 * x + y] * blocks[x] for x in range(4))
            cosines = jnp.sum(products, axis=1, keepdims=True)
            here = lane == labels_of(y, core, half)
            row += jnp.sum(jnp.where(here, cosines, 0.0), axis=0, keepdims=True)
    row = row * (logit_scale / FRAMES)
    for i in range(VIDEOS):
        row_out[i] = row
    for copy in copies:
        copy.wait()


def unfold_kernel(place_ref, w_ref, wide_out, narrow_out, w, wide, narrow, sems):
    core = place_ref[0]
    loads = [begin(w_ref.at[core ^ half], w.at[half], sems.at[half]) for half in range(2)]
    copies = []
    for half in range(2):
        loads[half].wait()
        unfold(w.at[half], wide.at[half], narrow.at[half])
        copies.append(begin(wide.at[half], wide_out.at[half], sems.at[2 + half]))
        copies.append(begin(narrow.at[half], narrow_out.at[half], sems.at[4 + half]))
    for copy in copies:
        copy.wait()


def mixed_grad_kernel(
    place_ref,
    shares_ref,
    teacher_ref,
    normed_ref,
    inv_ref,
    unit_ref,
    norm_ref,
    gain_ref,
    text_ref,
    wide_ref,
    narrow_ref,
    score_out,
    mixed_out,
    time_out,
    normed,
    inv_kept,
    w_wide,
    w_narrow,
    mixed_kept,
    sems,
):
    core, own = place_ref[0], place_ref[1]
    load_normed = begin(normed_ref, normed, sems.at[0])
    load_inv = begin(inv_ref, inv_kept, sems.at[1])
    load_wide = begin(wide_ref, w_wide, sems.at[2])
    load_narrow = begin(narrow_ref, w_narrow, sems.at[3])
    scores = shares_ref[...].reshape(8, 4, 2, 128).sum(axis=1)
    video = lax.broadcasted_iota(jnp.int32, scores.shape, 0) + 8 * lax.broadcasted_iota(
        jnp.int32, scores.shape, 1
    )
    lane = lax.broadcasted_iota(jnp.int32, (1, 128), 1)
    exps = jnp.exp(scores)
    own_exp = jnp.sum(jnp.sum(jnp.where(video == own, exps, 0.0), axis=0), axis=0, keepdims=True)
    own_exp = jnp.where(lane < VIDEOS, own_exp, 0.0)
    column = jnp.sum(jnp.sum(exps, axis=0), axis=0, keepdims=True)
    row_soft = own_exp / jnp.sum(own_exp, axis=1, keepdims=True)
    col_soft = own_exp / column
    teacher = jnp.exp(teacher_ref[...].astype(F32) / teacher_softness)
    teacher = jnp.where(lane < VIDEOS, teacher, 0.0)
    teacher_soft = teacher / jnp.sum(teacher, axis=1, keepdims=True)
    one_hot = (lane == own).astype(F32)
    score_grad = (row_soft - one_hot + (col_soft - one_hot)) / (2.0 * VIDEOS) + (
        row_soft - teacher_soft
    ) / VIDEOS
    score_out[...] = score_grad[:, :VIDEOS]
    pull = score_grad * (VIDEOS * logit_scale)
    wide_lane = lax.broadcasted_iota(jnp.int32, (8, 128), 1)
    blocks = [0.0] * 4
    for half in range(2):
        for y in range(4):
            here = wide_lane == labels_of(y, core, half)
            share = jnp.sum(jnp.where(here, pull, 0.0), axis=1, keepdims=True)
            for x in range(4):
                blocks[x] += share * text_ref[half, 4 * x + y]
    blocks = [b[:4] + b[4:] for b in blocks]
    by_core = []
    for c in range(2):
        row = []
        for y in range(4):
            for zh in range(2):
                q = y % 2 * 2 + c
                row.append(blocks[2 * zh + y // 2][q : q + 1, :HEAD_DIM])
        by_core.append(jnp.concatenate(row, axis=1))
    direction = [
        jnp.where(core == 0, by_core[0], by_core[1]),
        jnp.where(core == 0, by_core[1], by_core[0]),
    ]
    along = sum(
        jnp.sum(unit_ref[half] * direction[half], axis=1, keepdims=True) for half in range(2)
    )
    token = [
        (direction[half] - unit_ref[half] * along) / norm_ref[...] * gain_ref[half]
        for half in range(2)
    ]
    mean = sum(jnp.sum(t, axis=1, keepdims=True) for t in token) / WIDTH
    load_normed.wait()
    load_inv.wait()
    cross = (
        sum(jnp.sum(normed[half] * token[half], axis=1, keepdims=True) for half in range(2)) / WIDTH
    )
    inv = inv_kept[:, :1]
    load_wide.wait()
    load_narrow.wait()
    copies, wide, narrow = [], 0.0, 0.0
    for half in range(2):
        mixed = (inv * (token[half] - mean - normed[half] * cross)).astype(BF16)
        mixed_kept[half] = mixed
        copies.append(begin(mixed_kept.at[half], mixed_out.at[half], sems.at[4 + half]))
        wide += dot(mixed, w_wide[half], NN)
        narrow += dot(mixed, w_narrow[half], NN)
    parts = []
    for x in range(4):
        parts += [wide[:, MAIN * x : MAIN * (x + 1)], narrow[:, REST * x : REST * (x + 1)]]
    time_out[...] = jnp.concatenate(parts, axis=1).astype(BF16)
    for copy in copies:
        copy.wait()


def shaped(shape, dtype):
    return jax.ShapeDtypeStruct(shape, dtype)


def shards(time_qkv, space_qkv, residual, space_proj, time_proj, norm_gain, text_emb, teacher):
    core = lax.axis_index("c")
    own_video = lax.axis_index(VID)
    big = pltpu.VMEM
    place = jnp.stack([core, own_video])
    pack = call(
        pack_kernel,
        shaped((16, 48, 128), BF16),
        (lax.axis_index("zl")[None], space_proj, time_proj, text_emb),
        10**5,
        10**6,
        "sddd",
        "v",
    )
    ring = lax.all_to_all(pack, RING, 0, 0)

    space = space_qkv.reshape(3, TOKENS, ATT).swapaxes(1, 2)
    space_weights, att_wide, att_narrow = call(
        space_forward_kernel,
        (
            shaped((HEADS, TOKENS, TOKENS), BF16),
            shaped((TOKENS, 4 * MAIN), BF16),
            shaped((TOKENS, 4 * REST), BF16),
        ),
        (space,),
        6 * 10**8,
        3 * 10**6,
        "v",
        "hhh",
        [
            big((HEADS, TOKENS, TOKENS), BF16),
            big((TOKENS, 4 * MAIN), BF16),
            big((TOKENS, 4 * REST), BF16),
            big((4 * REST, TOKENS), F32),
        ],
        HEADS + 2,
    )
    res, gain = call(
        split_kernel,
        (shaped((2, TOKENS, HALF), BF16), shaped((2, 1, HALF), F32)),
        (core[None], residual.reshape(TOKENS, WIDTH), norm_gain[None]),
        10**8,
        2 * 10**6,
        "svv",
        "vv",
    )
    ring, res, gain, att_wide, att_narrow = lax.optimization_barrier(
        (ring, res, gain, att_wide, att_narrow)
    )

    space_copies, time_piece = call(
        assemble_kernel,
        (shaped((16, LABELLED, 128), BF16), shaped((PACKED, 128), BF16)),
        (lax.axis_index("x")[None], ring),
        2 * 10**7,
        2 * 10**6,
        "sv",
        "hh",
        [big((2, LABELLED, 128), BF16)],
        17,
    )
    w_time = lax.all_gather(time_piece, ("c", "x", "y")).reshape(2, 16, PACKED, 128)
    w_own = lax.all_to_all(space_copies, ("x", "y"), 0, 0)

    time = time_qkv.reshape(3, TOKENS, ATT)
    time_weights = call(
        time_forward_kernel,
        shaped((HEADS, TOKENS, TOKENS), BF16),
        (time,),
        6 * 10**8,
        3 * 10**6,
        "v",
        "h",
        [big((HEADS, TOKENS, TOKENS), BF16)],
        HEADS,
    )
    w_own, time_weights = lax.optimization_barrier((w_own, time_weights))
    w_other = swap(w_own, "c")
    mixed_own = call(
        embed_own_kernel,
        shaped((TOKENS, HALF), F32),
        (att_wide, att_narrow, res, w_own),
        5 * 10**8,
        3 * 10**6,
        "hhvv",
        "v",
        [
            big((TOKENS, 4 * MAIN), BF16),
            big((TOKENS, 4 * REST), BF16),
            big((HALF, 4 * MAIN), BF16),
            big((HALF, 4 * REST), BF16),
        ],
        2,
    )
    w_other, mixed_own = lax.optimization_barrier((w_other, mixed_own))
    normed, inv, unit, norm, text, row = call(
        embed_kernel,
        (
            shaped((2, TOKENS, HALF), F32),
            shaped((TOKENS, 128), F32),
            shaped((2, 1, HALF), F32),
            shaped((1, 1), F32),
            shaped((2, 16, 8, 128), F32),
            shaped((VIDEOS, 1, 128), F32),
        ),
        (core[None], att_wide, att_narrow, res, mixed_own, w_own, w_other, gain),
        10**9,
        6 * 10**6,
        "shhvvvvv",
        "hhvvvv",
        [
            big((TOKENS, 4 * MAIN), BF16),
            big((TOKENS, 4 * REST), BF16),
            big((HALF, 4 * MAIN), BF16),
            big((HALF, 4 * REST), BF16),
            big((2, TOKENS, HALF), F32),
            big((TOKENS, 128), F32),
        ],
        5,
    )
    ring_rows = lax.all_to_all(row, RING, 0, 0)
    shares = spread(ring_rows.reshape(2, 8, 128).sum(axis=1), ("y", "c", "x"))
    w_wide, w_narrow = call(
        unfold_kernel,
        (shaped((2, HALF, 4 * MAIN), BF16), shaped((2, HALF, 4 * REST), BF16)),
        (core[None], w_time),
        10**7,
        5 * 10**6,
        "sh",
        "hh",
        [
            big((2, 16, PACKED, 128), BF16),
            big((2, HALF, 4 * MAIN), BF16),
            big((2, HALF, 4 * REST), BF16),
        ],
        6,
    )
    shares, w_wide, w_narrow = lax.optimization_barrier((shares, w_wide, w_narrow))
    score_grad, mixed, time_grad = call(
        mixed_grad_kernel,
        (
            shaped((1, VIDEOS), F32),
            shaped((2, TOKENS, HALF), BF16),
            shaped((TOKENS, ATT), BF16),
        ),
        (
            place,
            shares,
            jnp.pad(teacher, ((0, 0), (0, 128 - VIDEOS))),
            normed,
            inv,
            unit,
            norm,
            gain,
            text,
            w_wide,
            w_narrow,
        ),
        10**9,
        6 * 10**6,
        "svvhhvvvvhh",
        "vhv",
        [
            big((2, TOKENS, HALF), F32),
            big((TOKENS, 128), F32),
            big((2, HALF, 4 * MAIN), BF16),
            big((2, HALF, 4 * REST), BF16),
            big((2, TOKENS, HALF), BF16),
        ],
        6,
    )
    moved = lax.all_to_all(time_grad.reshape(FRAMES, 8, ATT), SEQ, 0, 0).reshape(TOKENS, ATT)
    space_grad = call(
        space_back_kernel,
        shaped((3, ATT, TOKENS), BF16),
        (mixed, w_own, w_other, space, space_weights),
        2 * 10**9,
        8 * 10**6,
        "vvvvv",
        "v",
        [big((HALF, 4 * MAIN), BF16), big((HALF, 4 * REST), BF16)],
    )
    moved, space_grad = lax.optimization_barrier((moved, space_grad))
    time_out = call(
        time_back_kernel,
        shaped((3, TOKENS, ATT), BF16),
        (moved, time, time_weights),
        10**9,
        5 * 10**6,
        "vvh",
        "v",
        [big((HEADS, TOKENS, TOKENS), BF16), big((3, TOKENS, ATT), F32)],
        HEADS,
    )
    return (
        space_grad.swapaxes(1, 2).reshape(3, 1, 1, TOKENS, ATT),
        time_out.reshape(3, 1, FRAMES, 8, ATT),
        score_grad,
    )


def solution(mesh):
    fine = Mesh(mesh.devices.reshape(2, 4, 2, 4, 8), ("zh", "y", "c", "x", "zl"))
    in_specs = (
        P(None, VID, None, SEQ, None),
        P(None, VID, SEQ, None, None),
        P(VID, SEQ, None, None),
        P(SEQ, VID),
        P(SEQ, VID),
        P(),
        P(VID, None),
        P(VID, None),
    )
    out_specs = (
        P(None, VID, SEQ, None, None),
        P(None, VID, None, SEQ, None),
        P(VID, None),
    )
    return jax.shard_map(shards, mesh=fine, in_specs=in_specs, out_specs=out_specs, check_vma=False)
```

```python
import math

import jax
import jax.numpy as jnp
from jax import lax
from jax.experimental import pallas as pl
from jax.experimental.pallas import tpu as pltpu
from jax.sharding import Mesh
from jax.sharding import PartitionSpec as P

HEAD_DIM = 88
HEADS = 8
ATT = 704
WIDTH = 1408
HALF = 704
TOKENS = 256
VIDEOS = 16
FRAMES = 32
PAIR = 2 * HEAD_DIM
WINDOW = 96
BACK = PAIR - WINDOW
VID = ("zh", "y", "c")
SEQ = ("x", "zl")
RING = ("zh", "zl")
SIZES = {"zh": 2, "y": 4, "c": 2, "x": 4, "zl": 8}

logit_scale = 20.0
teacher_softness = 4.0
F32 = jnp.float32
BF16 = jnp.bfloat16
ROOT = 1.0 / math.sqrt(HEAD_DIM)
VMEM = pl.BlockSpec(memory_space=pltpu.VMEM)
SMEM = pl.BlockSpec(memory_space=pltpu.SMEM)
HBM = pl.BlockSpec(memory_space=pltpu.HBM)
MAIN = 128
REST = PAIR - MAIN
FOLD = 96
PACKED = PAIR + FOLD
LABELLED = PACKED + 16


def dot(a, b, contract):
    return lax.dot_general(a, b, (contract, ((), ())), preferred_element_type=F32)


NN = ((1,), (0,))
NT = ((1,), (1,))
TN = ((0,), (0,))


def call(kernel, out_shape, args, flops, moved, ins="", outs="", scratch=(), copies=0):
    places = {"s": SMEM, "v": VMEM, "m": VMEM, "h": HBM}
    pinned = {"m": pltpu.VMEM, "h": pltpu.HBM}
    sems = [pltpu.SemaphoreType.DMA((copies,))] if copies else []
    single = not isinstance(out_shape, tuple)
    shapes = [
        pinned[p](o.shape, o.dtype) if p in pinned else o
        for o, p in zip((out_shape,) if single else out_shape, outs)
    ]
    specs = [places[p] for p in outs]
    args = [
        pltpu.with_memory_space_constraint(a, pinned[p]) if p in pinned else a
        for a, p in zip(args, ins)
    ]
    return pl.pallas_call(
        kernel,
        out_shape=shapes[0] if single else tuple(shapes),
        in_specs=[places[p] for p in ins],
        out_specs=specs[0] if single else tuple(specs),
        scratch_shapes=list(scratch) + sems,
        compiler_params=pltpu.CompilerParams(vmem_limit_bytes=20 * 2**20),
        cost_estimate=pl.CostEstimate(flops=flops, bytes_accessed=moved, transcendentals=0),
    )(*args)


def begin(source, target, sem):
    copy = pltpu.make_async_copy(source, target, sem)
    copy.start()
    return copy


def spread(block, axes):
    count = math.prod(SIZES[axis] for axis in axes)
    return lax.all_to_all(jnp.broadcast_to(block[None], (count,) + block.shape), axes, 0, 0)


def swap(block, axis):
    return lax.ppermute(block, axis, [(0, 1), (1, 0)])


def halves(rows):
    parts = []
    for c in range(2):
        blocks = [(zh * 4 + y) * 2 + c for y in range(4) for zh in range(2)]
        parts.append(
            jnp.concatenate([rows[:, b * HEAD_DIM : (b + 1) * HEAD_DIM] for b in blocks], axis=1)
        )
    return parts


def split_kernel(core_ref, res_ref, gain_ref, res_out, gain_out):
    core = core_ref[0]
    for ref, out in ((res_ref, res_out), (gain_ref, gain_out)):
        parts = halves(ref[...])
        for c in range(2):
            out[core ^ c] = parts[c]


def pack_kernel(place_ref, space_hbm, time_hbm, text_hbm, out, space_ref, time_ref, text_ref, sems):
    zl = place_ref[0]
    loads = [
        begin(space_hbm, space_ref, sems.at[0]),
        begin(time_hbm, time_ref, sems.at[1]),
        begin(text_hbm, text_ref, sems.at[2]),
    ]
    for load in loads:
        load.wait()
    rows = []
    for side, ref in enumerate((space_ref, time_ref)):
        block = jnp.zeros((1, HEAD_DIM), F32)
        for i in range(8):
            first = (2 * i + side) * HEAD_DIM
            block = jnp.where(zl == i, text_ref[:, first : first + HEAD_DIM], block)
        high = block.astype(BF16).astype(F32)
        rows += [ref[...].astype(F32), high, block - high]
    rows = jnp.concatenate(rows)
    rows = jnp.concatenate([rows, jnp.zeros((48, 128 - HEAD_DIM), F32)], axis=1).astype(BF16)
    for i in range(16):
        out[i] = rows


def assemble_kernel(place_ref, ring_ref, space_out, time_out, pieces, sems):
    rows, x = 22, place_ref[0]
    labels = [[], []]
    for zh in range(2):
        for pair in range(2):
            block = ring_ref[8 * zh + 2 * x + pair].astype(F32)
            for side in range(2):
                for term in range(2):
                    row = rows + 24 * side + term
                    labels[term].append(block[row : row + 1])
    pieces[0, PACKED:] = jnp.concatenate(labels[0] + labels[1]).astype(BF16)
    piece = lax.broadcasted_iota(jnp.int32, (48, PAIR), 0)
    column = lax.broadcasted_iota(jnp.int32, (48, PAIR), 1)
    copies = []
    for slot, first in enumerate((0, 24)):
        pick = jnp.concatenate(
            [
                ((piece - first + rows * zl == column) & (piece >= first) & (piece < first + rows))
                .astype(F32)
                .astype(BF16)
                for zl in range(8)
            ]
        )
        both = []
        for zh in range(2):
            blocks = ring_ref[8 * zh : 8 * zh + 8].reshape(8 * 48, 128)
            both.append(dot(blocks, pick, TN)[:HEAD_DIM])
        whole = jnp.concatenate(both)
        rest = whole[:, MAIN:]
        low = jnp.concatenate([rest[FOLD:], jnp.zeros((2 * FOLD - PAIR, REST), F32)])
        fold = jnp.concatenate([rest[:FOLD], low, jnp.zeros((FOLD, 128 - 2 * REST), F32)], axis=1)
        pieces[slot, :PAIR] = whole[:, :MAIN].astype(BF16)
        pieces[slot, PAIR:PACKED] = fold.astype(BF16)
        if slot == 0:
            for i in range(16):
                copies.append(begin(pieces.at[0], space_out.at[i], sems.at[i]))
        else:
            copies.append(begin(pieces.at[1, pl.ds(0, PACKED)], time_out, sems.at[16]))
    for copy in copies:
        copy.wait()


def unfold(packed, wide, narrow):
    for y in range(4):
        rows = slice(PAIR * y, PAIR * (y + 1))
        rest = []
        for x in range(4):
            wide[rows, MAIN * x : MAIN * (x + 1)] = packed[4 * x + y, :PAIR]
            fold = packed[4 * x + y, PAIR:PACKED]
            rest.append(jnp.concatenate([fold[:, :REST], fold[: PAIR - FOLD, REST : 2 * REST]]))
        narrow[rows] = jnp.concatenate(rest, axis=1)


def head_rows(head):
    start = (head // 2) * PAIR + (head % 2) * BACK
    return slice(start, start + WINDOW)


def head_valid(head):
    row = lax.broadcasted_iota(jnp.int32, (WINDOW, 1), 0)
    return row < HEAD_DIM if head % 2 == 0 else row >= WINDOW - HEAD_DIM


def own_rows(block, head):
    return block[:HEAD_DIM] if head % 2 == 0 else block[WINDOW - HEAD_DIM :]


def keep(valid, block):
    return jnp.where(valid, block, jnp.zeros_like(block))


def softmax_down(scores):
    peak = jnp.max(scores, axis=0, keepdims=True)
    weights = jnp.exp(scores - peak)
    return (weights * (1.0 / jnp.sum(weights, axis=0, keepdims=True))).astype(BF16)


def slopes_down(weights, dots):
    weights = weights.astype(F32)
    delta = jnp.sum(weights * dots, axis=0, keepdims=True)
    return (weights * (dots - delta) * ROOT).astype(BF16)


def space_forward_kernel(qkv_ref, weights_out, wide_out, narrow_out, down):
    pair = []
    for head in range(HEADS):
        rows, valid = head_rows(head), head_valid(head)
        scores = dot(qkv_ref[1, rows], keep(valid, qkv_ref[0, rows]), TN) * ROOT
        weights = softmax_down(scores)
        weights_out[head] = weights
        pair.append(own_rows(dot(qkv_ref[2, rows], weights, NN), head))
        if head % 2:
            x = head // 2
            both = jnp.concatenate(pair)
            wide_out[:, MAIN * x : MAIN * (x + 1)] = both[:MAIN].T.astype(BF16)
            down[REST * x : REST * (x + 1)] = both[MAIN:]
            pair = []
    narrow_out[...] = down[...].T.astype(BF16)


def space_back_kernel(
    normed_ref, inv_ref, pulls_ref, token_ref, own_ref, other_ref, qkv_ref, weights_ref, out, wide, narrow
):
    grads = []
    for half, w_ref in enumerate((own_ref, other_ref)):
        unfold(w_ref, wide, narrow)
        token = jnp.sum(pulls_ref[TOKENS:, :1] * token_ref[half], axis=0, keepdims=True)
        mixed = inv_ref[:, :1] * (token - normed_ref[half].astype(F32) * pulls_ref[:TOKENS, :1])
        mixed = mixed.astype(BF16)
        grads.append((dot(mixed, wide[...], NN), dot(mixed, narrow[...], NN)))
    main = (grads[0][0] + grads[1][0]).T.astype(BF16)
    rest = (grads[0][1] + grads[1][1]).T.astype(BF16)
    for x in range(4):
        grad = jnp.concatenate([main[MAIN * x : MAIN * (x + 1)], rest[REST * x : REST * (x + 1)]])
        pairs = [[], [], []]
        for head in (2 * x, 2 * x + 1):
            rows, valid = head_rows(head), head_valid(head)
            grad_rows = grad[:WINDOW] if head % 2 == 0 else grad[BACK:]
            dots = dot(qkv_ref[2, rows], keep(valid, grad_rows), TN)
            weights = weights_ref[head]
            slopes = slopes_down(weights, dots)
            pairs[0].append(own_rows(dot(qkv_ref[1, rows], slopes, NN), head))
            pairs[1].append(own_rows(dot(qkv_ref[0, rows], slopes, NT), head))
            pairs[2].append(own_rows(dot(grad_rows, weights, NT), head))
        for slot in range(3):
            out[slot, x * PAIR : (x + 1) * PAIR] = jnp.concatenate(pairs[slot]).astype(BF16)


def head_lanes(head):
    start = (head * HEAD_DIM) // 128 * 128
    width = min(256, ATT - start)
    lane = lax.broadcasted_iota(jnp.int32, (1, width), 1) + (start - head * HEAD_DIM)
    return slice(start, start + width), (lane >= 0) & (lane < HEAD_DIM)


def time_forward_kernel(qkv_ref, weights_out):
    key = lax.broadcasted_iota(jnp.int32, (TOKENS, TOKENS), 0)
    query = lax.broadcasted_iota(jnp.int32, (TOKENS, TOKENS), 1)
    same = ((key ^ query) & 7) == 0
    for head in range(HEADS):
        lanes, valid = head_lanes(head)
        scores = dot(qkv_ref[1, :, lanes], keep(valid, qkv_ref[0, :, lanes]), NT) * ROOT
        weights_out[head] = softmax_down(jnp.where(same, scores, -1e30))


def time_back_kernel(grad_ref, qkv_ref, weights_ref, out, total):
    for head in range(HEADS):
        lanes, valid = head_lanes(head)
        grad = grad_ref[:, lanes]
        dots = dot(qkv_ref[2, :, lanes], keep(valid, grad), NT)
        weights = weights_ref[head]
        slopes = slopes_down(weights, dots)
        for slot, part in enumerate(
            (
                dot(slopes, qkv_ref[1, :, lanes], TN),
                dot(slopes, qkv_ref[0, :, lanes], NN),
                dot(weights, grad, NN),
            )
        ):
            total[slot, :, lanes] = jnp.where(valid, part, total[slot, :, lanes])
    out[...] = total[...].astype(BF16)


def labels_of(y, core, half):
    row = lax.broadcasted_iota(jnp.int32, (8, 1), 0)
    return (row // 4 * 4 + y) * 2 + (core ^ half)


def embed_own_kernel(wide_ref, narrow_ref, res_ref, own_ref, out, w_wide, w_narrow):
    unfold(own_ref, w_wide, w_narrow)
    out[...] = (
        res_ref[0].astype(F32)
        + dot(wide_ref[...], w_wide[...], NT)
        + dot(narrow_ref[...], w_narrow[...], NT)
    )


def embed_kernel(
    place_ref,
    wide_ref,
    narrow_ref,
    res_ref,
    mixed_ref,
    own_ref,
    other_ref,
    gain_ref,
    normed_out,
    inv_out,
    unit_out,
    norm_out,
    text_out,
    row_out,
    w_wide,
    w_narrow,
    normed,
    inv_kept,
    texts,
    sems,
):
    core = place_ref[0]
    unfold(other_ref, w_wide, w_narrow)
    for half, ref in enumerate((own_ref, other_ref)):
        for y in range(4):
            tiles, square = [], 0.0
            for x in range(4):
                terms = ref[4 * x + y, PACKED:].astype(F32)
                tiles.append(terms[:8] + terms[8:])
                square += jnp.sum(tiles[x] * tiles[x], axis=1, keepdims=True)
            upper = lax.broadcasted_iota(jnp.int32, (8, 1), 0) < 4
            first = jnp.sum(jnp.where(upper, square, 0.0), axis=0, keepdims=True)
            second = jnp.sum(jnp.where(upper, 0.0, square), axis=0, keepdims=True)
            size = jnp.sqrt(jnp.where(upper, first, second) + 1e-06)
            for x in range(4):
                texts[half, 4 * x + y] = tiles[x] / size
    copies = [begin(texts, text_out, sems.at[3])]
    sums = [mixed_ref[...]]
    sums.append(
        res_ref[1].astype(F32)
        + dot(wide_ref[...], w_wide[...], NT)
        + dot(narrow_ref[...], w_narrow[...], NT)
    )
    mean = sum(jnp.sum(s, axis=1, keepdims=True) for s in sums) / WIDTH
    sums = [s - mean for s in sums]
    square = sum(jnp.sum(s * s, axis=1, keepdims=True) for s in sums) / WIDTH
    inv = 1.0 / jnp.sqrt(square + 1e-05)
    inv_kept[...] = jnp.broadcast_to(inv, (TOKENS, 128))
    copies.append(begin(inv_kept, inv_out, sems.at[0]))
    embs = []
    for half in range(2):
        part = sums[half] * inv
        normed[half] = part.astype(BF16)
        copies.append(begin(normed.at[half], normed_out.at[half], sems.at[1 + half]))
        embs.append(jnp.sum(part, axis=0, keepdims=True) * gain_ref[half] / TOKENS)
    norm = jnp.sqrt(sum(jnp.sum(e * e, axis=1, keepdims=True) for e in embs) + 1e-06)
    norm_out[...] = norm
    units = [e / norm for e in embs]
    for half in range(2):
        unit_out[half] = units[half]
    by_core = [jnp.where(core == c, units[0], units[1]) for c in range(2)]
    blank = jnp.zeros((8, 128 - HEAD_DIM), F32)
    blocks = []
    for x in range(4):
        four = []
        for q in range(4):
            start = ((x % 2 * 2 + q // 2) * 2 + x // 2) * HEAD_DIM
            four.append(by_core[q % 2][:, start : start + HEAD_DIM])
        blocks.append(jnp.concatenate([jnp.concatenate(four + four), blank], axis=1))
    lane = lax.broadcasted_iota(jnp.int32, (8, 128), 1)
    row = jnp.zeros((1, 128), F32)
    for half in range(2):
        for y in range(4):
            products = sum(texts[half, 4 * x + y] * blocks[x] for x in range(4))
            cosines = jnp.sum(products, axis=1, keepdims=True)
            here = lane == labels_of(y, core, half)
            row += jnp.sum(jnp.where(here, cosines, 0.0), axis=0, keepdims=True)
    row = row * (logit_scale / FRAMES)
    for i in range(VIDEOS):
        row_out[i] = row
    for copy in copies:
        copy.wait()


def video_of(core):
    row = lax.broadcasted_iota(jnp.int32, (VIDEOS, 1), 0)
    return ((row & 1) * 4 + ((row >> 1) & 3)) * 2 + (core ^ (row >> 3))


def basis_kernel(place_ref, normed_ref, unit_ref, norm_ref, gain_ref, text_hbm, token_out, cross_out, normed, cross, text_ref, sems):
    core = place_ref[0]
    load_text = begin(text_hbm, text_ref, sems.at[2])
    load = begin(normed_ref, normed, sems.at[0])
    load_text.wait()
    by_core = []
    for c in range(2):
        parts = []
        for y in range(4):
            for zh in range(2):
                x, q = 2 * zh + y // 2, y % 2 * 2 + c
                rows = []
                for half in range(2):
                    for at in range(4):
                        tile = text_ref[half, 4 * x + at]
                        rows += [tile[q : q + 1, :HEAD_DIM], tile[4 + q : 5 + q, :HEAD_DIM]]
                parts.append(jnp.concatenate(rows))
        by_core.append(jnp.concatenate(parts, axis=1))
    texts = [
        jnp.where(core == 0, by_core[0], by_core[1]),
        jnp.where(core == 0, by_core[1], by_core[0]),
    ]
    along = sum(jnp.sum(texts[h] * unit_ref[h], axis=1, keepdims=True) for h in range(2))
    scale = VIDEOS * logit_scale / norm_ref[...]
    token = [(texts[h] - unit_ref[h] * along) * scale * gain_ref[h] for h in range(2)]
    mean = sum(jnp.sum(t, axis=1, keepdims=True) for t in token) / WIDTH
    load.wait()
    columns = sum(dot(normed[h], token[h].astype(BF16), NT) for h in range(2)) * (1.0 / WIDTH)
    cross[...] = jnp.concatenate([columns, jnp.zeros((TOKENS, 128 - VIDEOS), F32)], axis=1)
    copy = begin(cross, cross_out, sems.at[1])
    for half in range(2):
        token_out[half] = token[half] - mean
    copy.wait()


def project_kernel(
    place_ref,
    w_ref,
    normed_ref,
    token_ref,
    wide_out,
    narrow_out,
    pull_wide_out,
    pull_narrow_out,
    w,
    normed,
    w_wide,
    w_narrow,
    wide,
    narrow,
    pull_wide,
    pull_narrow,
    sems,
):
    core = place_ref[0]
    loads = [begin(w_ref.at[core ^ half], w.at[half], sems.at[half]) for half in range(2)]
    load_normed = begin(normed_ref, normed, sems.at[2])
    sums = [0.0] * 4
    for half in range(2):
        token = token_ref[half]
        high = token.astype(BF16)
        terms = jnp.concatenate([high.astype(F32), token - high.astype(F32)]).astype(BF16)
        loads[half].wait()
        unfold(w.at[half], w_wide, w_narrow)
        if half == 0:
            load_normed.wait()
        for i, part in enumerate((w_wide, w_narrow)):
            sums[i] += dot(normed[half], part[...], NN)
            sums[2 + i] += dot(terms, part[...], NN)
    wide[...] = sums[0].astype(BF16)
    narrow[...] = sums[1].astype(BF16)
    copies = [begin(wide, wide_out, sems.at[3]), begin(narrow, narrow_out, sems.at[4])]
    pull_wide[...] = sums[2][:VIDEOS] + sums[2][VIDEOS:]
    pull_narrow[...] = sums[3][:VIDEOS] + sums[3][VIDEOS:]
    copies.append(begin(pull_wide, pull_wide_out, sems.at[5]))
    copies.append(begin(pull_narrow, pull_narrow_out, sems.at[6]))
    for copy in copies:
        copy.wait()


def score_kernel(
    place_ref,
    shares_ref,
    teacher_ref,
    inv_ref,
    cross_ref,
    wide_ref,
    narrow_ref,
    pull_wide_ref,
    pull_narrow_ref,
    score_out,
    rows_out,
    time_out,
    inv,
    cross,
    wide,
    narrow,
    pull_wide,
    pull_narrow,
    rows,
    result,
    sems,
):
    core, own = place_ref[0], place_ref[1]
    pairs = (
        (cross_ref, cross),
        (pull_wide_ref, pull_wide),
        (pull_narrow_ref, pull_narrow),
        (inv_ref, inv),
        (wide_ref, wide),
        (narrow_ref, narrow),
    )
    loads = [begin(source, target, sems.at[i]) for i, (source, target) in enumerate(pairs)]
    scores = shares_ref[...].reshape(8, 4, 2, 128).sum(axis=1)
    video = lax.broadcasted_iota(jnp.int32, scores.shape, 0) + 8 * lax.broadcasted_iota(
        jnp.int32, scores.shape, 1
    )
    lane = lax.broadcasted_iota(jnp.int32, (1, 128), 1)
    exps = jnp.exp(scores)
    own_exp = jnp.sum(jnp.sum(jnp.where(video == own, exps, 0.0), axis=0), axis=0, keepdims=True)
    own_exp = jnp.where(lane < VIDEOS, own_exp, 0.0)
    column = jnp.sum(jnp.sum(exps, axis=0), axis=0, keepdims=True)
    row_soft = own_exp / jnp.sum(own_exp, axis=1, keepdims=True)
    col_soft = own_exp / column
    teacher = jnp.exp(teacher_ref[...].astype(F32) / teacher_softness)
    teacher = jnp.where(lane < VIDEOS, teacher, 0.0)
    teacher_soft = teacher / jnp.sum(teacher, axis=1, keepdims=True)
    one_hot = (lane == own).astype(F32)
    score_grad = (row_soft - one_hot + (col_soft - one_hot)) / (2.0 * VIDEOS) + (
        row_soft - teacher_soft
    ) / VIDEOS
    score_out[...] = score_grad[:, :VIDEOS]
    columns = lax.broadcasted_iota(jnp.int32, (VIDEOS, 128), 1)
    pull = jnp.sum(
        jnp.where(columns == video_of(core), score_grad, 0.0), axis=1, keepdims=True
    )
    rows[TOKENS:] = jnp.broadcast_to(pull, (VIDEOS, 128))
    column = lax.broadcasted_iota(jnp.int32, (VIDEOS, VIDEOS), 1)
    row = lax.broadcasted_iota(jnp.int32, (VIDEOS, VIDEOS), 0)
    pull_row = jnp.sum(jnp.where(row == column, pull, 0.0), axis=0, keepdims=True)
    for load in loads:
        load.wait()
    along = jnp.sum(cross[:, :VIDEOS] * pull_row, axis=1, keepdims=True)
    rows[:TOKENS] = jnp.broadcast_to(along, (TOKENS, 128))
    copy = begin(rows, rows_out, sems.at[6])
    base_wide = jnp.sum(pull * pull_wide[...], axis=0, keepdims=True)
    base_narrow = jnp.sum(pull * pull_narrow[...], axis=0, keepdims=True)
    scale = inv[:, :1]
    out_wide = scale * (base_wide - along * wide[...].astype(F32))
    out_narrow = scale * (base_narrow - along * narrow[...].astype(F32))
    parts = []
    for x in range(4):
        parts += [out_wide[:, MAIN * x : MAIN * (x + 1)], out_narrow[:, REST * x : REST * (x + 1)]]
    result[...] = jnp.concatenate(parts, axis=1).astype(BF16)
    send = begin(result, time_out, sems.at[7])
    copy.wait()
    send.wait()


def shaped(shape, dtype):
    return jax.ShapeDtypeStruct(shape, dtype)


def shards(time_qkv, space_qkv, residual, space_proj, time_proj, norm_gain, text_emb, teacher):
    core = lax.axis_index("c")
    own_video = lax.axis_index(VID)
    big = pltpu.VMEM
    place = jnp.stack([core, own_video])
    pack = call(
        pack_kernel,
        shaped((16, 48, 128), BF16),
        (lax.axis_index("zl")[None], space_proj, time_proj, text_emb),
        10**5,
        10**6,
        "shhh",
        "v",
        [big(space_proj.shape, BF16), big(time_proj.shape, BF16), big(text_emb.shape, F32)],
        3,
    )
    ring = lax.all_to_all(pack, RING, 0, 0)

    space_copies, time_piece = call(
        assemble_kernel,
        (shaped((16, LABELLED, 128), BF16), shaped((PACKED, 128), BF16)),
        (lax.axis_index("x")[None], ring),
        2 * 10**7,
        2 * 10**6,
        "sv",
        "hh",
        [big((2, LABELLED, 128), BF16)],
        17,
    )
    w_time = lax.all_gather(time_piece, ("c", "x", "y")).reshape(2, 16, PACKED, 128)
    w_own = lax.all_to_all(space_copies, ("x", "y"), 0, 0)

    space = space_qkv.reshape(3, TOKENS, ATT).swapaxes(1, 2)
    space_weights, att_wide, att_narrow = call(
        space_forward_kernel,
        (
            shaped((HEADS, TOKENS, TOKENS), BF16),
            shaped((TOKENS, 4 * MAIN), BF16),
            shaped((TOKENS, 4 * REST), BF16),
        ),
        (space,),
        6 * 10**8,
        3 * 10**6,
        "v",
        "mmm",
        [big((4 * REST, TOKENS), F32)],
    )
    res, gain = call(
        split_kernel,
        (shaped((2, TOKENS, HALF), BF16), shaped((2, 1, HALF), F32)),
        (core[None], residual.reshape(TOKENS, WIDTH), norm_gain[None]),
        10**8,
        2 * 10**6,
        "svv",
        "mm",
    )
    time = time_qkv.reshape(3, TOKENS, ATT)
    time_weights = call(
        time_forward_kernel,
        shaped((HEADS, TOKENS, TOKENS), BF16),
        (time,),
        6 * 10**8,
        3 * 10**6,
        "v",
        "m",
    )
    w_own, time_weights, res, gain, att_wide, att_narrow = lax.optimization_barrier(
        (w_own, time_weights, res, gain, att_wide, att_narrow)
    )
    w_other = swap(w_own, "c")
    mixed_own = call(
        embed_own_kernel,
        shaped((TOKENS, HALF), F32),
        (att_wide, att_narrow, res, w_own),
        5 * 10**8,
        3 * 10**6,
        "mmmv",
        "m",
        [big((HALF, 4 * MAIN), BF16), big((HALF, 4 * REST), BF16)],
    )
    w_other, mixed_own = lax.optimization_barrier((w_other, mixed_own))
    normed, inv, unit, norm, text, row = call(
        embed_kernel,
        (
            shaped((2, TOKENS, HALF), BF16),
            shaped((TOKENS, 128), F32),
            shaped((2, 1, HALF), F32),
            shaped((1, 1), F32),
            shaped((2, 16, 8, 128), F32),
            shaped((VIDEOS, 1, 128), F32),
        ),
        (core[None], att_wide, att_narrow, res, mixed_own, w_own, w_other, gain),
        10**9,
        6 * 10**6,
        "smmmmvvm",
        "hhvvhv",
        [
            big((HALF, 4 * MAIN), BF16),
            big((HALF, 4 * REST), BF16),
            big((2, TOKENS, HALF), BF16),
            big((TOKENS, 128), F32),
            big((2, 16, 8, 128), F32),
        ],
        4,
    )
    ring_rows = lax.all_to_all(row, RING, 0, 0)
    token, cross = call(
        basis_kernel,
        (shaped((2, VIDEOS, HALF), F32), shaped((TOKENS, 128), F32)),
        (core[None], normed, unit, norm, gain, text),
        10**8,
        2 * 10**6,
        "shvvmh",
        "vh",
        [big((2, TOKENS, HALF), BF16), big((TOKENS, 128), F32), big((2, 16, 8, 128), F32)],
        3,
    )
    ring_rows, token, cross = lax.optimization_barrier((ring_rows, token, cross))
    shares = spread(ring_rows.reshape(2, 8, 128).sum(axis=1), ("y", "c", "x"))
    wide, narrow, pull_wide, pull_narrow = call(
        project_kernel,
        (
            shaped((TOKENS, 4 * MAIN), BF16),
            shaped((TOKENS, 4 * REST), BF16),
            shaped((VIDEOS, 4 * MAIN), F32),
            shaped((VIDEOS, 4 * REST), F32),
        ),
        (core[None], w_time, normed, token),
        5 * 10**8,
        5 * 10**6,
        "shhv",
        "hhhh",
        [
            big((2, 16, PACKED, 128), BF16),
            big((2, TOKENS, HALF), BF16),
            big((HALF, 4 * MAIN), BF16),
            big((HALF, 4 * REST), BF16),
            big((TOKENS, 4 * MAIN), BF16),
            big((TOKENS, 4 * REST), BF16),
            big((VIDEOS, 4 * MAIN), F32),
            big((VIDEOS, 4 * REST), F32),
        ],
        7,
    )
    shares, wide, narrow, pull_wide, pull_narrow = lax.optimization_barrier(
        (shares, wide, narrow, pull_wide, pull_narrow)
    )
    score_grad, pulls, time_grad = call(
        score_kernel,
        (
            shaped((1, VIDEOS), F32),
            shaped((TOKENS + VIDEOS, 128), F32),
            shaped((TOKENS, ATT), BF16),
        ),
        (
            place,
            shares,
            jnp.pad(teacher, ((0, 0), (0, 128 - VIDEOS))),
            inv,
            cross,
            wide,
            narrow,
            pull_wide,
            pull_narrow,
        ),
        10**7,
        10**6,
        "svvhhhhhh",
        "vhh",
        [
            big((TOKENS, 128), F32),
            big((TOKENS, 128), F32),
            big((TOKENS, 4 * MAIN), BF16),
            big((TOKENS, 4 * REST), BF16),
            big((VIDEOS, 4 * MAIN), F32),
            big((VIDEOS, 4 * REST), F32),
            big((TOKENS + VIDEOS, 128), F32),
            big((TOKENS, ATT), BF16),
        ],
        8,
    )
    moved = lax.all_to_all(time_grad.reshape(FRAMES, 8, ATT), SEQ, 0, 0).reshape(TOKENS, ATT)
    space_grad = call(
        space_back_kernel,
        shaped((3, ATT, TOKENS), BF16),
        (normed, inv, pulls, token, w_own, w_other, space, space_weights),
        2 * 10**9,
        8 * 10**6,
        "vvvvvvvm",
        "v",
        [big((HALF, 4 * MAIN), BF16), big((HALF, 4 * REST), BF16)],
    )
    moved, space_grad = lax.optimization_barrier((moved, space_grad))
    time_out = call(
        time_back_kernel,
        shaped((3, TOKENS, ATT), BF16),
        (moved, time, time_weights),
        10**9,
        5 * 10**6,
        "vvm",
        "v",
        [big((3, TOKENS, ATT), F32)],
    )
    return (
        space_grad.swapaxes(1, 2).reshape(3, 1, 1, TOKENS, ATT),
        time_out.reshape(3, 1, FRAMES, 8, ATT),
        score_grad,
    )


def solution(mesh):
    fine = Mesh(mesh.devices.reshape(2, 4, 2, 4, 8), ("zh", "y", "c", "x", "zl"))
    in_specs = (
        P(None, VID, None, SEQ, None),
        P(None, VID, SEQ, None, None),
        P(VID, SEQ, None, None),
        P(SEQ, VID),
        P(SEQ, VID),
        P(),
        P(VID, None),
        P(VID, None),
    )
    out_specs = (
        P(None, VID, SEQ, None, None),
        P(None, VID, None, SEQ, None),
        P(VID, None),
    )
    return jax.shard_map(shards, mesh=fine, in_specs=in_specs, out_specs=out_specs, check_vma=False)
```

```python
import math

import jax
import jax.numpy as jnp
from jax import lax
from jax.experimental import pallas as pl
from jax.experimental.pallas import tpu as pltpu
from jax.sharding import Mesh
from jax.sharding import PartitionSpec as P

HEAD_DIM = 88
HEADS = 8
ATT = 704
WIDTH = 1408
HALF = 704
TOKENS = 256
VIDEOS = 16
FRAMES = 32
PAIR = 2 * HEAD_DIM
WINDOW = 96
BACK = PAIR - WINDOW
VID = ("zh", "y", "c")
SEQ = ("x", "zl")
RING = ("zh", "zl")
SIZES = {"zh": 2, "y": 4, "c": 2, "x": 4, "zl": 8}

logit_scale = 20.0
teacher_softness = 4.0
F32 = jnp.float32
BF16 = jnp.bfloat16
ROOT = 1.0 / math.sqrt(HEAD_DIM)
VMEM = pl.BlockSpec(memory_space=pltpu.VMEM)
SMEM = pl.BlockSpec(memory_space=pltpu.SMEM)
HBM = pl.BlockSpec(memory_space=pltpu.HBM)
MAIN = 128
REST = PAIR - MAIN
FOLD = 96
PACKED = PAIR + FOLD
LABELLED = PACKED + 16


def dot(a, b, contract):
    return lax.dot_general(a, b, (contract, ((), ())), preferred_element_type=F32)


NN = ((1,), (0,))
NT = ((1,), (1,))
TN = ((0,), (0,))


def call(kernel, out_shape, args, flops, moved, ins="", outs="", scratch=(), copies=0):
    places = {"s": SMEM, "v": VMEM, "m": VMEM, "h": HBM}
    pinned = {"m": pltpu.VMEM, "h": pltpu.HBM}
    sems = [pltpu.SemaphoreType.DMA((copies,))] if copies else []
    single = not isinstance(out_shape, tuple)
    shapes = [
        pinned[p](o.shape, o.dtype) if p in pinned else o
        for o, p in zip((out_shape,) if single else out_shape, outs)
    ]
    specs = [places[p] for p in outs]
    args = [
        pltpu.with_memory_space_constraint(a, pinned[p]) if p in pinned else a
        for a, p in zip(args, ins)
    ]
    return pl.pallas_call(
        kernel,
        out_shape=shapes[0] if single else tuple(shapes),
        in_specs=[places[p] for p in ins],
        out_specs=specs[0] if single else tuple(specs),
        scratch_shapes=list(scratch) + sems,
        compiler_params=pltpu.CompilerParams(vmem_limit_bytes=20 * 2**20),
        cost_estimate=pl.CostEstimate(flops=flops, bytes_accessed=moved, transcendentals=0),
    )(*args)


def begin(source, target, sem):
    copy = pltpu.make_async_copy(source, target, sem)
    copy.start()
    return copy


def spread(block, axes):
    count = math.prod(SIZES[axis] for axis in axes)
    return lax.all_to_all(jnp.broadcast_to(block[None], (count,) + block.shape), axes, 0, 0)


def swap(block, axis):
    return lax.ppermute(block, axis, [(0, 1), (1, 0)])


def halves(rows):
    parts = []
    for c in range(2):
        blocks = [(zh * 4 + y) * 2 + c for y in range(4) for zh in range(2)]
        parts.append(
            jnp.concatenate([rows[:, b * HEAD_DIM : (b + 1) * HEAD_DIM] for b in blocks], axis=1)
        )
    return parts


def split_kernel(core_ref, res_ref, gain_ref, res_out, gain_out):
    core = core_ref[0]
    for ref, out in ((res_ref, res_out), (gain_ref, gain_out)):
        parts = halves(ref[...])
        for c in range(2):
            out[core ^ c] = parts[c]


ROWS = 22
LATE = 10
SIDE = 128 - HEAD_DIM
TEXT = 44
TEXT_ROW = 27


def pack_kernel(place_ref, space_hbm, time_hbm, text_hbm, out, space_ref, time_ref, text_ref, sems):
    piece = place_ref[0]
    loads = [
        begin(space_hbm, space_ref, sems.at[0]),
        begin(time_hbm, time_ref, sems.at[1]),
        begin(text_hbm, text_ref, sems.at[2]),
    ]
    for load in loads:
        load.wait()
    time = time_ref[...].astype(F32)
    late = time[LATE:]
    side = [late[:, :SIDE], late[:, SIDE : 2 * SIDE]]
    ends = [late[i : i + 1, 2 * SIDE :] for i in range(ROWS - LATE)]
    ends += [jnp.zeros((1, HEAD_DIM - 2 * SIDE), F32)] * 3
    side += [jnp.concatenate(ends[5 * i : 5 * i + 5], axis=1) for i in range(3)]
    text = jnp.zeros((1, TEXT), F32)
    for i in range(32):
        text = jnp.where(piece == i, text_ref[:, TEXT * i : TEXT * (i + 1)], text)
    high = text.astype(BF16).astype(F32)
    for term in (high, text - high):
        blank = jnp.zeros((1, 2 * SIDE - TEXT), F32)
        side += [term[:, :SIDE], jnp.concatenate([term[:, SIDE:], blank], axis=1)]
    side.append(jnp.zeros((1, SIDE), F32))
    main = jnp.concatenate([space_ref[...].astype(F32), time[:LATE]])
    rows = jnp.concatenate([main, jnp.concatenate(side)], axis=1).astype(BF16)
    for i in range(16):
        out[i] = rows


def assemble_kernel(ring_ref, space_out, time_out, pieces, sems):
    rows = []
    for term in range(2):
        for zh in range(2):
            blocks = ring_ref[8 * zh : 8 * zh + 8].astype(F32)
            first = TEXT_ROW + 2 * term
            parts = jnp.concatenate(
                [blocks[:, first, HEAD_DIM:], blocks[:, first + 1, HEAD_DIM : HEAD_DIM + TEXT - SIDE]],
                axis=1,
            )
            for q in range(4):
                both = [parts[2 * q : 2 * q + 1], parts[2 * q + 1 : 2 * q + 2]]
                rows.append(jnp.concatenate(both, axis=1))
    rows = jnp.concatenate([jnp.concatenate(rows), jnp.zeros((16, SIDE), F32)], axis=1)
    pieces[0, PACKED:] = rows.astype(BF16)

    line = lax.broadcasted_iota(jnp.int32, (256, 1), 0) & 31
    ahead = lax.broadcasted_iota(jnp.int32, (256, PAIR), 1) - ROWS * (
        lax.broadcasted_iota(jnp.int32, (256, PAIR), 0) >> 5
    )

    def pick(first, count, target, step=1):
        there = (line >= first) & (line < first + count)
        column = jnp.where(there, (line - first) * step + target, -1000)
        return (ahead == column).astype(F32).astype(BF16)

    picks = [pick(0, ROWS, 0), pick(ROWS, LATE, 0)]
    picks += [pick(0, ROWS - LATE, LATE), pick(ROWS - LATE, ROWS - LATE, LATE)]
    picks += [pick(24, 3 if n < 2 else 2, LATE + n, 5) for n in range(5)]
    copies = []
    ring = [ring_ref[8 * zh : 8 * zh + 8].reshape(256, 128) for zh in range(2)]
    for slot in range(2):
        both = []
        for zh in range(2):
            if slot == 0:
                both.append(dot(ring[zh], picks[0], TN)[:HEAD_DIM])
                continue
            main = dot(ring[zh], picks[1], TN)[:HEAD_DIM]
            side = [dot(ring[zh], p, TN)[HEAD_DIM:] for p in picks[2:4]]
            width = HEAD_DIM - 2 * SIDE
            last = sum(
                dot(ring[zh], p, TN)[HEAD_DIM + width * n : HEAD_DIM + width * (n + 1)]
                for n, p in enumerate(picks[4:])
            )
            both.append(main + jnp.concatenate(side + [last]))
        whole = jnp.concatenate(both)
        rest = whole[:, MAIN:]
        low = jnp.concatenate([rest[FOLD:], jnp.zeros((2 * FOLD - PAIR, REST), F32)])
        fold = jnp.concatenate([rest[:FOLD], low, jnp.zeros((FOLD, 128 - 2 * REST), F32)], axis=1)
        pieces[slot, :PAIR] = whole[:, :MAIN].astype(BF16)
        pieces[slot, PAIR:PACKED] = fold.astype(BF16)
        if slot == 0:
            for i in range(16):
                copies.append(begin(pieces.at[0], space_out.at[i], sems.at[i]))
        else:
            copies.append(begin(pieces.at[1, pl.ds(0, PACKED)], time_out, sems.at[16]))
    for copy in copies:
        copy.wait()


def unfold(packed, wide, narrow):
    for y in range(4):
        rows = slice(PAIR * y, PAIR * (y + 1))
        rest = []
        for x in range(4):
            wide[rows, MAIN * x : MAIN * (x + 1)] = packed[4 * x + y, :PAIR]
            fold = packed[4 * x + y, PAIR:PACKED]
            rest.append(jnp.concatenate([fold[:, :REST], fold[: PAIR - FOLD, REST : 2 * REST]]))
        narrow[rows] = jnp.concatenate(rest, axis=1)


def head_rows(head):
    start = (head // 2) * PAIR + (head % 2) * BACK
    return slice(start, start + WINDOW)


def head_valid(head):
    row = lax.broadcasted_iota(jnp.int32, (WINDOW, 1), 0)
    return row < HEAD_DIM if head % 2 == 0 else row >= WINDOW - HEAD_DIM


def own_rows(block, head):
    return block[:HEAD_DIM] if head % 2 == 0 else block[WINDOW - HEAD_DIM :]


def keep(valid, block):
    return jnp.where(valid, block, jnp.zeros_like(block))


def softmax_down(scores):
    peak = jnp.max(scores, axis=0, keepdims=True)
    weights = jnp.exp(scores - peak)
    return (weights * (1.0 / jnp.sum(weights, axis=0, keepdims=True))).astype(BF16)


def slopes_down(weights, dots):
    weights = weights.astype(F32)
    delta = jnp.sum(weights * dots, axis=0, keepdims=True)
    return (weights * (dots - delta) * ROOT).astype(BF16)


def space_forward_kernel(qkv_ref, weights_out, wide_out, narrow_out, down):
    pair = []
    for head in range(HEADS):
        rows, valid = head_rows(head), head_valid(head)
        scores = dot(qkv_ref[1, rows], keep(valid, qkv_ref[0, rows]), TN) * ROOT
        weights = softmax_down(scores)
        weights_out[head] = weights
        pair.append(own_rows(dot(qkv_ref[2, rows], weights, NN), head))
        if head % 2:
            x = head // 2
            both = jnp.concatenate(pair)
            wide_out[:, MAIN * x : MAIN * (x + 1)] = both[:MAIN].T.astype(BF16)
            down[REST * x : REST * (x + 1)] = both[MAIN:]
            pair = []
    narrow_out[...] = down[...].T.astype(BF16)


def space_back_kernel(
    normed_ref, inv_ref, pulls_ref, token_ref, own_ref, other_ref, qkv_ref, weights_ref, out, wide, narrow
):
    grads = []
    for half, w_ref in enumerate((own_ref, other_ref)):
        unfold(w_ref, wide, narrow)
        token = jnp.sum(pulls_ref[TOKENS:, :1] * token_ref[half], axis=0, keepdims=True)
        mixed = inv_ref[:, :1] * (token - normed_ref[half].astype(F32) * pulls_ref[:TOKENS, :1])
        mixed = mixed.astype(BF16)
        grads.append((dot(mixed, wide[...], NN), dot(mixed, narrow[...], NN)))
    main = (grads[0][0] + grads[1][0]).T.astype(BF16)
    rest = (grads[0][1] + grads[1][1]).T.astype(BF16)
    for x in range(4):
        grad = jnp.concatenate([main[MAIN * x : MAIN * (x + 1)], rest[REST * x : REST * (x + 1)]])
        pairs = [[], [], []]
        for head in (2 * x, 2 * x + 1):
            rows, valid = head_rows(head), head_valid(head)
            grad_rows = grad[:WINDOW] if head % 2 == 0 else grad[BACK:]
            dots = dot(qkv_ref[2, rows], keep(valid, grad_rows), TN)
            weights = weights_ref[head]
            slopes = slopes_down(weights, dots)
            pairs[0].append(own_rows(dot(qkv_ref[1, rows], slopes, NN), head))
            pairs[1].append(own_rows(dot(qkv_ref[0, rows], slopes, NT), head))
            pairs[2].append(own_rows(dot(grad_rows, weights, NT), head))
        for slot in range(3):
            out[slot, x * PAIR : (x + 1) * PAIR] = jnp.concatenate(pairs[slot]).astype(BF16)


def head_lanes(head):
    start = (head * HEAD_DIM) // 128 * 128
    width = min(256, ATT - start)
    lane = lax.broadcasted_iota(jnp.int32, (1, width), 1) + (start - head * HEAD_DIM)
    return slice(start, start + width), (lane >= 0) & (lane < HEAD_DIM)


def time_forward_kernel(qkv_ref, weights_out):
    key = lax.broadcasted_iota(jnp.int32, (TOKENS, TOKENS), 0)
    query = lax.broadcasted_iota(jnp.int32, (TOKENS, TOKENS), 1)
    same = ((key ^ query) & 7) == 0
    for head in range(HEADS):
        lanes, valid = head_lanes(head)
        scores = dot(qkv_ref[1, :, lanes], keep(valid, qkv_ref[0, :, lanes]), NT) * ROOT
        weights_out[head] = softmax_down(jnp.where(same, scores, -1e30))


def time_back_kernel(grad_ref, qkv_ref, weights_ref, out, slopes, result, sems):
    copies = []

    def put(slot, head, part):
        lanes, valid = head_lanes(head)
        result[slot, :, lanes] = jnp.where(valid, part.astype(BF16), result[slot, :, lanes])

    for head in range(HEADS):
        lanes, valid = head_lanes(head)
        grad = grad_ref[:, lanes]
        dots = dot(qkv_ref[2, :, lanes], keep(valid, grad), NT)
        slopes[head] = slopes_down(weights_ref[head], dots)
        put(2, head, dot(weights_ref[head], grad, NN))
    copies.append(begin(result.at[2], out.at[2], sems.at[2]))
    for slot, contract in ((1, NN), (0, TN)):
        for head in range(HEADS):
            put(slot, head, dot(slopes[head], qkv_ref[1 - slot, :, head_lanes(head)[0]], contract))
        copies.append(begin(result.at[slot], out.at[slot], sems.at[slot]))
    for copy in copies:
        copy.wait()


def labels_of(y, core, half):
    row = lax.broadcasted_iota(jnp.int32, (8, 1), 0)
    return (row // 4 * 4 + y) * 2 + (core ^ half)


def embed_own_kernel(wide_ref, narrow_ref, res_ref, own_ref, out, w_wide, w_narrow):
    unfold(own_ref, w_wide, w_narrow)
    out[...] = (
        res_ref[0].astype(F32)
        + dot(wide_ref[...], w_wide[...], NT)
        + dot(narrow_ref[...], w_narrow[...], NT)
    )


def embed_kernel(
    place_ref,
    wide_ref,
    narrow_ref,
    res_ref,
    mixed_ref,
    own_ref,
    other_ref,
    gain_ref,
    normed_out,
    inv_out,
    unit_out,
    norm_out,
    text_out,
    row_out,
    w_wide,
    w_narrow,
    normed,
    inv_kept,
    texts,
    sems,
):
    core = place_ref[0]
    unfold(other_ref, w_wide, w_narrow)
    for half, ref in enumerate((own_ref, other_ref)):
        for y in range(4):
            tiles, square = [], 0.0
            for x in range(4):
                terms = ref[4 * x + y, PACKED:].astype(F32)
                tiles.append(terms[:8] + terms[8:])
                square += jnp.sum(tiles[x] * tiles[x], axis=1, keepdims=True)
            upper = lax.broadcasted_iota(jnp.int32, (8, 1), 0) < 4
            first = jnp.sum(jnp.where(upper, square, 0.0), axis=0, keepdims=True)
            second = jnp.sum(jnp.where(upper, 0.0, square), axis=0, keepdims=True)
            size = jnp.sqrt(jnp.where(upper, first, second) + 1e-06)
            for x in range(4):
                texts[half, 4 * x + y] = tiles[x] / size
    copies = [begin(texts, text_out, sems.at[3])]
    sums = [mixed_ref[...]]
    sums.append(
        res_ref[1].astype(F32)
        + dot(wide_ref[...], w_wide[...], NT)
        + dot(narrow_ref[...], w_narrow[...], NT)
    )
    mean = sum(jnp.sum(s, axis=1, keepdims=True) for s in sums) / WIDTH
    sums = [s - mean for s in sums]
    square = sum(jnp.sum(s * s, axis=1, keepdims=True) for s in sums) / WIDTH
    inv = 1.0 / jnp.sqrt(square + 1e-05)
    inv_kept[...] = jnp.broadcast_to(inv, (TOKENS, 128))
    copies.append(begin(inv_kept, inv_out, sems.at[0]))
    embs = []
    for half in range(2):
        part = sums[half] * inv
        normed[half] = part.astype(BF16)
        copies.append(begin(normed.at[half], normed_out.at[half], sems.at[1 + half]))
        embs.append(jnp.sum(part, axis=0, keepdims=True) * gain_ref[half] / TOKENS)
    norm = jnp.sqrt(sum(jnp.sum(e * e, axis=1, keepdims=True) for e in embs) + 1e-06)
    norm_out[...] = norm
    units = [e / norm for e in embs]
    for half in range(2):
        unit_out[half] = units[half]
    by_core = [jnp.where(core == c, units[0], units[1]) for c in range(2)]
    blank = jnp.zeros((8, 128 - HEAD_DIM), F32)
    blocks = []
    for x in range(4):
        four = []
        for q in range(4):
            start = ((x % 2 * 2 + q // 2) * 2 + x // 2) * HEAD_DIM
            four.append(by_core[q % 2][:, start : start + HEAD_DIM])
        blocks.append(jnp.concatenate([jnp.concatenate(four + four), blank], axis=1))
    lane = lax.broadcasted_iota(jnp.int32, (8, 128), 1)
    row = jnp.zeros((1, 128), F32)
    for half in range(2):
        for y in range(4):
            products = sum(texts[half, 4 * x + y] * blocks[x] for x in range(4))
            cosines = jnp.sum(products, axis=1, keepdims=True)
            here = lane == labels_of(y, core, half)
            row += jnp.sum(jnp.where(here, cosines, 0.0), axis=0, keepdims=True)
    row = row * (logit_scale / FRAMES)
    for i in range(VIDEOS):
        row_out[i] = row
    for copy in copies:
        copy.wait()


def video_of(core):
    row = lax.broadcasted_iota(jnp.int32, (VIDEOS, 1), 0)
    return ((row & 1) * 4 + ((row >> 1) & 3)) * 2 + (core ^ (row >> 3))


def basis_kernel(place_ref, normed_ref, unit_ref, norm_ref, gain_ref, text_hbm, token_out, cross_out, normed, cross, text_ref, sems):
    core = place_ref[0]
    load_text = begin(text_hbm, text_ref, sems.at[2])
    load = begin(normed_ref, normed, sems.at[0])
    load_text.wait()
    by_core = []
    for c in range(2):
        parts = []
        for y in range(4):
            for zh in range(2):
                x, q = 2 * zh + y // 2, y % 2 * 2 + c
                rows = []
                for half in range(2):
                    for at in range(4):
                        tile = text_ref[half, 4 * x + at]
                        rows += [tile[q : q + 1, :HEAD_DIM], tile[4 + q : 5 + q, :HEAD_DIM]]
                parts.append(jnp.concatenate(rows))
        by_core.append(jnp.concatenate(parts, axis=1))
    texts = [
        jnp.where(core == 0, by_core[0], by_core[1]),
        jnp.where(core == 0, by_core[1], by_core[0]),
    ]
    along = sum(jnp.sum(texts[h] * unit_ref[h], axis=1, keepdims=True) for h in range(2))
    scale = VIDEOS * logit_scale / norm_ref[...]
    token = [(texts[h] - unit_ref[h] * along) * scale * gain_ref[h] for h in range(2)]
    mean = sum(jnp.sum(t, axis=1, keepdims=True) for t in token) / WIDTH
    load.wait()
    columns = sum(dot(normed[h], token[h].astype(BF16), NT) for h in range(2)) * (1.0 / WIDTH)
    cross[...] = jnp.concatenate([columns, jnp.zeros((TOKENS, 128 - VIDEOS), F32)], axis=1)
    copy = begin(cross, cross_out, sems.at[1])
    for half in range(2):
        token_out[half] = token[half] - mean
    copy.wait()


def project_kernel(
    place_ref,
    w_ref,
    normed_ref,
    token_ref,
    wide_out,
    narrow_out,
    pull_wide_out,
    pull_narrow_out,
    w,
    normed,
    w_wide,
    w_narrow,
    wide,
    narrow,
    pull_wide,
    pull_narrow,
    sems,
):
    core = place_ref[0]
    loads = [begin(w_ref.at[:, core ^ half], w.at[half], sems.at[half]) for half in range(2)]
    load_normed = begin(normed_ref, normed, sems.at[2])
    sums = [0.0] * 4
    for half in range(2):
        token = token_ref[half]
        high = token.astype(BF16)
        terms = jnp.concatenate([high.astype(F32), token - high.astype(F32)]).astype(BF16)
        loads[half].wait()
        unfold(w.at[half], w_wide, w_narrow)
        if half == 0:
            load_normed.wait()
        for i, part in enumerate((w_wide, w_narrow)):
            sums[i] += dot(normed[half], part[...], NN)
            sums[2 + i] += dot(terms, part[...], NN)
    wide[...] = sums[0].astype(BF16)
    narrow[...] = sums[1].astype(BF16)
    copies = [begin(wide, wide_out, sems.at[3]), begin(narrow, narrow_out, sems.at[4])]
    pull_wide[...] = sums[2][:VIDEOS] + sums[2][VIDEOS:]
    pull_narrow[...] = sums[3][:VIDEOS] + sums[3][VIDEOS:]
    copies.append(begin(pull_wide, pull_wide_out, sems.at[5]))
    copies.append(begin(pull_narrow, pull_narrow_out, sems.at[6]))
    for copy in copies:
        copy.wait()


def score_kernel(
    place_ref,
    shares_ref,
    teacher_ref,
    inv_ref,
    cross_ref,
    wide_ref,
    narrow_ref,
    pull_wide_ref,
    pull_narrow_ref,
    score_out,
    rows_out,
    time_out,
    inv,
    cross,
    wide,
    narrow,
    pull_wide,
    pull_narrow,
    rows,
    result,
    sems,
):
    core, own = place_ref[0], place_ref[1]
    pairs = (
        (cross_ref, cross),
        (pull_wide_ref, pull_wide),
        (pull_narrow_ref, pull_narrow),
        (inv_ref, inv),
        (wide_ref, wide),
        (narrow_ref, narrow),
    )
    loads = [begin(source, target, sems.at[i]) for i, (source, target) in enumerate(pairs)]
    scores = shares_ref[...].reshape(8, 4, 2, 128).sum(axis=1)
    video = lax.broadcasted_iota(jnp.int32, scores.shape, 0) + 8 * lax.broadcasted_iota(
        jnp.int32, scores.shape, 1
    )
    lane = lax.broadcasted_iota(jnp.int32, (1, 128), 1)
    exps = jnp.exp(scores)
    own_exp = jnp.sum(jnp.sum(jnp.where(video == own, exps, 0.0), axis=0), axis=0, keepdims=True)
    own_exp = jnp.where(lane < VIDEOS, own_exp, 0.0)
    column = jnp.sum(jnp.sum(exps, axis=0), axis=0, keepdims=True)
    row_soft = own_exp / jnp.sum(own_exp, axis=1, keepdims=True)
    col_soft = own_exp / column
    teacher = jnp.exp(teacher_ref[...].astype(F32) / teacher_softness)
    teacher = jnp.where(lane < VIDEOS, teacher, 0.0)
    teacher_soft = teacher / jnp.sum(teacher, axis=1, keepdims=True)
    one_hot = (lane == own).astype(F32)
    score_grad = (row_soft - one_hot + (col_soft - one_hot)) / (2.0 * VIDEOS) + (
        row_soft - teacher_soft
    ) / VIDEOS
    score_out[...] = score_grad[:, :VIDEOS]
    columns = lax.broadcasted_iota(jnp.int32, (VIDEOS, 128), 1)
    pull = jnp.sum(
        jnp.where(columns == video_of(core), score_grad, 0.0), axis=1, keepdims=True
    )
    rows[TOKENS:] = jnp.broadcast_to(pull, (VIDEOS, 128))
    column = lax.broadcasted_iota(jnp.int32, (VIDEOS, VIDEOS), 1)
    row = lax.broadcasted_iota(jnp.int32, (VIDEOS, VIDEOS), 0)
    pull_row = jnp.sum(jnp.where(row == column, pull, 0.0), axis=0, keepdims=True)
    for load in loads:
        load.wait()
    along = jnp.sum(cross[:, :VIDEOS] * pull_row, axis=1, keepdims=True)
    rows[:TOKENS] = jnp.broadcast_to(along, (TOKENS, 128))
    copy = begin(rows, rows_out, sems.at[6])
    base_wide = jnp.sum(pull * pull_wide[...], axis=0, keepdims=True)
    base_narrow = jnp.sum(pull * pull_narrow[...], axis=0, keepdims=True)
    scale = inv[:, :1]
    out_wide = scale * (base_wide - along * wide[...].astype(F32))
    out_narrow = scale * (base_narrow - along * narrow[...].astype(F32))
    parts = []
    for x in range(4):
        parts += [out_wide[:, MAIN * x : MAIN * (x + 1)], out_narrow[:, REST * x : REST * (x + 1)]]
    result[...] = jnp.concatenate(parts, axis=1).astype(BF16)
    send = begin(result, time_out, sems.at[7])
    copy.wait()
    send.wait()


def shaped(shape, dtype):
    return jax.ShapeDtypeStruct(shape, dtype)


def shards(time_qkv, space_qkv, residual, space_proj, time_proj, norm_gain, text_emb, teacher):
    core = lax.axis_index("c")
    own_video = lax.axis_index(VID)
    big = pltpu.VMEM
    place = jnp.stack([core, own_video])
    pack = call(
        pack_kernel,
        shaped((16, 32, 128), BF16),
        (lax.axis_index(SEQ)[None], space_proj, time_proj, text_emb),
        10**5,
        10**6,
        "shhh",
        "v",
        [big(space_proj.shape, BF16), big(time_proj.shape, BF16), big(text_emb.shape, F32)],
        3,
    )
    ring = lax.all_to_all(pack, RING, 0, 0)

    space_copies, time_piece = call(
        assemble_kernel,
        (shaped((16, LABELLED, 128), BF16), shaped((PACKED, 128), BF16)),
        (ring,),
        2 * 10**7,
        2 * 10**6,
        "v",
        "hh",
        [big((2, LABELLED, 128), BF16)],
        17,
    )
    w_time = lax.all_gather(time_piece, ("x", "y", "c")).reshape(16, 2, PACKED, 128)
    w_own = lax.all_to_all(space_copies, ("x", "y"), 0, 0)

    space = space_qkv.reshape(3, TOKENS, ATT).swapaxes(1, 2)
    space_weights, att_wide, att_narrow = call(
        space_forward_kernel,
        (
            shaped((HEADS, TOKENS, TOKENS), BF16),
            shaped((TOKENS, 4 * MAIN), BF16),
            shaped((TOKENS, 4 * REST), BF16),
        ),
        (space,),
        6 * 10**8,
        3 * 10**6,
        "v",
        "mmm",
        [big((4 * REST, TOKENS), F32)],
    )
    res, gain = call(
        split_kernel,
        (shaped((2, TOKENS, HALF), BF16), shaped((2, 1, HALF), F32)),
        (core[None], residual.reshape(TOKENS, WIDTH), norm_gain[None]),
        10**8,
        2 * 10**6,
        "svv",
        "mm",
    )
    time = time_qkv.reshape(3, TOKENS, ATT)
    time_weights = call(
        time_forward_kernel,
        shaped((HEADS, TOKENS, TOKENS), BF16),
        (time,),
        6 * 10**8,
        3 * 10**6,
        "v",
        "m",
    )
    w_own, time_weights, res, gain, att_wide, att_narrow = lax.optimization_barrier(
        (w_own, time_weights, res, gain, att_wide, att_narrow)
    )
    w_other = swap(w_own, "c")
    mixed_own = call(
        embed_own_kernel,
        shaped((TOKENS, HALF), F32),
        (att_wide, att_narrow, res, w_own),
        5 * 10**8,
        3 * 10**6,
        "mmmv",
        "m",
        [big((HALF, 4 * MAIN), BF16), big((HALF, 4 * REST), BF16)],
    )
    w_other, mixed_own = lax.optimization_barrier((w_other, mixed_own))
    normed, inv, unit, norm, text, row = call(
        embed_kernel,
        (
            shaped((2, TOKENS, HALF), BF16),
            shaped((TOKENS, 128), F32),
            shaped((2, 1, HALF), F32),
            shaped((1, 1), F32),
            shaped((2, 16, 8, 128), F32),
            shaped((VIDEOS, 1, 128), F32),
        ),
        (core[None], att_wide, att_narrow, res, mixed_own, w_own, w_other, gain),
        10**9,
        6 * 10**6,
        "smmmmvvm",
        "hhvvhv",
        [
            big((HALF, 4 * MAIN), BF16),
            big((HALF, 4 * REST), BF16),
            big((2, TOKENS, HALF), BF16),
            big((TOKENS, 128), F32),
            big((2, 16, 8, 128), F32),
        ],
        4,
    )
    ring_rows = lax.all_to_all(row, RING, 0, 0)
    token, cross = call(
        basis_kernel,
        (shaped((2, VIDEOS, HALF), F32), shaped((TOKENS, 128), F32)),
        (core[None], normed, unit, norm, gain, text),
        10**8,
        2 * 10**6,
        "shvvmh",
        "vh",
        [big((2, TOKENS, HALF), BF16), big((TOKENS, 128), F32), big((2, 16, 8, 128), F32)],
        3,
    )
    ring_rows, token, cross = lax.optimization_barrier((ring_rows, token, cross))
    shares = spread(ring_rows.reshape(2, 8, 128).sum(axis=1), ("y", "c", "x"))
    wide, narrow, pull_wide, pull_narrow = call(
        project_kernel,
        (
            shaped((TOKENS, 4 * MAIN), BF16),
            shaped((TOKENS, 4 * REST), BF16),
            shaped((VIDEOS, 4 * MAIN), F32),
            shaped((VIDEOS, 4 * REST), F32),
        ),
        (core[None], w_time, normed, token),
        5 * 10**8,
        5 * 10**6,
        "shhv",
        "hhhh",
        [
            big((2, 16, PACKED, 128), BF16),
            big((2, TOKENS, HALF), BF16),
            big((HALF, 4 * MAIN), BF16),
            big((HALF, 4 * REST), BF16),
            big((TOKENS, 4 * MAIN), BF16),
            big((TOKENS, 4 * REST), BF16),
            big((VIDEOS, 4 * MAIN), F32),
            big((VIDEOS, 4 * REST), F32),
        ],
        7,
    )
    shares, wide, narrow, pull_wide, pull_narrow = lax.optimization_barrier(
        (shares, wide, narrow, pull_wide, pull_narrow)
    )
    score_grad, pulls, time_grad = call(
        score_kernel,
        (
            shaped((1, VIDEOS), F32),
            shaped((TOKENS + VIDEOS, 128), F32),
            shaped((TOKENS, ATT), BF16),
        ),
        (
            place,
            shares,
            jnp.pad(teacher, ((0, 0), (0, 128 - VIDEOS))),
            inv,
            cross,
            wide,
            narrow,
            pull_wide,
            pull_narrow,
        ),
        10**7,
        10**6,
        "svvhhhhhh",
        "vhh",
        [
            big((TOKENS, 128), F32),
            big((TOKENS, 128), F32),
            big((TOKENS, 4 * MAIN), BF16),
            big((TOKENS, 4 * REST), BF16),
            big((VIDEOS, 4 * MAIN), F32),
            big((VIDEOS, 4 * REST), F32),
            big((TOKENS + VIDEOS, 128), F32),
            big((TOKENS, ATT), BF16),
        ],
        8,
    )
    moved = lax.all_to_all(time_grad.reshape(FRAMES, 8, ATT), SEQ, 0, 0).reshape(TOKENS, ATT)
    space_grad = call(
        space_back_kernel,
        shaped((3, ATT, TOKENS), BF16),
        (normed, inv, pulls, token, w_own, w_other, space, space_weights),
        2 * 10**9,
        8 * 10**6,
        "vvvvvvvm",
        "v",
        [big((HALF, 4 * MAIN), BF16), big((HALF, 4 * REST), BF16)],
    )
    moved, space_grad = lax.optimization_barrier((moved, space_grad))
    time_out = call(
        time_back_kernel,
        shaped((3, TOKENS, ATT), BF16),
        (moved, time, time_weights),
        10**9,
        5 * 10**6,
        "vvm",
        "h",
        [big((HEADS, TOKENS, TOKENS), BF16), big((3, TOKENS, ATT), BF16)],
        3,
    )
    return (
        space_grad.swapaxes(1, 2).reshape(3, 1, 1, TOKENS, ATT),
        time_out.reshape(3, 1, FRAMES, 8, ATT),
        score_grad,
    )


def solution(mesh):
    fine = Mesh(mesh.devices.reshape(2, 4, 2, 4, 8), ("zh", "y", "c", "x", "zl"))
    in_specs = (
        P(None, VID, None, SEQ, None),
        P(None, VID, SEQ, None, None),
        P(VID, SEQ, None, None),
        P(SEQ, VID),
        P(SEQ, VID),
        P(),
        P(VID, None),
        P(VID, None),
    )
    out_specs = (
        P(None, VID, SEQ, None, None),
        P(None, VID, None, SEQ, None),
        P(VID, None),
    )
    return jax.shard_map(shards, mesh=fine, in_specs=in_specs, out_specs=out_specs, check_vma=False)
```

```python
import math

import jax
import jax.numpy as jnp
from jax import lax
from jax.experimental import pallas as pl
from jax.experimental.pallas import tpu as pltpu
from jax.sharding import Mesh
from jax.sharding import PartitionSpec as P

HEAD_DIM = 88
HEADS = 8
ATT = 704
WIDTH = 1408
HALF = 704
TOKENS = 256
VIDEOS = 16
FRAMES = 32
PAIR = 2 * HEAD_DIM
WINDOW = 96
BACK = PAIR - WINDOW
VID = ("zh", "y", "c")
SEQ = ("x", "zl")
RING = ("zh", "zl")
SIZES = {"zh": 2, "y": 4, "c": 2, "x": 4, "zl": 8}

logit_scale = 20.0
teacher_softness = 4.0
F32 = jnp.float32
BF16 = jnp.bfloat16
ROOT = 1.0 / math.sqrt(HEAD_DIM)
VMEM = pl.BlockSpec(memory_space=pltpu.VMEM)
SMEM = pl.BlockSpec(memory_space=pltpu.SMEM)
HBM = pl.BlockSpec(memory_space=pltpu.HBM)
MAIN = 128
REST = PAIR - MAIN
FOLD = 96
PACKED = PAIR + FOLD
LABELLED = PACKED + 16


def dot(a, b, contract):
    return lax.dot_general(a, b, (contract, ((), ())), preferred_element_type=F32)


NN = ((1,), (0,))
NT = ((1,), (1,))
TN = ((0,), (0,))


def call(kernel, out_shape, args, flops, moved, ins="", outs="", scratch=(), copies=0):
    places = {"s": SMEM, "v": VMEM, "m": VMEM, "h": HBM}
    pinned = {"m": pltpu.VMEM, "h": pltpu.HBM}
    sems = [pltpu.SemaphoreType.DMA((copies,))] if copies else []
    single = not isinstance(out_shape, tuple)
    shapes = [
        pinned[p](o.shape, o.dtype) if p in pinned else o
        for o, p in zip((out_shape,) if single else out_shape, outs)
    ]
    specs = [places[p] for p in outs]
    args = [
        pltpu.with_memory_space_constraint(a, pinned[p]) if p in pinned else a
        for a, p in zip(args, ins)
    ]
    return pl.pallas_call(
        kernel,
        out_shape=shapes[0] if single else tuple(shapes),
        in_specs=[places[p] for p in ins],
        out_specs=specs[0] if single else tuple(specs),
        scratch_shapes=list(scratch) + sems,
        compiler_params=pltpu.CompilerParams(vmem_limit_bytes=20 * 2**20),
        cost_estimate=pl.CostEstimate(flops=flops, bytes_accessed=moved, transcendentals=0),
    )(*args)


def begin(source, target, sem):
    copy = pltpu.make_async_copy(source, target, sem)
    copy.start()
    return copy


def spread(block, axes):
    count = math.prod(SIZES[axis] for axis in axes)
    return lax.all_to_all(jnp.broadcast_to(block[None], (count,) + block.shape), axes, 0, 0)


def swap(block, axis):
    return lax.ppermute(block, axis, [(0, 1), (1, 0)])


def halves(rows):
    parts = []
    for c in range(2):
        blocks = [(zh * 4 + y) * 2 + c for y in range(4) for zh in range(2)]
        parts.append(
            jnp.concatenate([rows[:, b * HEAD_DIM : (b + 1) * HEAD_DIM] for b in blocks], axis=1)
        )
    return parts


def split_kernel(core_ref, res_ref, gain_ref, res_out, gain_out):
    core = core_ref[0]
    for ref, out in ((res_ref, res_out), (gain_ref, gain_out)):
        parts = halves(ref[...])
        for c in range(2):
            out[core ^ c] = parts[c]


ROWS = 22
LATE = 10
SIDE = 128 - HEAD_DIM
TEXT = 44
TEXT_ROW = 27


def pack_kernel(place_ref, space_hbm, time_hbm, text_hbm, out, space_ref, time_ref, text_ref, sems):
    piece = place_ref[0]
    loads = [
        begin(space_hbm, space_ref, sems.at[0]),
        begin(time_hbm, time_ref, sems.at[1]),
        begin(text_hbm, text_ref.at[:, pl.ds(0, WIDTH)], sems.at[2]),
    ]
    for load in loads:
        load.wait()
    time = time_ref[...].astype(F32)
    late = time[LATE:]
    side = [late[:, :SIDE], late[:, SIDE : 2 * SIDE]]
    ends = [late[i : i + 1, 2 * SIDE :] for i in range(ROWS - LATE)]
    ends += [jnp.zeros((1, HEAD_DIM - 2 * SIDE), F32)] * 3
    side += [jnp.concatenate(ends[5 * i : 5 * i + 5], axis=1) for i in range(3)]
    start = piece * TEXT
    near = pl.multiple_of(start // 128 * 128, 128)
    window = jnp.broadcast_to(text_ref[:, pl.ds(near, 256)], (8, 256))
    text = pltpu.roll(window, 256 - (start - near), 1)[:1, :TEXT]
    high = text.astype(BF16).astype(F32)
    for term in (high, text - high):
        blank = jnp.zeros((1, 2 * SIDE - TEXT), F32)
        side += [term[:, :SIDE], jnp.concatenate([term[:, SIDE:], blank], axis=1)]
    side.append(jnp.zeros((1, SIDE), F32))
    main = jnp.concatenate([space_ref[...].astype(F32), time[:LATE]])
    rows = jnp.concatenate([main, jnp.concatenate(side)], axis=1).astype(BF16)
    for i in range(16):
        out[i] = rows


def assemble_kernel(ring_ref, space_out, time_out, pieces, sems):
    rows = []
    for term in range(2):
        for zh in range(2):
            blocks = ring_ref[8 * zh : 8 * zh + 8].astype(F32)
            first = TEXT_ROW + 2 * term
            parts = jnp.concatenate(
                [blocks[:, first, HEAD_DIM:], blocks[:, first + 1, HEAD_DIM : HEAD_DIM + TEXT - SIDE]],
                axis=1,
            )
            for q in range(4):
                both = [parts[2 * q : 2 * q + 1], parts[2 * q + 1 : 2 * q + 2]]
                rows.append(jnp.concatenate(both, axis=1))
    rows = jnp.concatenate([jnp.concatenate(rows), jnp.zeros((16, SIDE), F32)], axis=1)
    pieces[0, PACKED:] = rows.astype(BF16)

    line = lax.broadcasted_iota(jnp.int32, (256, 1), 0) & 31
    ahead = lax.broadcasted_iota(jnp.int32, (256, PAIR), 1) - ROWS * (
        lax.broadcasted_iota(jnp.int32, (256, PAIR), 0) >> 5
    )

    def pick(first, count, target, step=1):
        there = (line >= first) & (line < first + count)
        column = jnp.where(there, (line - first) * step + target, -1000)
        return (ahead == column).astype(F32).astype(BF16)

    picks = [pick(0, ROWS, 0), pick(ROWS, LATE, 0)]
    picks += [pick(0, ROWS - LATE, LATE), pick(ROWS - LATE, ROWS - LATE, LATE)]
    picks += [pick(24, 3 if n < 2 else 2, LATE + n, 5) for n in range(5)]
    copies = []
    ring = [ring_ref[8 * zh : 8 * zh + 8].reshape(256, 128) for zh in range(2)]
    for slot in range(2):
        both = []
        for zh in range(2):
            if slot == 0:
                both.append(dot(ring[zh], picks[0], TN)[:HEAD_DIM])
                continue
            main = dot(ring[zh], picks[1], TN)[:HEAD_DIM]
            side = [dot(ring[zh], p, TN)[HEAD_DIM:] for p in picks[2:4]]
            width = HEAD_DIM - 2 * SIDE
            last = sum(
                dot(ring[zh], p, TN)[HEAD_DIM + width * n : HEAD_DIM + width * (n + 1)]
                for n, p in enumerate(picks[4:])
            )
            both.append(main + jnp.concatenate(side + [last]))
        whole = jnp.concatenate(both)
        rest = whole[:, MAIN:]
        low = jnp.concatenate([rest[FOLD:], jnp.zeros((2 * FOLD - PAIR, REST), F32)])
        fold = jnp.concatenate([rest[:FOLD], low, jnp.zeros((FOLD, 128 - 2 * REST), F32)], axis=1)
        pieces[slot, :PAIR] = whole[:, :MAIN].astype(BF16)
        pieces[slot, PAIR:PACKED] = fold.astype(BF16)
        if slot == 0:
            for i in range(16):
                copies.append(begin(pieces.at[0], space_out.at[i], sems.at[i]))
        else:
            copies.append(begin(pieces.at[1, pl.ds(0, PACKED)], time_out, sems.at[16]))
    for copy in copies:
        copy.wait()


def unfold(packed, wide, narrow):
    for y in range(4):
        rows = slice(PAIR * y, PAIR * (y + 1))
        rest = []
        for x in range(4):
            wide[rows, MAIN * x : MAIN * (x + 1)] = packed[4 * x + y, :PAIR]
            fold = packed[4 * x + y, PAIR:PACKED]
            rest.append(jnp.concatenate([fold[:, :REST], fold[: PAIR - FOLD, REST : 2 * REST]]))
        narrow[rows] = jnp.concatenate(rest, axis=1)


def head_rows(head):
    start = (head // 2) * PAIR + (head % 2) * BACK
    return slice(start, start + WINDOW)


def head_valid(head):
    row = lax.broadcasted_iota(jnp.int32, (WINDOW, 1), 0)
    return row < HEAD_DIM if head % 2 == 0 else row >= WINDOW - HEAD_DIM


def own_rows(block, head):
    return block[:HEAD_DIM] if head % 2 == 0 else block[WINDOW - HEAD_DIM :]


def keep(valid, block):
    return jnp.where(valid, block, jnp.zeros_like(block))


def softmax_down(scores):
    peak = jnp.max(scores, axis=0, keepdims=True)
    weights = jnp.exp(scores - peak)
    return (weights * (1.0 / jnp.sum(weights, axis=0, keepdims=True))).astype(BF16)


def slopes_down(weights, dots):
    weights = weights.astype(F32)
    delta = jnp.sum(weights * dots, axis=0, keepdims=True)
    return (weights * (dots - delta) * ROOT).astype(BF16)


def space_forward_kernel(qkv_ref, weights_out, wide_out, narrow_out, down):
    pair = []
    for head in range(HEADS):
        rows, valid = head_rows(head), head_valid(head)
        scores = dot(qkv_ref[1, rows], keep(valid, qkv_ref[0, rows]), TN) * ROOT
        weights = softmax_down(scores)
        weights_out[head] = weights
        pair.append(own_rows(dot(qkv_ref[2, rows], weights, NN), head))
        if head % 2:
            x = head // 2
            both = jnp.concatenate(pair)
            wide_out[:, MAIN * x : MAIN * (x + 1)] = both[:MAIN].T.astype(BF16)
            down[REST * x : REST * (x + 1)] = both[MAIN:]
            pair = []
    narrow_out[...] = down[...].T.astype(BF16)


def space_back_kernel(
    normed_ref, inv_ref, pulls_ref, token_ref, own_ref, other_ref, qkv_ref, weights_ref, out, wide, narrow
):
    grads = []
    for half, w_ref in enumerate((own_ref, other_ref)):
        unfold(w_ref, wide, narrow)
        token = jnp.sum(pulls_ref[TOKENS:, :1] * token_ref[half], axis=0, keepdims=True)
        mixed = inv_ref[:, :1] * (token - normed_ref[half].astype(F32) * pulls_ref[:TOKENS, :1])
        mixed = mixed.astype(BF16)
        grads.append((dot(mixed, wide[...], NN), dot(mixed, narrow[...], NN)))
    main = (grads[0][0] + grads[1][0]).T.astype(BF16)
    rest = (grads[0][1] + grads[1][1]).T.astype(BF16)
    for x in range(4):
        grad = jnp.concatenate([main[MAIN * x : MAIN * (x + 1)], rest[REST * x : REST * (x + 1)]])
        pairs = [[], [], []]
        for head in (2 * x, 2 * x + 1):
            rows, valid = head_rows(head), head_valid(head)
            grad_rows = grad[:WINDOW] if head % 2 == 0 else grad[BACK:]
            dots = dot(qkv_ref[2, rows], keep(valid, grad_rows), TN)
            weights = weights_ref[head]
            slopes = slopes_down(weights, dots)
            pairs[0].append(own_rows(dot(qkv_ref[1, rows], slopes, NN), head))
            pairs[1].append(own_rows(dot(qkv_ref[0, rows], slopes, NT), head))
            pairs[2].append(own_rows(dot(grad_rows, weights, NT), head))
        for slot in range(3):
            out[slot, x * PAIR : (x + 1) * PAIR] = jnp.concatenate(pairs[slot]).astype(BF16)


def head_lanes(head):
    start = (head * HEAD_DIM) // 128 * 128
    width = min(256, ATT - start)
    lane = lax.broadcasted_iota(jnp.int32, (1, width), 1) + (start - head * HEAD_DIM)
    return slice(start, start + width), (lane >= 0) & (lane < HEAD_DIM)


def time_forward_kernel(qkv_ref, weights_out):
    key = lax.broadcasted_iota(jnp.int32, (TOKENS, TOKENS), 0)
    query = lax.broadcasted_iota(jnp.int32, (TOKENS, TOKENS), 1)
    same = ((key ^ query) & 7) == 0
    for head in range(HEADS):
        lanes, valid = head_lanes(head)
        scores = dot(qkv_ref[1, :, lanes], keep(valid, qkv_ref[0, :, lanes]), NT) * ROOT
        weights_out[head] = softmax_down(jnp.where(same, scores, -1e30))


def time_back_kernel(grad_ref, qkv_ref, weights_ref, out, slopes, result, sems):
    copies = []

    def put(slot, head, part):
        lanes, valid = head_lanes(head)
        result[slot, :, lanes] = jnp.where(valid, part.astype(BF16), result[slot, :, lanes])

    for head in range(HEADS):
        lanes, valid = head_lanes(head)
        grad = grad_ref[:, lanes]
        dots = dot(qkv_ref[2, :, lanes], keep(valid, grad), NT)
        slopes[head] = slopes_down(weights_ref[head], dots)
        put(2, head, dot(weights_ref[head], grad, NN))
    copies.append(begin(result.at[2], out.at[2], sems.at[2]))
    for slot, contract in ((1, NN), (0, TN)):
        for head in range(HEADS):
            put(slot, head, dot(slopes[head], qkv_ref[1 - slot, :, head_lanes(head)[0]], contract))
        copies.append(begin(result.at[slot], out.at[slot], sems.at[slot]))
    for copy in copies:
        copy.wait()


def labels_of(y, core, half):
    row = lax.broadcasted_iota(jnp.int32, (8, 1), 0)
    return (row // 4 * 4 + y) * 2 + (core ^ half)


def embed_own_kernel(wide_ref, narrow_ref, res_ref, own_ref, out, w_wide, w_narrow):
    unfold(own_ref, w_wide, w_narrow)
    out[...] = (
        res_ref[0].astype(F32)
        + dot(wide_ref[...], w_wide[...], NT)
        + dot(narrow_ref[...], w_narrow[...], NT)
    )


def embed_kernel(
    place_ref,
    wide_ref,
    narrow_ref,
    res_ref,
    mixed_ref,
    own_ref,
    other_ref,
    gain_ref,
    normed_out,
    inv_out,
    unit_out,
    norm_out,
    text_out,
    row_out,
    w_wide,
    w_narrow,
    normed,
    inv_kept,
    texts,
    sems,
):
    core = place_ref[0]
    unfold(other_ref, w_wide, w_narrow)
    for half, ref in enumerate((own_ref, other_ref)):
        for y in range(4):
            tiles, square = [], 0.0
            for x in range(4):
                terms = ref[4 * x + y, PACKED:].astype(F32)
                tiles.append(terms[:8] + terms[8:])
                square += jnp.sum(tiles[x] * tiles[x], axis=1, keepdims=True)
            upper = lax.broadcasted_iota(jnp.int32, (8, 1), 0) < 4
            first = jnp.sum(jnp.where(upper, square, 0.0), axis=0, keepdims=True)
            second = jnp.sum(jnp.where(upper, 0.0, square), axis=0, keepdims=True)
            size = jnp.sqrt(jnp.where(upper, first, second) + 1e-06)
            for x in range(4):
                texts[half, 4 * x + y] = tiles[x] / size
    copies = [begin(texts, text_out, sems.at[3])]
    sums = [mixed_ref[...]]
    sums.append(
        res_ref[1].astype(F32)
        + dot(wide_ref[...], w_wide[...], NT)
        + dot(narrow_ref[...], w_narrow[...], NT)
    )
    mean = sum(jnp.sum(s, axis=1, keepdims=True) for s in sums) / WIDTH
    sums = [s - mean for s in sums]
    square = sum(jnp.sum(s * s, axis=1, keepdims=True) for s in sums) / WIDTH
    inv = 1.0 / jnp.sqrt(square + 1e-05)
    inv_kept[...] = jnp.broadcast_to(inv, (TOKENS, 128))
    copies.append(begin(inv_kept, inv_out, sems.at[0]))
    embs = []
    for half in range(2):
        part = sums[half] * inv
        normed[half] = part.astype(BF16)
        copies.append(begin(normed.at[half], normed_out.at[half], sems.at[1 + half]))
        embs.append(jnp.sum(part, axis=0, keepdims=True) * gain_ref[half] / TOKENS)
    norm = jnp.sqrt(sum(jnp.sum(e * e, axis=1, keepdims=True) for e in embs) + 1e-06)
    norm_out[...] = norm
    units = [e / norm for e in embs]
    for half in range(2):
        unit_out[half] = units[half]
    by_core = [jnp.where(core == c, units[0], units[1]) for c in range(2)]
    blank = jnp.zeros((8, 128 - HEAD_DIM), F32)
    blocks = []
    for x in range(4):
        four = []
        for q in range(4):
            start = ((x % 2 * 2 + q // 2) * 2 + x // 2) * HEAD_DIM
            four.append(by_core[q % 2][:, start : start + HEAD_DIM])
        blocks.append(jnp.concatenate([jnp.concatenate(four + four), blank], axis=1))
    lane = lax.broadcasted_iota(jnp.int32, (8, 128), 1)
    row = jnp.zeros((1, 128), F32)
    for half in range(2):
        for y in range(4):
            products = sum(texts[half, 4 * x + y] * blocks[x] for x in range(4))
            cosines = jnp.sum(products, axis=1, keepdims=True)
            here = lane == labels_of(y, core, half)
            row += jnp.sum(jnp.where(here, cosines, 0.0), axis=0, keepdims=True)
    row = row * (logit_scale / FRAMES)
    for i in range(VIDEOS):
        row_out[i] = row
    for copy in copies:
        copy.wait()


def video_of(core):
    row = lax.broadcasted_iota(jnp.int32, (VIDEOS, 1), 0)
    return ((row & 1) * 4 + ((row >> 1) & 3)) * 2 + (core ^ (row >> 3))


def basis_kernel(place_ref, normed_ref, unit_ref, norm_ref, gain_ref, text_hbm, token_out, cross_out, normed, cross, text_ref, sems):
    core = place_ref[0]
    load_text = begin(text_hbm, text_ref, sems.at[2])
    load = begin(normed_ref, normed, sems.at[0])
    load_text.wait()
    by_core = []
    for c in range(2):
        parts = []
        for y in range(4):
            for zh in range(2):
                x, q = 2 * zh + y // 2, y % 2 * 2 + c
                rows = []
                for half in range(2):
                    for at in range(4):
                        tile = text_ref[half, 4 * x + at]
                        rows += [tile[q : q + 1, :HEAD_DIM], tile[4 + q : 5 + q, :HEAD_DIM]]
                parts.append(jnp.concatenate(rows))
        by_core.append(jnp.concatenate(parts, axis=1))
    texts = [
        jnp.where(core == 0, by_core[0], by_core[1]),
        jnp.where(core == 0, by_core[1], by_core[0]),
    ]
    along = sum(jnp.sum(texts[h] * unit_ref[h], axis=1, keepdims=True) for h in range(2))
    scale = VIDEOS * logit_scale / norm_ref[...]
    token = [(texts[h] - unit_ref[h] * along) * scale * gain_ref[h] for h in range(2)]
    mean = sum(jnp.sum(t, axis=1, keepdims=True) for t in token) / WIDTH
    load.wait()
    columns = sum(dot(normed[h], token[h].astype(BF16), NT) for h in range(2)) * (1.0 / WIDTH)
    cross[...] = jnp.concatenate([columns, jnp.zeros((TOKENS, 128 - VIDEOS), F32)], axis=1)
    copy = begin(cross, cross_out, sems.at[1])
    for half in range(2):
        token_out[half] = token[half] - mean
    copy.wait()


def project_kernel(
    place_ref,
    w_ref,
    normed_ref,
    token_ref,
    wide_out,
    narrow_out,
    pull_wide_out,
    pull_narrow_out,
    w,
    normed,
    w_wide,
    w_narrow,
    wide,
    narrow,
    pull_wide,
    pull_narrow,
    sems,
):
    core = place_ref[0]
    loads = [begin(w_ref.at[:, core ^ half], w.at[half], sems.at[half]) for half in range(2)]
    load_normed = begin(normed_ref, normed, sems.at[2])
    sums = [0.0] * 4
    for half in range(2):
        token = token_ref[half]
        high = token.astype(BF16)
        terms = jnp.concatenate([high.astype(F32), token - high.astype(F32)]).astype(BF16)
        loads[half].wait()
        unfold(w.at[half], w_wide, w_narrow)
        if half == 0:
            load_normed.wait()
        for i, part in enumerate((w_wide, w_narrow)):
            sums[i] += dot(normed[half], part[...], NN)
            sums[2 + i] += dot(terms, part[...], NN)
    wide[...] = sums[0].astype(BF16)
    narrow[...] = sums[1].astype(BF16)
    copies = [begin(wide, wide_out, sems.at[3]), begin(narrow, narrow_out, sems.at[4])]
    pull_wide[...] = sums[2][:VIDEOS] + sums[2][VIDEOS:]
    pull_narrow[...] = sums[3][:VIDEOS] + sums[3][VIDEOS:]
    copies.append(begin(pull_wide, pull_wide_out, sems.at[5]))
    copies.append(begin(pull_narrow, pull_narrow_out, sems.at[6]))
    for copy in copies:
        copy.wait()


def score_kernel(
    core_ref,
    own_ref,
    shares_ref,
    teacher_ref,
    inv_ref,
    cross_ref,
    wide_ref,
    narrow_ref,
    pull_wide_ref,
    pull_narrow_ref,
    score_out,
    rows_out,
    time_out,
    inv,
    cross,
    wide,
    narrow,
    pull_wide,
    pull_narrow,
    rows,
    result,
    sems,
):
    core, own = core_ref[0], own_ref[0]
    pairs = (
        (cross_ref, cross),
        (pull_wide_ref, pull_wide),
        (pull_narrow_ref, pull_narrow),
        (inv_ref, inv),
        (wide_ref, wide),
        (narrow_ref, narrow),
    )
    loads = [begin(source, target, sems.at[i]) for i, (source, target) in enumerate(pairs)]
    scores = shares_ref[...].reshape(8, 4, 2, 128).sum(axis=1)
    video = lax.broadcasted_iota(jnp.int32, scores.shape, 0) + 8 * lax.broadcasted_iota(
        jnp.int32, scores.shape, 1
    )
    lane = lax.broadcasted_iota(jnp.int32, (1, 128), 1)
    exps = jnp.exp(scores)
    own_exp = jnp.sum(jnp.sum(jnp.where(video == own, exps, 0.0), axis=0), axis=0, keepdims=True)
    own_exp = jnp.where(lane < VIDEOS, own_exp, 0.0)
    column = jnp.sum(jnp.sum(exps, axis=0), axis=0, keepdims=True)
    row_soft = own_exp / jnp.sum(own_exp, axis=1, keepdims=True)
    col_soft = own_exp / column
    teacher = jnp.exp(teacher_ref[...].astype(F32) / teacher_softness)
    teacher = jnp.concatenate([teacher, jnp.zeros((1, 128 - VIDEOS), F32)], axis=1)
    teacher_soft = teacher / jnp.sum(teacher, axis=1, keepdims=True)
    one_hot = (lane == own).astype(F32)
    score_grad = (row_soft - one_hot + (col_soft - one_hot)) / (2.0 * VIDEOS) + (
        row_soft - teacher_soft
    ) / VIDEOS
    score_out[...] = score_grad[:, :VIDEOS]
    columns = lax.broadcasted_iota(jnp.int32, (VIDEOS, 128), 1)
    pull = jnp.sum(
        jnp.where(columns == video_of(core), score_grad, 0.0), axis=1, keepdims=True
    )
    rows[TOKENS:] = jnp.broadcast_to(pull, (VIDEOS, 128))
    column = lax.broadcasted_iota(jnp.int32, (VIDEOS, VIDEOS), 1)
    row = lax.broadcasted_iota(jnp.int32, (VIDEOS, VIDEOS), 0)
    pull_row = jnp.sum(jnp.where(row == column, pull, 0.0), axis=0, keepdims=True)
    for load in loads:
        load.wait()
    along = jnp.sum(cross[:, :VIDEOS] * pull_row, axis=1, keepdims=True)
    rows[:TOKENS] = jnp.broadcast_to(along, (TOKENS, 128))
    copy = begin(rows, rows_out, sems.at[6])
    base_wide = jnp.sum(pull * pull_wide[...], axis=0, keepdims=True)
    base_narrow = jnp.sum(pull * pull_narrow[...], axis=0, keepdims=True)
    scale = inv[:, :1]
    out_wide = scale * (base_wide - along * wide[...].astype(F32))
    out_narrow = scale * (base_narrow - along * narrow[...].astype(F32))
    parts = []
    for x in range(4):
        parts += [out_wide[:, MAIN * x : MAIN * (x + 1)], out_narrow[:, REST * x : REST * (x + 1)]]
    result[...] = jnp.concatenate(parts, axis=1).astype(BF16)
    send = begin(result, time_out, sems.at[7])
    copy.wait()
    send.wait()


def shaped(shape, dtype):
    return jax.ShapeDtypeStruct(shape, dtype)


def shards(time_qkv, space_qkv, residual, space_proj, time_proj, norm_gain, text_emb, teacher):
    core = lax.axis_index("c")
    own_video = lax.axis_index(VID)
    big = pltpu.VMEM
    pack = call(
        pack_kernel,
        shaped((16, 32, 128), BF16),
        (lax.axis_index(SEQ)[None], space_proj, time_proj, text_emb),
        10**5,
        10**6,
        "shhh",
        "v",
        [big(space_proj.shape, BF16), big(time_proj.shape, BF16), big((1, WIDTH + 128), F32)],
        3,
    )
    ring = lax.all_to_all(pack, RING, 0, 0)

    space_copies, time_piece = call(
        assemble_kernel,
        (shaped((16, LABELLED, 128), BF16), shaped((PACKED, 128), BF16)),
        (ring,),
        2 * 10**7,
        2 * 10**6,
        "v",
        "hh",
        [big((2, LABELLED, 128), BF16)],
        17,
    )
    w_time = lax.all_gather(time_piece, ("x", "y", "c")).reshape(16, 2, PACKED, 128)
    w_own = lax.all_to_all(space_copies, ("x", "y"), 0, 0)

    space = space_qkv.reshape(3, TOKENS, ATT).swapaxes(1, 2)
    space_weights, att_wide, att_narrow = call(
        space_forward_kernel,
        (
            shaped((HEADS, TOKENS, TOKENS), BF16),
            shaped((TOKENS, 4 * MAIN), BF16),
            shaped((TOKENS, 4 * REST), BF16),
        ),
        (space,),
        6 * 10**8,
        3 * 10**6,
        "v",
        "mmm",
        [big((4 * REST, TOKENS), F32)],
    )
    res, gain = call(
        split_kernel,
        (shaped((2, TOKENS, HALF), BF16), shaped((2, 1, HALF), F32)),
        (core[None], residual.reshape(TOKENS, WIDTH), norm_gain[None]),
        10**8,
        2 * 10**6,
        "svv",
        "mm",
    )
    time = time_qkv.reshape(3, TOKENS, ATT)
    time_weights = call(
        time_forward_kernel,
        shaped((HEADS, TOKENS, TOKENS), BF16),
        (time,),
        6 * 10**8,
        3 * 10**6,
        "v",
        "m",
    )
    w_own, time_weights, res, gain, att_wide, att_narrow = lax.optimization_barrier(
        (w_own, time_weights, res, gain, att_wide, att_narrow)
    )
    w_other = swap(w_own, "c")
    mixed_own = call(
        embed_own_kernel,
        shaped((TOKENS, HALF), F32),
        (att_wide, att_narrow, res, w_own),
        5 * 10**8,
        3 * 10**6,
        "mmmv",
        "m",
        [big((HALF, 4 * MAIN), BF16), big((HALF, 4 * REST), BF16)],
    )
    w_other, mixed_own = lax.optimization_barrier((w_other, mixed_own))
    normed, inv, unit, norm, text, row = call(
        embed_kernel,
        (
            shaped((2, TOKENS, HALF), BF16),
            shaped((TOKENS, 128), F32),
            shaped((2, 1, HALF), F32),
            shaped((1, 1), F32),
            shaped((2, 16, 8, 128), F32),
            shaped((VIDEOS, 1, 128), F32),
        ),
        (core[None], att_wide, att_narrow, res, mixed_own, w_own, w_other, gain),
        10**9,
        6 * 10**6,
        "smmmmvvm",
        "hhvvhv",
        [
            big((HALF, 4 * MAIN), BF16),
            big((HALF, 4 * REST), BF16),
            big((2, TOKENS, HALF), BF16),
            big((TOKENS, 128), F32),
            big((2, 16, 8, 128), F32),
        ],
        4,
    )
    ring_rows = lax.all_to_all(row, RING, 0, 0)
    token, cross = call(
        basis_kernel,
        (shaped((2, VIDEOS, HALF), F32), shaped((TOKENS, 128), F32)),
        (core[None], normed, unit, norm, gain, text),
        10**8,
        2 * 10**6,
        "shvvmh",
        "vh",
        [big((2, TOKENS, HALF), BF16), big((TOKENS, 128), F32), big((2, 16, 8, 128), F32)],
        3,
    )
    ring_rows, token, cross = lax.optimization_barrier((ring_rows, token, cross))
    shares = spread(ring_rows.reshape(2, 8, 128).sum(axis=1), ("y", "c", "x"))
    wide, narrow, pull_wide, pull_narrow = call(
        project_kernel,
        (
            shaped((TOKENS, 4 * MAIN), BF16),
            shaped((TOKENS, 4 * REST), BF16),
            shaped((VIDEOS, 4 * MAIN), F32),
            shaped((VIDEOS, 4 * REST), F32),
        ),
        (core[None], w_time, normed, token),
        5 * 10**8,
        5 * 10**6,
        "shhv",
        "hhhh",
        [
            big((2, 16, PACKED, 128), BF16),
            big((2, TOKENS, HALF), BF16),
            big((HALF, 4 * MAIN), BF16),
            big((HALF, 4 * REST), BF16),
            big((TOKENS, 4 * MAIN), BF16),
            big((TOKENS, 4 * REST), BF16),
            big((VIDEOS, 4 * MAIN), F32),
            big((VIDEOS, 4 * REST), F32),
        ],
        7,
    )
    shares, wide, narrow, pull_wide, pull_narrow = lax.optimization_barrier(
        (shares, wide, narrow, pull_wide, pull_narrow)
    )
    score_grad, pulls, time_grad = call(
        score_kernel,
        (
            shaped((1, VIDEOS), F32),
            shaped((TOKENS + VIDEOS, 128), F32),
            shaped((TOKENS, ATT), BF16),
        ),
        (
            core[None],
            own_video[None],
            shares,
            teacher,
            inv,
            cross,
            wide,
            narrow,
            pull_wide,
            pull_narrow,
        ),
        10**7,
        10**6,
        "ssvvhhhhhh",
        "vhh",
        [
            big((TOKENS, 128), F32),
            big((TOKENS, 128), F32),
            big((TOKENS, 4 * MAIN), BF16),
            big((TOKENS, 4 * REST), BF16),
            big((VIDEOS, 4 * MAIN), F32),
            big((VIDEOS, 4 * REST), F32),
            big((TOKENS + VIDEOS, 128), F32),
            big((TOKENS, ATT), BF16),
        ],
        8,
    )
    moved = lax.all_to_all(time_grad.reshape(FRAMES, 8, ATT), SEQ, 0, 0).reshape(TOKENS, ATT)
    space_grad = call(
        space_back_kernel,
        shaped((3, ATT, TOKENS), BF16),
        (normed, inv, pulls, token, w_own, w_other, space, space_weights),
        2 * 10**9,
        8 * 10**6,
        "vvvvvvvm",
        "v",
        [big((HALF, 4 * MAIN), BF16), big((HALF, 4 * REST), BF16)],
    )
    moved, space_grad = lax.optimization_barrier((moved, space_grad))
    time_out = call(
        time_back_kernel,
        shaped((3, TOKENS, ATT), BF16),
        (moved, time, time_weights),
        10**9,
        5 * 10**6,
        "vvm",
        "h",
        [big((HEADS, TOKENS, TOKENS), BF16), big((3, TOKENS, ATT), BF16)],
        3,
    )
    return (
        space_grad.swapaxes(1, 2).reshape(3, 1, 1, TOKENS, ATT),
        time_out.reshape(3, 1, FRAMES, 8, ATT),
        score_grad,
    )


def solution(mesh):
    fine = Mesh(mesh.devices.reshape(2, 4, 2, 4, 8), ("zh", "y", "c", "x", "zl"))
    in_specs = (
        P(None, VID, None, SEQ, None),
        P(None, VID, SEQ, None, None),
        P(VID, SEQ, None, None),
        P(SEQ, VID),
        P(SEQ, VID),
        P(),
        P(VID, None),
        P(VID, None),
    )
    out_specs = (
        P(None, VID, SEQ, None, None),
        P(None, VID, None, SEQ, None),
        P(VID, None),
    )
    return jax.shard_map(shards, mesh=fine, in_specs=in_specs, out_specs=out_specs, check_vma=False)
```

```python
import math

import jax
import jax.numpy as jnp
from jax import lax
from jax.experimental import pallas as pl
from jax.experimental.pallas import tpu as pltpu
from jax.sharding import Mesh
from jax.sharding import PartitionSpec as P

HEAD_DIM = 88
HEADS = 8
ATT = 704
WIDTH = 1408
HALF = 704
TOKENS = 256
VIDEOS = 16
FRAMES = 32
PAIR = 2 * HEAD_DIM
WINDOW = 96
BACK = PAIR - WINDOW
VID = ("zh", "y", "c")
SEQ = ("x", "zl")
RING = ("zh", "zl")
SIZES = {"zh": 2, "y": 4, "c": 2, "x": 4, "zl": 8}

logit_scale = 20.0
teacher_softness = 4.0
F32 = jnp.float32
BF16 = jnp.bfloat16
ROOT = 1.0 / math.sqrt(HEAD_DIM)
VMEM = pl.BlockSpec(memory_space=pltpu.VMEM)
SMEM = pl.BlockSpec(memory_space=pltpu.SMEM)
HBM = pl.BlockSpec(memory_space=pltpu.HBM)
MAIN = 128
REST = PAIR - MAIN
FOLD = 96
PACKED = PAIR + FOLD
LABELLED = PACKED + 16


def dot(a, b, contract):
    return lax.dot_general(a, b, (contract, ((), ())), preferred_element_type=F32)


NN = ((1,), (0,))
NT = ((1,), (1,))
TN = ((0,), (0,))


def call(kernel, out_shape, args, flops, moved, ins="", outs="", scratch=(), copies=0):
    places = {"s": SMEM, "v": VMEM, "m": VMEM, "h": HBM}
    pinned = {"m": pltpu.VMEM, "h": pltpu.HBM}
    sems = [pltpu.SemaphoreType.DMA((copies,))] if copies else []
    single = not isinstance(out_shape, tuple)
    shapes = [
        pinned[p](o.shape, o.dtype) if p in pinned else o
        for o, p in zip((out_shape,) if single else out_shape, outs)
    ]
    specs = [places[p] for p in outs]
    args = [
        pltpu.with_memory_space_constraint(a, pinned[p]) if p in pinned else a
        for a, p in zip(args, ins)
    ]
    return pl.pallas_call(
        kernel,
        out_shape=shapes[0] if single else tuple(shapes),
        in_specs=[places[p] for p in ins],
        out_specs=specs[0] if single else tuple(specs),
        scratch_shapes=list(scratch) + sems,
        compiler_params=pltpu.CompilerParams(vmem_limit_bytes=20 * 2**20),
        cost_estimate=pl.CostEstimate(flops=flops, bytes_accessed=moved, transcendentals=0),
    )(*args)


def begin(source, target, sem):
    copy = pltpu.make_async_copy(source, target, sem)
    copy.start()
    return copy


def spread(block, axes):
    count = math.prod(SIZES[axis] for axis in axes)
    return lax.all_to_all(jnp.broadcast_to(block[None], (count,) + block.shape), axes, 0, 0)


def swap(block, axis):
    return lax.ppermute(block, axis, [(0, 1), (1, 0)])


def halves(rows):
    parts = []
    for c in range(2):
        blocks = [(zh * 4 + y) * 2 + c for y in range(4) for zh in range(2)]
        parts.append(
            jnp.concatenate([rows[:, b * HEAD_DIM : (b + 1) * HEAD_DIM] for b in blocks], axis=1)
        )
    return parts


def split_kernel(core_ref, res_ref, gain_ref, res_out, gain_out):
    core = core_ref[0]
    for ref, out in ((res_ref, res_out), (gain_ref, gain_out)):
        parts = halves(ref[...])
        for c in range(2):
            out[core ^ c] = parts[c]


ROWS = 22
LATE = 10
SIDE = 128 - HEAD_DIM
TEXT = 44
TEXT_ROW = 27


def pack_kernel(place_ref, space_hbm, time_hbm, text_hbm, out, space_ref, time_ref, text_ref, sems):
    piece = place_ref[0]
    loads = [
        begin(space_hbm, space_ref, sems.at[0]),
        begin(time_hbm, time_ref, sems.at[1]),
        begin(text_hbm, text_ref.at[:, pl.ds(0, WIDTH)], sems.at[2]),
    ]
    for load in loads:
        load.wait()
    time = time_ref[...].astype(F32)
    late = time[LATE:]
    side = [late[:, :SIDE], late[:, SIDE : 2 * SIDE]]
    ends = [late[i : i + 1, 2 * SIDE :] for i in range(ROWS - LATE)]
    ends += [jnp.zeros((1, HEAD_DIM - 2 * SIDE), F32)] * 3
    side += [jnp.concatenate(ends[5 * i : 5 * i + 5], axis=1) for i in range(3)]
    start = piece * TEXT
    near = pl.multiple_of(start // 128 * 128, 128)
    window = jnp.broadcast_to(text_ref[:, pl.ds(near, 256)], (8, 256))
    text = pltpu.roll(window, (256 - (start - near)) & 255, 1)[:1, :TEXT]
    high = text.astype(BF16).astype(F32)
    for term in (high, text - high):
        blank = jnp.zeros((1, 2 * SIDE - TEXT), F32)
        side += [term[:, :SIDE], jnp.concatenate([term[:, SIDE:], blank], axis=1)]
    side.append(jnp.zeros((1, SIDE), F32))
    main = jnp.concatenate([space_ref[...].astype(F32), time[:LATE]])
    rows = jnp.concatenate([main, jnp.concatenate(side)], axis=1).astype(BF16)
    for i in range(16):
        out[i] = rows


def assemble_kernel(ring_ref, space_out, time_out, pieces, sems):
    rows = []
    for term in range(2):
        for zh in range(2):
            blocks = ring_ref[8 * zh : 8 * zh + 8].astype(F32)
            first = TEXT_ROW + 2 * term
            parts = jnp.concatenate(
                [blocks[:, first, HEAD_DIM:], blocks[:, first + 1, HEAD_DIM : HEAD_DIM + TEXT - SIDE]],
                axis=1,
            )
            for q in range(4):
                both = [parts[2 * q : 2 * q + 1], parts[2 * q + 1 : 2 * q + 2]]
                rows.append(jnp.concatenate(both, axis=1))
    rows = jnp.concatenate([jnp.concatenate(rows), jnp.zeros((16, SIDE), F32)], axis=1)
    pieces[0, PACKED:] = rows.astype(BF16)

    line = lax.broadcasted_iota(jnp.int32, (256, 1), 0) & 31
    ahead = lax.broadcasted_iota(jnp.int32, (256, PAIR), 1) - ROWS * (
        lax.broadcasted_iota(jnp.int32, (256, PAIR), 0) >> 5
    )

    def pick(first, count, target, step=1):
        there = (line >= first) & (line < first + count)
        column = jnp.where(there, (line - first) * step + target, -1000)
        return (ahead == column).astype(F32).astype(BF16)

    picks = [pick(0, ROWS, 0), pick(ROWS, LATE, 0)]
    picks += [pick(0, ROWS - LATE, LATE), pick(ROWS - LATE, ROWS - LATE, LATE)]
    picks += [pick(24, 3 if n < 2 else 2, LATE + n, 5) for n in range(5)]
    copies = []
    ring = [ring_ref[8 * zh : 8 * zh + 8].reshape(256, 128) for zh in range(2)]
    for slot in range(2):
        both = []
        for zh in range(2):
            if slot == 0:
                both.append(dot(ring[zh], picks[0], TN)[:HEAD_DIM])
                continue
            main = dot(ring[zh], picks[1], TN)[:HEAD_DIM]
            side = [dot(ring[zh], p, TN)[HEAD_DIM:] for p in picks[2:4]]
            width = HEAD_DIM - 2 * SIDE
            last = sum(
                dot(ring[zh], p, TN)[HEAD_DIM + width * n : HEAD_DIM + width * (n + 1)]
                for n, p in enumerate(picks[4:])
            )
            both.append(main + jnp.concatenate(side + [last]))
        whole = jnp.concatenate(both)
        rest = whole[:, MAIN:]
        low = jnp.concatenate([rest[FOLD:], jnp.zeros((2 * FOLD - PAIR, REST), F32)])
        fold = jnp.concatenate([rest[:FOLD], low, jnp.zeros((FOLD, 128 - 2 * REST), F32)], axis=1)
        pieces[slot, :PAIR] = whole[:, :MAIN].astype(BF16)
        pieces[slot, PAIR:PACKED] = fold.astype(BF16)
        if slot == 0:
            for i in range(16):
                copies.append(begin(pieces.at[0], space_out.at[i], sems.at[i]))
        else:
            copies.append(begin(pieces.at[1, pl.ds(0, PACKED)], time_out, sems.at[16]))
    for copy in copies:
        copy.wait()


def unfold(packed, wide, narrow):
    for y in range(4):
        rows = slice(PAIR * y, PAIR * (y + 1))
        rest = []
        for x in range(4):
            wide[rows, MAIN * x : MAIN * (x + 1)] = packed[4 * x + y, :PAIR]
            fold = packed[4 * x + y, PAIR:PACKED]
            rest.append(jnp.concatenate([fold[:, :REST], fold[: PAIR - FOLD, REST : 2 * REST]]))
        narrow[rows] = jnp.concatenate(rest, axis=1)


def head_rows(head):
    start = (head // 2) * PAIR + (head % 2) * BACK
    return slice(start, start + WINDOW)


def head_valid(head):
    row = lax.broadcasted_iota(jnp.int32, (WINDOW, 1), 0)
    return row < HEAD_DIM if head % 2 == 0 else row >= WINDOW - HEAD_DIM


def own_rows(block, head):
    return block[:HEAD_DIM] if head % 2 == 0 else block[WINDOW - HEAD_DIM :]


def keep(valid, block):
    return jnp.where(valid, block, jnp.zeros_like(block))


def softmax_down(scores):
    peak = jnp.max(scores, axis=0, keepdims=True)
    weights = jnp.exp(scores - peak)
    return (weights * (1.0 / jnp.sum(weights, axis=0, keepdims=True))).astype(BF16)


def slopes_down(weights, dots):
    weights = weights.astype(F32)
    delta = jnp.sum(weights * dots, axis=0, keepdims=True)
    return (weights * (dots - delta) * ROOT).astype(BF16)


def space_forward_kernel(qkv_ref, weights_out, wide_out, narrow_out, down):
    pair = []
    for head in range(HEADS):
        rows, valid = head_rows(head), head_valid(head)
        scores = dot(qkv_ref[1, rows], keep(valid, qkv_ref[0, rows]), TN) * ROOT
        weights = softmax_down(scores)
        weights_out[head] = weights
        pair.append(own_rows(dot(qkv_ref[2, rows], weights, NN), head))
        if head % 2:
            x = head // 2
            both = jnp.concatenate(pair)
            wide_out[:, MAIN * x : MAIN * (x + 1)] = both[:MAIN].T.astype(BF16)
            down[REST * x : REST * (x + 1)] = both[MAIN:]
            pair = []
    narrow_out[...] = down[...].T.astype(BF16)


def space_back_kernel(
    normed_ref, inv_ref, pulls_ref, token_ref, own_ref, other_ref, qkv_ref, weights_ref, out, wide, narrow
):
    grads = []
    for half, w_ref in enumerate((own_ref, other_ref)):
        unfold(w_ref, wide, narrow)
        token = jnp.sum(pulls_ref[TOKENS:, :1] * token_ref[half], axis=0, keepdims=True)
        mixed = inv_ref[:, :1] * (token - normed_ref[half].astype(F32) * pulls_ref[:TOKENS, :1])
        mixed = mixed.astype(BF16)
        grads.append((dot(mixed, wide[...], NN), dot(mixed, narrow[...], NN)))
    main = (grads[0][0] + grads[1][0]).T.astype(BF16)
    rest = (grads[0][1] + grads[1][1]).T.astype(BF16)
    for x in range(4):
        grad = jnp.concatenate([main[MAIN * x : MAIN * (x + 1)], rest[REST * x : REST * (x + 1)]])
        pairs = [[], [], []]
        for head in (2 * x, 2 * x + 1):
            rows, valid = head_rows(head), head_valid(head)
            grad_rows = grad[:WINDOW] if head % 2 == 0 else grad[BACK:]
            dots = dot(qkv_ref[2, rows], keep(valid, grad_rows), TN)
            weights = weights_ref[head]
            slopes = slopes_down(weights, dots)
            pairs[0].append(own_rows(dot(qkv_ref[1, rows], slopes, NN), head))
            pairs[1].append(own_rows(dot(qkv_ref[0, rows], slopes, NT), head))
            pairs[2].append(own_rows(dot(grad_rows, weights, NT), head))
        for slot in range(3):
            out[slot, x * PAIR : (x + 1) * PAIR] = jnp.concatenate(pairs[slot]).astype(BF16)


def head_lanes(head):
    start = (head * HEAD_DIM) // 128 * 128
    width = min(256, ATT - start)
    lane = lax.broadcasted_iota(jnp.int32, (1, width), 1) + (start - head * HEAD_DIM)
    return slice(start, start + width), (lane >= 0) & (lane < HEAD_DIM)


def time_forward_kernel(qkv_ref, weights_out):
    key = lax.broadcasted_iota(jnp.int32, (TOKENS, TOKENS), 0)
    query = lax.broadcasted_iota(jnp.int32, (TOKENS, TOKENS), 1)
    same = ((key ^ query) & 7) == 0
    for head in range(HEADS):
        lanes, valid = head_lanes(head)
        scores = dot(qkv_ref[1, :, lanes], keep(valid, qkv_ref[0, :, lanes]), NT) * ROOT
        weights_out[head] = softmax_down(jnp.where(same, scores, -1e30))


def time_back_kernel(grad_ref, qkv_ref, weights_ref, out, slopes, result, sems):
    copies = []

    def put(slot, head, part):
        lanes, valid = head_lanes(head)
        result[slot, :, lanes] = jnp.where(valid, part.astype(BF16), result[slot, :, lanes])

    for head in range(HEADS):
        lanes, valid = head_lanes(head)
        grad = grad_ref[:, lanes]
        dots = dot(qkv_ref[2, :, lanes], keep(valid, grad), NT)
        slopes[head] = slopes_down(weights_ref[head], dots)
        put(2, head, dot(weights_ref[head], grad, NN))
    copies.append(begin(result.at[2], out.at[2], sems.at[2]))
    for slot, contract in ((1, NN), (0, TN)):
        for head in range(HEADS):
            put(slot, head, dot(slopes[head], qkv_ref[1 - slot, :, head_lanes(head)[0]], contract))
        copies.append(begin(result.at[slot], out.at[slot], sems.at[slot]))
    for copy in copies:
        copy.wait()


def labels_of(y, core, half):
    row = lax.broadcasted_iota(jnp.int32, (8, 1), 0)
    return (row // 4 * 4 + y) * 2 + (core ^ half)


def embed_own_kernel(wide_ref, narrow_ref, res_ref, own_ref, out, w_wide, w_narrow):
    unfold(own_ref, w_wide, w_narrow)
    out[...] = (
        res_ref[0].astype(F32)
        + dot(wide_ref[...], w_wide[...], NT)
        + dot(narrow_ref[...], w_narrow[...], NT)
    )


def embed_kernel(
    place_ref,
    wide_ref,
    narrow_ref,
    res_ref,
    mixed_ref,
    own_ref,
    other_ref,
    gain_ref,
    normed_out,
    inv_out,
    unit_out,
    norm_out,
    text_out,
    row_out,
    w_wide,
    w_narrow,
    normed,
    inv_kept,
    texts,
    sems,
):
    core = place_ref[0]
    unfold(other_ref, w_wide, w_narrow)
    for half, ref in enumerate((own_ref, other_ref)):
        for y in range(4):
            tiles, square = [], 0.0
            for x in range(4):
                terms = ref[4 * x + y, PACKED:].astype(F32)
                tiles.append(terms[:8] + terms[8:])
                square += jnp.sum(tiles[x] * tiles[x], axis=1, keepdims=True)
            upper = lax.broadcasted_iota(jnp.int32, (8, 1), 0) < 4
            first = jnp.sum(jnp.where(upper, square, 0.0), axis=0, keepdims=True)
            second = jnp.sum(jnp.where(upper, 0.0, square), axis=0, keepdims=True)
            size = jnp.sqrt(jnp.where(upper, first, second) + 1e-06)
            for x in range(4):
                texts[half, 4 * x + y] = tiles[x] / size
    copies = [begin(texts, text_out, sems.at[3])]
    sums = [mixed_ref[...]]
    sums.append(
        res_ref[1].astype(F32)
        + dot(wide_ref[...], w_wide[...], NT)
        + dot(narrow_ref[...], w_narrow[...], NT)
    )
    mean = sum(jnp.sum(s, axis=1, keepdims=True) for s in sums) / WIDTH
    sums = [s - mean for s in sums]
    square = sum(jnp.sum(s * s, axis=1, keepdims=True) for s in sums) / WIDTH
    inv = 1.0 / jnp.sqrt(square + 1e-05)
    inv_kept[...] = jnp.broadcast_to(inv, (TOKENS, 128))
    copies.append(begin(inv_kept, inv_out, sems.at[0]))
    embs = []
    for half in range(2):
        part = sums[half] * inv
        normed[half] = part.astype(BF16)
        copies.append(begin(normed.at[half], normed_out.at[half], sems.at[1 + half]))
        embs.append(jnp.sum(part, axis=0, keepdims=True) * gain_ref[half] / TOKENS)
    norm = jnp.sqrt(sum(jnp.sum(e * e, axis=1, keepdims=True) for e in embs) + 1e-06)
    norm_out[...] = norm
    units = [e / norm for e in embs]
    for half in range(2):
        unit_out[half] = units[half]
    by_core = [jnp.where(core == c, units[0], units[1]) for c in range(2)]
    blank = jnp.zeros((8, 128 - HEAD_DIM), F32)
    blocks = []
    for x in range(4):
        four = []
        for q in range(4):
            start = ((x % 2 * 2 + q // 2) * 2 + x // 2) * HEAD_DIM
            four.append(by_core[q % 2][:, start : start + HEAD_DIM])
        blocks.append(jnp.concatenate([jnp.concatenate(four + four), blank], axis=1))
    lane = lax.broadcasted_iota(jnp.int32, (8, 128), 1)
    row = jnp.zeros((1, 128), F32)
    for half in range(2):
        for y in range(4):
            products = sum(texts[half, 4 * x + y] * blocks[x] for x in range(4))
            cosines = jnp.sum(products, axis=1, keepdims=True)
            here = lane == labels_of(y, core, half)
            row += jnp.sum(jnp.where(here, cosines, 0.0), axis=0, keepdims=True)
    row = row * (logit_scale / FRAMES)
    for i in range(VIDEOS):
        row_out[i] = row
    for copy in copies:
        copy.wait()


def video_of(core):
    row = lax.broadcasted_iota(jnp.int32, (VIDEOS, 1), 0)
    return ((row & 1) * 4 + ((row >> 1) & 3)) * 2 + (core ^ (row >> 3))


def basis_kernel(place_ref, normed_ref, unit_ref, norm_ref, gain_ref, text_hbm, token_out, cross_out, normed, cross, text_ref, sems):
    core = place_ref[0]
    load_text = begin(text_hbm, text_ref, sems.at[2])
    load = begin(normed_ref, normed, sems.at[0])
    load_text.wait()
    by_core = []
    for c in range(2):
        parts = []
        for y in range(4):
            for zh in range(2):
                x, q = 2 * zh + y // 2, y % 2 * 2 + c
                rows = []
                for half in range(2):
                    for at in range(4):
                        tile = text_ref[half, 4 * x + at]
                        rows += [tile[q : q + 1, :HEAD_DIM], tile[4 + q : 5 + q, :HEAD_DIM]]
                parts.append(jnp.concatenate(rows))
        by_core.append(jnp.concatenate(parts, axis=1))
    texts = [
        jnp.where(core == 0, by_core[0], by_core[1]),
        jnp.where(core == 0, by_core[1], by_core[0]),
    ]
    along = sum(jnp.sum(texts[h] * unit_ref[h], axis=1, keepdims=True) for h in range(2))
    scale = VIDEOS * logit_scale / norm_ref[...]
    token = [(texts[h] - unit_ref[h] * along) * scale * gain_ref[h] for h in range(2)]
    mean = sum(jnp.sum(t, axis=1, keepdims=True) for t in token) / WIDTH
    load.wait()
    columns = sum(dot(normed[h], token[h].astype(BF16), NT) for h in range(2)) * (1.0 / WIDTH)
    cross[...] = jnp.concatenate([columns, jnp.zeros((TOKENS, 128 - VIDEOS), F32)], axis=1)
    copy = begin(cross, cross_out, sems.at[1])
    for half in range(2):
        token_out[half] = token[half] - mean
    copy.wait()


def project_kernel(
    place_ref,
    w_ref,
    normed_ref,
    token_ref,
    wide_out,
    narrow_out,
    pull_wide_out,
    pull_narrow_out,
    w,
    normed,
    w_wide,
    w_narrow,
    wide,
    narrow,
    pull_wide,
    pull_narrow,
    sems,
):
    core = place_ref[0]
    loads = [begin(w_ref.at[:, core ^ half], w.at[half], sems.at[half]) for half in range(2)]
    load_normed = begin(normed_ref, normed, sems.at[2])
    sums = [0.0] * 4
    for half in range(2):
        token = token_ref[half]
        high = token.astype(BF16)
        terms = jnp.concatenate([high.astype(F32), token - high.astype(F32)]).astype(BF16)
        loads[half].wait()
        unfold(w.at[half], w_wide, w_narrow)
        if half == 0:
            load_normed.wait()
        for i, part in enumerate((w_wide, w_narrow)):
            sums[i] += dot(normed[half], part[...], NN)
            sums[2 + i] += dot(terms, part[...], NN)
    wide[...] = sums[0].astype(BF16)
    narrow[...] = sums[1].astype(BF16)
    copies = [begin(wide, wide_out, sems.at[3]), begin(narrow, narrow_out, sems.at[4])]
    pull_wide[...] = sums[2][:VIDEOS] + sums[2][VIDEOS:]
    pull_narrow[...] = sums[3][:VIDEOS] + sums[3][VIDEOS:]
    copies.append(begin(pull_wide, pull_wide_out, sems.at[5]))
    copies.append(begin(pull_narrow, pull_narrow_out, sems.at[6]))
    for copy in copies:
        copy.wait()


def score_kernel(
    core_ref,
    own_ref,
    shares_ref,
    teacher_ref,
    inv_ref,
    cross_ref,
    wide_ref,
    narrow_ref,
    pull_wide_ref,
    pull_narrow_ref,
    score_out,
    rows_out,
    time_out,
    inv,
    cross,
    wide,
    narrow,
    pull_wide,
    pull_narrow,
    rows,
    result,
    sems,
):
    core, own = core_ref[0], own_ref[0]
    pairs = (
        (cross_ref, cross),
        (pull_wide_ref, pull_wide),
        (pull_narrow_ref, pull_narrow),
        (inv_ref, inv),
        (wide_ref, wide),
        (narrow_ref, narrow),
    )
    loads = [begin(source, target, sems.at[i]) for i, (source, target) in enumerate(pairs)]
    scores = shares_ref[...].reshape(8, 4, 2, 128).sum(axis=1)
    video = lax.broadcasted_iota(jnp.int32, scores.shape, 0) + 8 * lax.broadcasted_iota(
        jnp.int32, scores.shape, 1
    )
    lane = lax.broadcasted_iota(jnp.int32, (1, 128), 1)
    exps = jnp.exp(scores)
    own_exp = jnp.sum(jnp.sum(jnp.where(video == own, exps, 0.0), axis=0), axis=0, keepdims=True)
    own_exp = jnp.where(lane < VIDEOS, own_exp, 0.0)
    column = jnp.sum(jnp.sum(exps, axis=0), axis=0, keepdims=True)
    row_soft = own_exp / jnp.sum(own_exp, axis=1, keepdims=True)
    col_soft = own_exp / column
    teacher = jnp.exp(teacher_ref[...].astype(F32) / teacher_softness)
    teacher = jnp.concatenate([teacher, jnp.zeros((1, 128 - VIDEOS), F32)], axis=1)
    teacher_soft = teacher / jnp.sum(teacher, axis=1, keepdims=True)
    one_hot = (lane == own).astype(F32)
    score_grad = (row_soft - one_hot + (col_soft - one_hot)) / (2.0 * VIDEOS) + (
        row_soft - teacher_soft
    ) / VIDEOS
    score_out[...] = score_grad[:, :VIDEOS]
    columns = lax.broadcasted_iota(jnp.int32, (VIDEOS, 128), 1)
    pull = jnp.sum(
        jnp.where(columns == video_of(core), score_grad, 0.0), axis=1, keepdims=True
    )
    rows[TOKENS:] = jnp.broadcast_to(pull, (VIDEOS, 128))
    column = lax.broadcasted_iota(jnp.int32, (VIDEOS, VIDEOS), 1)
    row = lax.broadcasted_iota(jnp.int32, (VIDEOS, VIDEOS), 0)
    pull_row = jnp.sum(jnp.where(row == column, pull, 0.0), axis=0, keepdims=True)
    for load in loads:
        load.wait()
    along = jnp.sum(cross[:, :VIDEOS] * pull_row, axis=1, keepdims=True)
    base_wide = jnp.sum(pull * pull_wide[...], axis=0, keepdims=True)
    base_narrow = jnp.sum(pull * pull_narrow[...], axis=0, keepdims=True)
    sends = []
    for i in range(2):
        part = slice(i * TOKENS // 2, (i + 1) * TOKENS // 2)
        scale = inv[part, :1]
        out_wide = scale * (base_wide - along[part] * wide[part].astype(F32))
        out_narrow = scale * (base_narrow - along[part] * narrow[part].astype(F32))
        parts = []
        for x in range(4):
            parts.append(out_wide[:, MAIN * x : MAIN * (x + 1)])
            parts.append(out_narrow[:, REST * x : REST * (x + 1)])
        result[part] = jnp.concatenate(parts, axis=1).astype(BF16)
        span = pl.ds(i * TOKENS // 2, TOKENS // 2)
        sends.append(begin(result.at[span], time_out.at[span], sems.at[7 + i]))
    rows[:TOKENS] = jnp.broadcast_to(along, (TOKENS, 128))
    sends.append(begin(rows, rows_out, sems.at[6]))
    for send in sends:
        send.wait()


def shaped(shape, dtype):
    return jax.ShapeDtypeStruct(shape, dtype)


def shards(time_qkv, space_qkv, residual, space_proj, time_proj, norm_gain, text_emb, teacher):
    core = lax.axis_index("c")
    own_video = lax.axis_index(VID)
    big = pltpu.VMEM
    pack = call(
        pack_kernel,
        shaped((16, 32, 128), BF16),
        (lax.axis_index(SEQ)[None], space_proj, time_proj, text_emb),
        10**5,
        10**6,
        "shhh",
        "v",
        [big(space_proj.shape, BF16), big(time_proj.shape, BF16), big((1, WIDTH + 128), F32)],
        3,
    )
    ring = lax.all_to_all(pack, RING, 0, 0)

    space_copies, time_piece = call(
        assemble_kernel,
        (shaped((16, LABELLED, 128), BF16), shaped((PACKED, 128), BF16)),
        (ring,),
        2 * 10**7,
        2 * 10**6,
        "v",
        "hh",
        [big((2, LABELLED, 128), BF16)],
        17,
    )
    w_time = lax.all_gather(time_piece, ("x", "y", "c")).reshape(16, 2, PACKED, 128)
    w_own = lax.all_to_all(space_copies, ("x", "y"), 0, 0)

    space = space_qkv.reshape(3, TOKENS, ATT).swapaxes(1, 2)
    space_weights, att_wide, att_narrow = call(
        space_forward_kernel,
        (
            shaped((HEADS, TOKENS, TOKENS), BF16),
            shaped((TOKENS, 4 * MAIN), BF16),
            shaped((TOKENS, 4 * REST), BF16),
        ),
        (space,),
        6 * 10**8,
        3 * 10**6,
        "v",
        "mmm",
        [big((4 * REST, TOKENS), F32)],
    )
    res, gain = call(
        split_kernel,
        (shaped((2, TOKENS, HALF), BF16), shaped((2, 1, HALF), F32)),
        (core[None], residual.reshape(TOKENS, WIDTH), norm_gain[None]),
        10**8,
        2 * 10**6,
        "svv",
        "mm",
    )
    time = time_qkv.reshape(3, TOKENS, ATT)
    time_weights = call(
        time_forward_kernel,
        shaped((HEADS, TOKENS, TOKENS), BF16),
        (time,),
        6 * 10**8,
        3 * 10**6,
        "v",
        "m",
    )
    w_own, time_weights, res, gain, att_wide, att_narrow = lax.optimization_barrier(
        (w_own, time_weights, res, gain, att_wide, att_narrow)
    )
    w_other = swap(w_own, "c")
    mixed_own = call(
        embed_own_kernel,
        shaped((TOKENS, HALF), F32),
        (att_wide, att_narrow, res, w_own),
        5 * 10**8,
        3 * 10**6,
        "mmmv",
        "m",
        [big((HALF, 4 * MAIN), BF16), big((HALF, 4 * REST), BF16)],
    )
    w_other, mixed_own = lax.optimization_barrier((w_other, mixed_own))
    normed, inv, unit, norm, text, row = call(
        embed_kernel,
        (
            shaped((2, TOKENS, HALF), BF16),
            shaped((TOKENS, 128), F32),
            shaped((2, 1, HALF), F32),
            shaped((1, 1), F32),
            shaped((2, 16, 8, 128), F32),
            shaped((VIDEOS, 1, 128), F32),
        ),
        (core[None], att_wide, att_narrow, res, mixed_own, w_own, w_other, gain),
        10**9,
        6 * 10**6,
        "smmmmvvm",
        "hhvvhv",
        [
            big((HALF, 4 * MAIN), BF16),
            big((HALF, 4 * REST), BF16),
            big((2, TOKENS, HALF), BF16),
            big((TOKENS, 128), F32),
            big((2, 16, 8, 128), F32),
        ],
        4,
    )
    ring_rows = lax.all_to_all(row, RING, 0, 0)
    token, cross = call(
        basis_kernel,
        (shaped((2, VIDEOS, HALF), F32), shaped((TOKENS, 128), F32)),
        (core[None], normed, unit, norm, gain, text),
        10**8,
        2 * 10**6,
        "shvvmh",
        "vh",
        [big((2, TOKENS, HALF), BF16), big((TOKENS, 128), F32), big((2, 16, 8, 128), F32)],
        3,
    )
    ring_rows, token, cross = lax.optimization_barrier((ring_rows, token, cross))
    shares = spread(ring_rows.reshape(2, 8, 128).sum(axis=1), ("y", "c", "x"))
    wide, narrow, pull_wide, pull_narrow = call(
        project_kernel,
        (
            shaped((TOKENS, 4 * MAIN), BF16),
            shaped((TOKENS, 4 * REST), BF16),
            shaped((VIDEOS, 4 * MAIN), F32),
            shaped((VIDEOS, 4 * REST), F32),
        ),
        (core[None], w_time, normed, token),
        5 * 10**8,
        5 * 10**6,
        "shhv",
        "hhhh",
        [
            big((2, 16, PACKED, 128), BF16),
            big((2, TOKENS, HALF), BF16),
            big((HALF, 4 * MAIN), BF16),
            big((HALF, 4 * REST), BF16),
            big((TOKENS, 4 * MAIN), BF16),
            big((TOKENS, 4 * REST), BF16),
            big((VIDEOS, 4 * MAIN), F32),
            big((VIDEOS, 4 * REST), F32),
        ],
        7,
    )
    shares, wide, narrow, pull_wide, pull_narrow = lax.optimization_barrier(
        (shares, wide, narrow, pull_wide, pull_narrow)
    )
    score_grad, pulls, time_grad = call(
        score_kernel,
        (
            shaped((1, VIDEOS), F32),
            shaped((TOKENS + VIDEOS, 128), F32),
            shaped((TOKENS, ATT), BF16),
        ),
        (
            core[None],
            own_video[None],
            shares,
            teacher,
            inv,
            cross,
            wide,
            narrow,
            pull_wide,
            pull_narrow,
        ),
        10**7,
        10**6,
        "ssvvhhhhhh",
        "vhh",
        [
            big((TOKENS, 128), F32),
            big((TOKENS, 128), F32),
            big((TOKENS, 4 * MAIN), BF16),
            big((TOKENS, 4 * REST), BF16),
            big((VIDEOS, 4 * MAIN), F32),
            big((VIDEOS, 4 * REST), F32),
            big((TOKENS + VIDEOS, 128), F32),
            big((TOKENS, ATT), BF16),
        ],
        9,
    )
    moved = lax.all_to_all(time_grad.reshape(FRAMES, 8, ATT), SEQ, 0, 0).reshape(TOKENS, ATT)
    space_grad = call(
        space_back_kernel,
        shaped((3, ATT, TOKENS), BF16),
        (normed, inv, pulls, token, w_own, w_other, space, space_weights),
        2 * 10**9,
        8 * 10**6,
        "vvvvvvvm",
        "v",
        [big((HALF, 4 * MAIN), BF16), big((HALF, 4 * REST), BF16)],
    )
    moved, space_grad = lax.optimization_barrier((moved, space_grad))
    time_out = call(
        time_back_kernel,
        shaped((3, TOKENS, ATT), BF16),
        (moved, time, time_weights),
        10**9,
        5 * 10**6,
        "vvm",
        "h",
        [big((HEADS, TOKENS, TOKENS), BF16), big((3, TOKENS, ATT), BF16)],
        3,
    )
    return (
        space_grad.swapaxes(1, 2).reshape(3, 1, 1, TOKENS, ATT),
        time_out.reshape(3, 1, FRAMES, 8, ATT),
        score_grad,
    )


def solution(mesh):
    fine = Mesh(mesh.devices.reshape(2, 4, 2, 4, 8), ("zh", "y", "c", "x", "zl"))
    in_specs = (
        P(None, VID, None, SEQ, None),
        P(None, VID, SEQ, None, None),
        P(VID, SEQ, None, None),
        P(SEQ, VID),
        P(SEQ, VID),
        P(),
        P(VID, None),
        P(VID, None),
    )
    out_specs = (
        P(None, VID, SEQ, None, None),
        P(None, VID, None, SEQ, None),
        P(VID, None),
    )
    return jax.shard_map(shards, mesh=fine, in_specs=in_specs, out_specs=out_specs, check_vma=False)
```
